32 devices in a mesh: wide: 8 (over z, x), narrow: 4 (over y, core).
Axes of the slice: x: 2, y: 2, z: 4, core: 2. Of those that a mesh axis runs over, the one named last changes fastest.
Arguments:
- field_a: bfloat16 [96, 4, 180, 768], P('wide', 'narrow'), may hold values from -6 to 6
- field_b: bfloat16 [48, 4, 90, 768], P('wide', 'narrow'), may hold values from -6 to 6
- cotangent_a: bfloat16 [96, 4, 180, 768], P('wide', 'narrow'), may hold values from -6 to 6
- cotangent_b: bfloat16 [48, 4, 90, 768], P('wide', 'narrow'), may hold values from -6 to 6
- offsets_a: int32 [9], replicated, may hold values from 0 to 90, as said below
- offsets_b: int32 [9], replicated, may hold values from 0 to 45, as said below
- first_gain: bfloat16 [768], replicated, may hold values from 0.5 to 1.5
- first_bias: bfloat16 [768], replicated, may hold values from -1.75 to 1.75
- inner_weight: bfloat16 [2, 96, 768], replicated, may hold values from -0.4375 to 0.4375
- inner_bias: bfloat16 [2, 768], replicated, may hold values from -1.75 to 1.75
- outer_weight: bfloat16 [2, 96, 768], replicated, may hold values from -0.4375 to 0.4375
- outer_bias: bfloat16 [2, 768], replicated, may hold values from -1.75 to 1.75
- second_gain: bfloat16 [768], replicated, may hold values from 0.5 to 1.5
- second_norm_bias: bfloat16 [768], replicated, may hold values from -1.75 to 1.75
- expand_weight: bfloat16 [768, 3072], P(None, 'narrow'), may hold values from -0.21875 to 0.21875
- expand_bias: bfloat16 [3072], P('narrow'), may hold values from -1.75 to 1.75
- reduce_weight: bfloat16 [3072, 768], P('narrow'), may hold values from -0.109375 to 0.109375
- reduce_bias: bfloat16 [768], replicated, may hold values from -1.75 to 1.75
Outputs:
- mixed_a: bfloat16 [96, 4, 180, 768], P('wide', 'narrow')
- mixed_b: bfloat16 [48, 4, 90, 768], P('wide', 'narrow')
- grad_field_a: float32 [96, 4, 180, 768], P('wide', 'narrow')
- grad_field_b: float32 [48, 4, 90, 768], P('wide', 'narrow')
- grad_first_gain: float32 [768], replicated
- grad_first_bias: float32 [768], replicated
- grad_inner_weight: float32 [2, 96, 768], replicated
- grad_inner_bias: float32 [2, 768], replicated
- grad_outer_weight: float32 [2, 96, 768], replicated
- grad_outer_bias: float32 [2, 768], replicated
- grad_second_gain: float32 [768], replicated
- grad_second_bias: float32 [768], replicated
- grad_expand_weight: float32 [768, 3072], P(None, 'narrow')
- grad_expand_bias: float32 [3072], P('narrow')
- grad_reduce_weight: float32 [3072, 768], P('narrow')
- grad_reduce_bias: float32 [768], replicated
The draws below stay inside these ranges and needn't reach their ends.
Inputs may be any that keep to these rules, and one draw needn't show every extreme that they name: offsets_a starts at 0, ends at 90 and never falls; each wide device holds 11 or 12 patch rows, and exactly 90 % 8 devices hold 12. offsets_b starts at 0, ends at 45 and never falls; each wide device holds 5 or 6 patch rows, and exactly 45 % 8 devices hold 6.
All inputs are finite; a program needn't handle non-finite values.
Results may differ from the reference program's by a relative error of at most 0.015.
The reference program's roundings to bfloat16 on the way count: a program that leaves them out, or rounds other values in their place, can miss the bound.
Values may be sent and summed in bfloat16 or wider, within the bound.
No kernel may reach another device: no remote copies, remote signals or barrier semaphores. Data moves between devices by JAX's collectives and lax.ppermute only.
A program may use at most 320 MiB of HBM per device.

```python
import jax
import jax.numpy as jnp
from jax import lax

D = 768
NBL = 8
BS = 96
FF = 3072
H_A = 90
W_A = 180
H_B = 45
W_B = 90
S_A = 4
S_B = 4
RCAP_A = 12
RCAP_B = 6
ROWS_A = 96
ROWS_B = 48
N_WIDE = 8


def row_offsets(key, height, devices):
    base = height // devices
    extra = height % devices
    order = jax.random.permutation(key, devices).astype(jnp.int32)
    counts = base + (order < extra).astype(jnp.int32)
    return jnp.concatenate([jnp.zeros((1,), jnp.int32), jnp.cumsum(counts).astype(jnp.int32)])


def draw_offsets_a(key, part):
    key = jax.random.fold_in(key, 11)
    return row_offsets(key, H_A, N_WIDE)


def draw_offsets_b(key, part):
    key = jax.random.fold_in(key, 23)
    return row_offsets(key, H_B, N_WIDE)


def level_of(own_key, dims, cuts, smallest, top_value):
    def one(dim, shards_of):
        steps = jax.random.uniform(jax.random.fold_in(jax.random.fold_in(own_key, 6), dim), (shards_of,), jnp.float32, smallest / len(cuts), top_value / len(cuts))
        return jnp.repeat(jnp.exp(steps), dims[dim] // shards_of).reshape((-1,) + (1,) * (len(dims) - dim - 1))

    level = one(*cuts[0])
    for cut in cuts[1:]:
        level = level * one(*cut)
    return level


def noise(key, extent, spread, most, cuts=(), kind=jnp.bfloat16):
    entries = spread * jax.random.normal(key, extent, jnp.float32)
    if cuts:
        entries = entries * level_of(key, extent, cuts, -0.22, 0.18)
    return jnp.clip(entries, -most, most).astype(kind)


def setup_inputs(seed: int = 0) -> dict:
    streams_of = jax.random.split(jax.random.key(seed), 19)
    field_a = noise(streams_of[0], (ROWS_A, S_A, W_A, D), 1.0, 6.0, ((0, 8), (1, 4)))
    field_b = noise(streams_of[1], (ROWS_B, S_B, W_B, D), 1.0, 6.0, ((0, 8), (1, 4)))
    cotangent_a = noise(streams_of[2], (ROWS_A, S_A, W_A, D), 1.0, 6.0, ((0, 8), (1, 4)))
    cotangent_b = noise(streams_of[3], (ROWS_B, S_B, W_B, D), 1.0, 6.0, ((0, 8), (1, 4)))
    offsets_a = draw_offsets_a(jax.random.fold_in(streams_of[18], 71), 0)
    offsets_b = draw_offsets_b(jax.random.fold_in(streams_of[18], 71), 0)
    first_gain = jnp.clip(1.0 + 0.1 * jax.random.normal(streams_of[6], (D,), jnp.float32), 0.5, 1.5).astype(jnp.bfloat16)
    first_bias = noise(streams_of[7], (D,), 0.3, 1.75)
    inner_weight = noise(streams_of[8], (2, BS, D), (2 * BS) ** -0.5, 0.4375)
    inner_bias = noise(streams_of[9], (2, D), 0.3, 1.75)
    outer_weight = noise(streams_of[10], (2, BS, D), (2 * BS) ** -0.5, 0.4375)
    outer_bias = noise(streams_of[11], (2, D), 0.3, 1.75)
    second_gain = jnp.clip(1.0 + 0.1 * jax.random.normal(streams_of[12], (D,), jnp.float32), 0.5, 1.5).astype(jnp.bfloat16)
    second_norm_bias = noise(streams_of[13], (D,), 0.3, 1.75)
    expand_weight = noise(streams_of[14], (D, FF), D ** -0.5, 0.21875, ((1, 4),))
    expand_bias = noise(streams_of[15], (FF,), 0.3, 1.75, ((0, 4),))
    reduce_weight = noise(streams_of[16], (FF, D), FF ** -0.5, 0.109375, ((0, 4),))
    reduce_bias = noise(streams_of[17], (D,), 0.3, 1.75)
    return {"field_a": field_a, "field_b": field_b, "cotangent_a": cotangent_a, "cotangent_b": cotangent_b, "offsets_a": offsets_a, "offsets_b": offsets_b, "first_gain": first_gain, "first_bias": first_bias, "inner_weight": inner_weight, "inner_bias": inner_bias, "outer_weight": outer_weight, "outer_bias": outer_bias, "second_gain": second_gain, "second_norm_bias": second_norm_bias, "expand_weight": expand_weight, "expand_bias": expand_bias, "reduce_weight": reduce_weight, "reduce_bias": reduce_bias}


EPSILON = 1e-05
SHRINK = 0.01
HIGH = lax.Precision.HIGHEST

@jax.custom_vjp
def low(v):
    return lax.optimization_barrier(v.astype(jnp.bfloat16)).astype(jnp.float32)

@jax.custom_vjp
def low_back(v):
    return v

def low_keep(v):
    return (low(v), None)

def low_pass(kept, grad):
    return (grad,)

def back_keep(v):
    return (v, None)

def back_low(kept, grad):
    return (low(grad),)
low.defvjp(low_keep, low_pass)
low_back.defvjp(back_keep, back_low)

def gelu(value):
    return 0.5 * value * (1.0 + lax.erf(value * 0.7071067811865476))

def shrink(value):
    return value - SHRINK * jnp.tanh(value / SHRINK)

def layer_norm(value, gain, bias):
    row_average = lax.optimization_barrier(jnp.mean(value, axis=-1, keepdims=True))
    centred = value - row_average
    var = lax.optimization_barrier(jnp.mean(centred * centred, axis=-1, keepdims=True))
    return centred * lax.rsqrt(var + EPSILON) * gain + bias

def complex_block(real, imag, weight, bias):
    shape = real.shape
    real = real.reshape(shape[:-1] + (NBL, BS))
    imag = imag.reshape(shape[:-1] + (NBL, BS))
    w_real = weight[0].reshape(BS, NBL, BS)
    w_imag = weight[1].reshape(BS, NBL, BS)

    def mixing(left, right):
        return jnp.einsum('...bi,ibo->...bo', left, right, precision=HIGH)
    out_real = (mixing(real, w_real) - mixing(imag, w_imag)).reshape(shape) + bias[0]
    out_imag = (mixing(imag, w_real) + mixing(real, w_imag)).reshape(shape) + bias[1]
    return (out_real, out_imag)

def snapshot(field, params):
    first_norm_gain, first_norm_bias, weight_in, bias_in, weight_out, bias_out, second_norm_gain, bias_two, expand, expand_b, reduce_w, reduce_b = params
    normalized_rows = layer_norm(field, first_norm_gain, first_norm_bias)
    spectrum = jnp.fft.rfft(normalized_rows, axis=1, norm='ortho')
    spec_real = low(low_back(spectrum.real))
    spec_imag = low(low_back(spectrum.imag))
    whole = jnp.fft.fft(spec_real + 1j * spec_imag, axis=0, norm='ortho')
    zed_real = low(whole.real)
    zed_imag = low(whole.imag)
    pre_real, pre_imag = complex_block(zed_real, zed_imag, weight_in, bias_in)
    act_real = low(gelu(low_back(pre_real)))
    act_imag = low(gelu(low_back(pre_imag)))
    out_real, out_imag = complex_block(act_real, act_imag, weight_out, bias_out)
    shrunk_real = shrink(low_back(out_real))
    shrunk_imag = shrink(low_back(out_imag))
    inverse = jnp.fft.ifft(shrunk_real + 1j * shrunk_imag, axis=0, norm='ortho')
    back_real = low(low_back(inverse.real))
    back_imag = low(low_back(inverse.imag))
    filtered = jnp.fft.irfft(back_real + 1j * back_imag, n=field.shape[1], axis=1, norm='ortho') + normalized_rows
    middle = filtered + field
    input_rows = low(layer_norm(middle, second_norm_gain, bias_two)).reshape(-1, D)
    hidden = low(gelu(low_back(jnp.dot(input_rows, expand, precision=HIGH) + expand_b)))
    output = low_back(jnp.dot(hidden, reduce_w, precision=HIGH) + reduce_b)
    return middle + output.reshape(middle.shape)

def grid_layer(padded, offsets, rcap, height, params):
    line = jnp.arange(height, dtype=jnp.int32)
    owner = lax.optimization_barrier(jnp.sum((offsets[1:][None, :] <= line[:, None]).astype(jnp.int32), axis=1))
    source = (owner * rcap + line - offsets[owner]).astype(jnp.int32)
    whole = jnp.swapaxes(jnp.take(padded, source, axis=0), 0, 1)
    result = lax.map(jax.checkpoint(lambda field: snapshot(field, params)), whole)
    result = jnp.swapaxes(result, 0, 1)
    slots = jnp.arange(N_WIDE * rcap, dtype=jnp.int32)
    holder = slots // rcap
    offset = slots % rcap
    begin = offsets[holder]
    valid = offset < offsets[holder + 1] - begin
    picked = jnp.take(result, jnp.clip(begin + offset, 0, height - 1).astype(jnp.int32), axis=0)
    return jnp.where(valid[:, None, None, None], picked, 0.0)

def reference(field_a, field_b, cotangent_a, cotangent_b, offsets_a, offsets_b, first_gain, first_bias, inner_weight, inner_bias, outer_weight, outer_bias, second_gain, second_norm_bias, expand_weight, expand_bias, reduce_weight, reduce_bias):
    params = (first_gain.astype(jnp.float32), first_bias.astype(jnp.float32), inner_weight.astype(jnp.float32), inner_bias.astype(jnp.float32), outer_weight.astype(jnp.float32), outer_bias.astype(jnp.float32), second_gain.astype(jnp.float32), second_norm_bias.astype(jnp.float32), expand_weight.astype(jnp.float32), expand_bias.astype(jnp.float32), reduce_weight.astype(jnp.float32), reduce_bias.astype(jnp.float32))

    def forward(grid_a, grid_b, weights):
        return (grid_layer(grid_a, offsets_a, RCAP_A, H_A, weights), grid_layer(grid_b, offsets_b, RCAP_B, H_B, weights))
    outputs, pullback = jax.vjp(forward, field_a.astype(jnp.float32), field_b.astype(jnp.float32), params)
    grad_a, grad_b, grads = pullback((cotangent_a.astype(jnp.float32), cotangent_b.astype(jnp.float32)))
    return (outputs[0].astype(jnp.bfloat16), outputs[1].astype(jnp.bfloat16), grad_a, grad_b, grads[0], grads[1], grads[2], grads[3], grads[4], grads[5], grads[6], grads[7], grads[8], grads[9], grads[10], grads[11])
```

```python
import functools
import math

import jax
import jax.numpy as jnp
import numpy as np
from jax import lax
from jax.experimental import pallas as pl
from jax.experimental.pallas import tpu as pltpu
from jax.sharding import PartitionSpec as P

NBL = 8
BS = 96
H_A = 90
H_B = 45


EPSILON = 1e-05
SHRINK = 0.01
HIGH = lax.Precision.HIGHEST
ROOT_HALF = 0.7071067811865476
ROOT_TWO_PI = 2.5066282746310002


def gelu_value(value):
    return 0.5 * value * (1.0 + lax.erf(value * ROOT_HALF))


def gelu_slope(value):
    return (
        0.5 * (1.0 + lax.erf(value * ROOT_HALF))
        + value * jnp.exp(-0.5 * value * value) / ROOT_TWO_PI
    )


def shrink_value(value):
    return value - SHRINK * jnp.tanh(value / SHRINK)


def shrink_slope(value):
    bent = jnp.tanh(value / SHRINK)
    return bent * bent


def phase(left, right, length):
    turns = left * right % length
    return turns.astype(jnp.float32) * (2.0 * math.pi / length)


def row_slots(offsets, depth, width):
    offset = jnp.arange(depth, dtype=jnp.int32)
    begin = offsets[:width]
    counts = offsets[1:] - begin
    line = (begin[:, None] + offset[None, :]).reshape(-1)
    valid = (offset[None, :] < counts[:, None]).reshape(-1).astype(jnp.float32)
    return (line, valid)


def column_slots(freqs, spread, width):
    edges = jnp.arange(width + 1, dtype=jnp.int32) * freqs // width
    offset = jnp.arange(spread, dtype=jnp.int32)
    begin = edges[:width]
    valid = (offset[None, :] < (edges[1:] - begin)[:, None]).reshape(-1).astype(jnp.float32)
    return ((begin[:, None] + offset[None, :]).reshape(-1), valid)


def forward_w_table(columns, freq, valid, width, spread):
    angle = phase(jnp.arange(columns, dtype=jnp.int32)[:, None], freq[None, :], columns)
    scale = valid[None, :] / math.sqrt(columns)
    table = jnp.stack([jnp.cos(angle) * scale, -jnp.sin(angle) * scale], axis=1)
    return table.reshape(columns, 2, width, spread)


def inverse_w_table(columns, freq, valid, width, spread):
    angle = phase(freq[:, None], jnp.arange(columns, dtype=jnp.int32)[None, :], columns)
    edge = (freq == 0) | (2 * freq == columns)
    weight = jnp.where(edge, 1.0, 2.0) * valid / math.sqrt(columns)
    real = jnp.cos(angle) * weight[:, None]
    imag = jnp.where(edge[:, None], 0.0, -jnp.sin(angle)) * weight[:, None]
    return jnp.stack([real, imag], axis=1).reshape(width, spread, 2, columns)


def forward_h_table(height, line, valid):
    angle = phase(jnp.arange(height, dtype=jnp.int32)[:, None], line[None, :], height)
    scale = valid[None, :] / math.sqrt(height)
    cosine = jnp.cos(angle) * scale
    sine = jnp.sin(angle) * scale
    upper = jnp.stack([cosine, sine], axis=-1)
    lower = jnp.stack([-sine, cosine], axis=-1)
    return jnp.stack([upper, lower], axis=1)


def inverse_h_table(height, line, valid):
    angle = phase(line[:, None], jnp.arange(height, dtype=jnp.int32)[None, :], height)
    scale = valid[:, None] / math.sqrt(height)
    cosine = jnp.cos(angle) * scale
    sine = jnp.sin(angle) * scale
    upper = jnp.stack([cosine, -sine], axis=-1)
    lower = jnp.stack([sine, cosine], axis=-1)
    return jnp.stack([upper, lower], axis=1)


def complex_weight(weight):
    blocked = weight.reshape(2, BS, NBL, BS).transpose(0, 2, 1, 3)
    return jnp.stack([jnp.stack([blocked[0], blocked[1]]), jnp.stack([-blocked[1], blocked[0]])])


def fold_weight(grad):
    folded = jnp.stack([grad[0, 0] + grad[1, 1], grad[0, 1] - grad[1, 0]])
    return folded.transpose(0, 2, 1, 3).reshape(2, BS, NBL * BS)


def general_device(
    field_a,
    field_b,
    cotangent_a,
    cotangent_b,
    offsets_a,
    offsets_b,
    first_gain,
    first_bias,
    inner_weight,
    inner_bias,
    outer_weight,
    outer_bias,
    second_gain,
    second_norm_bias,
    expand_weight,
    expand_bias,
    reduce_weight,
    reduce_bias,
):
    width = lax.axis_size("wide")
    myself = lax.axis_index("wide")
    local = field_a.shape[-1]
    layouts = []
    for field, offsets, height in ((field_a, offsets_a, H_A), (field_b, offsets_b, H_B)):
        depth, snaps, columns = (field.shape[0], field.shape[1], field.shape[2])
        freqs = columns // 2 + 1
        spread = (freqs + width - 1) // width
        line, row_valid = row_slots(offsets, depth, width)
        freq, freq_valid = column_slots(freqs, spread, width)
        layouts.append(
            (
                depth,
                snaps,
                columns,
                spread,
                height,
                forward_w_table(columns, freq, freq_valid, width, spread),
                inverse_w_table(columns, freq, freq_valid, width, spread),
                forward_h_table(height, line, row_valid),
                inverse_h_table(height, line, row_valid),
                lax.dynamic_slice_in_dim(row_valid, myself * depth, depth),
            )
        )
    token_count = layouts[0][0] * layouts[0][1] * layouts[0][2]
    point_count = layouts[0][4] * layouts[0][1] * layouts[0][3]

    def to_grids(tokens):
        return [
            tokens[:token_count].reshape(
                layouts[0][0], layouts[0][1], layouts[0][2], tokens.shape[-1]
            ),
            tokens[token_count:].reshape(
                layouts[1][0], layouts[1][1], layouts[1][2], tokens.shape[-1]
            ),
        ]

    def to_tokens(parts):
        return jnp.concatenate([piece.reshape(-1, piece.shape[-1]) for piece in parts])

    def to_spectra(points):
        pieces = (points[:point_count], points[point_count:])
        return [
            pieces[index].reshape(layouts[index][4], layouts[index][1], layouts[index][3], 2, local)
            for index in range(2)
        ]

    def to_sends(parts):
        return [
            parts[index].reshape(
                width, layouts[index][0], layouts[index][1], layouts[index][3], 2, local
            )
            for index in range(2)
        ]

    mask = to_tokens(
        [
            jnp.broadcast_to(lay[9][:, None, None, None], (lay[0], lay[1], lay[2], 1))
            for lay in layouts
        ]
    )
    first_norm_gain = first_gain.astype(jnp.float32)
    first_norm_bias = first_bias.astype(jnp.float32)
    bias_out = reduce_bias.astype(jnp.float32)
    weight_one = complex_weight(inner_weight)
    weight_two = complex_weight(outer_weight)
    shift_one = inner_bias.astype(jnp.float32).reshape(2, NBL, BS)
    shift_two = outer_bias.astype(jnp.float32).reshape(2, NBL, BS)
    source = jnp.concatenate([field_a.reshape(-1, local), field_b.reshape(-1, local)]).astype(
        jnp.float32
    )
    mean_one = jnp.mean(source, axis=1, keepdims=True)
    first_centered_input = source - mean_one
    first_inverse_deviation = lax.rsqrt(
        jnp.mean(first_centered_input * first_centered_input, axis=1, keepdims=True) + EPSILON
    )
    first_standardized = first_centered_input * first_inverse_deviation
    normalized_rows = first_standardized * first_norm_gain + first_norm_bias
    normed_parts = to_grids(normalized_rows)
    sends = [
        jnp.einsum(
            "rswc,wtjk->jrsktc", normed_parts[index], layouts[index][5], precision=HIGH
        ).astype(jnp.bfloat16)
        for index in range(2)
    ]
    arrived = (
        lax.all_to_all(sends[0], "wide", split_axis=0, concat_axis=1, tiled=True),
        lax.all_to_all(sends[1], "wide", split_axis=0, concat_axis=1, tiled=True),
    )
    spectra = [
        jnp.einsum(
            "kumt,msqtc->ksquc",
            layouts[index][7],
            arrived[index][0].astype(jnp.float32),
            precision=HIGH,
        )
        for index in range(2)
    ]
    zed = jnp.concatenate([piece.reshape(-1, 2, NBL, BS) for piece in spectra]).astype(jnp.bfloat16)
    pre_one = (
        jnp.einsum("pcbi,cdbio->pdbo", zed, weight_one, preferred_element_type=jnp.float32)
        + shift_one
    )
    act_one = gelu_value(pre_one).astype(jnp.bfloat16)
    pre_two = (
        jnp.einsum("pcbi,cdbio->pdbo", act_one, weight_two, preferred_element_type=jnp.float32)
        + shift_two
    )
    shrunk = to_spectra(shrink_value(pre_two))
    outgoing = to_sends(
        [
            jnp.einsum(
                "mukt,ksqtc->msquc", layouts[index][8], shrunk[index], precision=HIGH
            ).astype(jnp.bfloat16)
            for index in range(2)
        ]
    )
    returned = (
        lax.all_to_all(outgoing[0], "wide", split_axis=0, concat_axis=1, tiled=True),
        lax.all_to_all(outgoing[1], "wide", split_axis=0, concat_axis=1, tiled=True),
    )
    field_parts = to_grids(source)
    middle_parts = []
    for index in range(2):
        lay = layouts[index]
        received = (
            returned[index][0].reshape(width, lay[0], lay[1], lay[3], 2, local).astype(jnp.float32)
        )
        middle_parts.append(
            jnp.einsum("jrsktc,jktw->rswc", received, lay[6], precision=HIGH)
            + normed_parts[index]
            + field_parts[index]
        )
    middle = to_tokens(middle_parts)
    mean_two = jnp.mean(middle, axis=1, keepdims=True)
    second_centered_input = middle - mean_two
    second_inverse_deviation = lax.rsqrt(
        jnp.mean(second_centered_input * second_centered_input, axis=1, keepdims=True) + EPSILON
    )
    second_standardized = second_centered_input * second_inverse_deviation
    second_norm_gain = second_gain.astype(jnp.float32)
    input_rows = (
        second_standardized * second_norm_gain + second_norm_bias.astype(jnp.float32)
    ).astype(jnp.bfloat16)
    full_inputs = lax.all_gather(input_rows, "narrow", axis=0, tiled=True)
    pre_three = jnp.dot(
        full_inputs, expand_weight, preferred_element_type=jnp.float32
    ) + expand_bias.astype(jnp.float32)
    act_three = gelu_value(pre_three).astype(jnp.bfloat16)
    partial_value = jnp.dot(act_three, reduce_weight, preferred_element_type=jnp.float32)
    mixed = (
        lax.psum_scatter(
            partial_value.astype(jnp.bfloat16), "narrow", scatter_dimension=0, tiled=True
        ).astype(jnp.float32)
        + bias_out
    )
    result = to_grids((middle + mixed) * mask)
    upstream = jnp.concatenate([cotangent_a.reshape(-1, local), cotangent_b.reshape(-1, local)])
    upstream = jnp.where(mask > 0.0, upstream, jnp.zeros_like(upstream))
    upstream_f = upstream.astype(jnp.float32)
    grad_out_b = jnp.sum(upstream_f, 0)
    full_upstream = lax.all_gather(upstream, "narrow", axis=0, tiled=True)
    grad_act = jnp.einsum(
        "td,fd->tf", full_upstream, reduce_weight, preferred_element_type=jnp.float32
    )
    grad_pre = (grad_act * gelu_slope(pre_three)).astype(jnp.bfloat16)
    grad_reduce = jnp.einsum(
        "tf,td->fd", act_three, full_upstream, preferred_element_type=jnp.float32
    )
    grad_expand = jnp.einsum("td,tf->df", full_inputs, grad_pre, preferred_element_type=jnp.float32)
    grad_expand_b = jnp.sum(grad_pre.astype(jnp.float32), 0)
    grad_terms = jnp.einsum(
        "tf,df->td", grad_pre, expand_weight, preferred_element_type=jnp.float32
    )
    input_gradient = lax.psum_scatter(
        grad_terms.astype(jnp.bfloat16), "narrow", scatter_dimension=0, tiled=True
    ).astype(jnp.float32)
    scaled_rows = input_gradient * second_norm_gain
    gradient_second_norm_gain = jnp.sum(input_gradient * second_standardized, 0)
    grad_bias_two = jnp.sum(input_gradient, 0)
    grad_full = second_inverse_deviation * (
        scaled_rows
        - jnp.mean(scaled_rows, axis=1, keepdims=True)
        - second_standardized * jnp.mean(scaled_rows * second_standardized, axis=1, keepdims=True)
    )
    grad_middle = grad_full + upstream_f
    grad_parts = to_grids(grad_middle)
    sends = [
        jnp.einsum(
            "rswc,jktw->jrsktc", grad_parts[index], layouts[index][6], precision=HIGH
        ).astype(jnp.bfloat16)
        for index in range(2)
    ]
    arrived = (
        lax.all_to_all(sends[0], "wide", split_axis=0, concat_axis=1, tiled=True),
        lax.all_to_all(sends[1], "wide", split_axis=0, concat_axis=1, tiled=True),
    )
    grad_points = jnp.concatenate(
        [
            jnp.einsum(
                "mukt,msquc->ksqtc",
                layouts[index][8],
                arrived[index][0].astype(jnp.float32),
                precision=HIGH,
            ).reshape(-1, 2, NBL, BS)
            for index in range(2)
        ]
    )
    grad_two = (grad_points * shrink_slope(pre_two)).astype(jnp.bfloat16)
    grad_hidden = jnp.einsum(
        "pdbo,cdbio->pcbi", grad_two, weight_two, preferred_element_type=jnp.float32
    )
    grad_weight_two = fold_weight(
        jnp.einsum("pcbi,pdbo->cdbio", act_one, grad_two, preferred_element_type=jnp.float32)
    )
    grad_shift_two = jnp.sum(grad_two.astype(jnp.float32), 0).reshape(2, -1)
    grad_one = (grad_hidden * gelu_slope(pre_one)).astype(jnp.bfloat16)
    grad_zed = jnp.einsum(
        "pdbo,cdbio->pcbi", grad_one, weight_one, preferred_element_type=jnp.float32
    )
    grad_weight_one = fold_weight(
        jnp.einsum("pcbi,pdbo->cdbio", zed, grad_one, preferred_element_type=jnp.float32)
    )
    grad_shift_one = jnp.sum(grad_one.astype(jnp.float32), 0).reshape(2, -1)
    grad_spectra = to_spectra(grad_zed)
    outgoing = to_sends(
        [
            jnp.einsum(
                "kumt,ksquc->msqtc", layouts[index][7], grad_spectra[index], precision=HIGH
            ).astype(jnp.bfloat16)
            for index in range(2)
        ]
    )
    returned = (
        lax.all_to_all(outgoing[0], "wide", split_axis=0, concat_axis=1, tiled=True),
        lax.all_to_all(outgoing[1], "wide", split_axis=0, concat_axis=1, tiled=True),
    )
    grad_normed_parts = []
    for index in range(2):
        lay = layouts[index]
        received = (
            returned[index][0].reshape(width, lay[0], lay[1], lay[3], 2, local).astype(jnp.float32)
        )
        grad_normed_parts.append(
            jnp.einsum("jrsktc,wtjk->rswc", received, lay[5], precision=HIGH) + grad_parts[index]
        )
    normalized_gradient = to_tokens(grad_normed_parts)
    scaled_rows = normalized_gradient * first_norm_gain
    grad_source = (
        first_inverse_deviation
        * (
            scaled_rows
            - jnp.mean(scaled_rows, axis=1, keepdims=True)
            - first_standardized * jnp.mean(scaled_rows * first_standardized, axis=1, keepdims=True)
        )
        + grad_middle
    )
    grad_fields = to_grids(grad_source * mask)
    gradient_first_norm_gain = jnp.sum(normalized_gradient * first_standardized, 0)
    grad_bias_one = jnp.sum(normalized_gradient, 0)
    mlp_sums = lax.psum((grad_expand, grad_expand_b, grad_reduce), "wide")
    shared = lax.psum(
        (
            grad_weight_one,
            grad_shift_one,
            grad_weight_two,
            grad_shift_two,
            gradient_first_norm_gain,
            grad_bias_one,
            gradient_second_norm_gain,
            grad_bias_two,
            grad_out_b,
        ),
        ("wide", "narrow"),
    )
    return (
        result[0].astype(jnp.bfloat16),
        result[1].astype(jnp.bfloat16),
        grad_fields[0],
        grad_fields[1],
        shared[4],
        shared[5],
        shared[0],
        shared[1],
        shared[2],
        shared[3],
        shared[6],
        shared[7],
        mlp_sums[0],
        mlp_sums[1],
        mlp_sums[2],
        shared[8],
    )


F32 = jnp.float32
BF16 = jnp.bfloat16
MIB = 1024 * 1024
PAD = 8
LANES = 128


def halves(value):
    high = lax.reduce_precision(value, 8, 7)
    return high.astype(BF16), (value - high).astype(BF16)


def round_up(value, unit):
    return -(-value // unit) * unit


def call(kernel, grid, in_specs, out_specs, out_shape, scratch=(), limit=56, after=0):
    first = len(in_specs)

    def body(*refs):
        kernel(*refs[:first], *refs[first + after :])

    return pl.pallas_call(
        body,
        grid=grid,
        in_specs=in_specs + [pl.BlockSpec(memory_space=pl.ANY)] * after,
        out_specs=out_specs,
        out_shape=out_shape,
        scratch_shapes=list(scratch),
        compiler_params=pltpu.CompilerParams(vmem_limit_bytes=limit * MIB),
    )


def whole(array):
    zeros = (0,) * array.ndim
    return pl.BlockSpec(array.shape, lambda *_: zeros)


def dot(left, right):
    return jnp.dot(left, right, preferred_element_type=F32)


def dot_t(left, right):
    return lax.dot_general(left, right, (((1,), (1,)), ((), ())), preferred_element_type=F32)


def column_tables(columns, spread, width, repeat, tokens):
    freqs = columns // 2 + 1
    freq = np.arange(width * spread)
    valid = (freq < freqs).astype(np.float64)
    angle = 2.0 * np.pi * (np.outer(freq, np.arange(columns)) % columns) / columns
    scale = valid[:, None] / math.sqrt(columns)
    weight = np.where((freq == 0) | (2 * freq == columns), 1.0, 2.0)[:, None]
    parts = np.stack([np.cos(angle) * scale, -np.sin(angle) * scale], axis=1)
    parts = parts.reshape(width, spread, 2, columns).transpose(0, 2, 1, 3)
    heavy = np.broadcast_to(weight.reshape(width, 1, spread, 1), parts.shape)
    forward = np.zeros((width, repeat, 2, spread, tokens))
    inverse = np.zeros((width, repeat, 2, spread, tokens))
    for index in range(repeat):
        span = slice(index * columns, (index + 1) * columns)
        forward[:, index, :, :, span] = parts
        inverse[:, index, :, :, span] = parts * heavy
    return forward.reshape(-1, tokens), inverse.reshape(-1, tokens)


def row_table(height, line, valid, padded):
    angle = phase(jnp.arange(padded, dtype=jnp.int32)[:, None], line[None, :], height)
    inside = (jnp.arange(padded) < height).astype(F32)[:, None]
    scale = inside * valid[None, :] / math.sqrt(height)
    cosine = jnp.cos(angle) * scale
    sine = jnp.sin(angle) * scale
    upper = jnp.stack([cosine, sine], axis=-1)
    lower = jnp.stack([-sine, cosine], axis=-1)
    return jnp.stack([upper, lower]).reshape(2 * padded, -1)


def half_weight(weight, half, blocks):
    side = blocks * BS
    pieces = weight[:, :, half * side : (half + 1) * side].reshape(2, BS, blocks, BS)
    eye = jnp.eye(blocks, dtype=weight.dtype)
    wide = pieces.transpose(0, 2, 1, 3)[:, :, :, None, :] * eye[None, :, None, :, None]
    wide = wide.reshape(2, side, side)
    return jnp.concatenate(
        [
            jnp.concatenate([wide[0], wide[1]], axis=1),
            jnp.concatenate([-wide[1], wide[0]], axis=1),
        ],
        axis=0,
    )


def layer_norm(value):
    mean = jnp.mean(value, axis=1, keepdims=True)
    centred = value - mean
    scale = lax.rsqrt(jnp.mean(centred * centred, axis=1, keepdims=True) + EPSILON)
    return centred * scale, scale


def layer_norm_back(grad, gain, standard, scale):
    scaled = grad * gain
    return scale * (
        scaled
        - jnp.mean(scaled, axis=1, keepdims=True)
        - standard * jnp.mean(scaled * standard, axis=1, keepdims=True)
    )


def row_sums(*values):
    rows = [jnp.sum(value, axis=0, keepdims=True) for value in values]
    blank = jnp.zeros((PAD - len(rows), rows[0].shape[1]), F32)
    return jnp.concatenate(rows + [blank], axis=0)


class Plan:
    def __init__(self, width, rows_a, columns_a, rows_b, columns_b, local):
        self.width = width
        self.rows_a, self.columns_a = rows_a, columns_a
        self.rows_b, self.columns_b = rows_b, columns_b
        self.local = local
        self.half = local // 2
        self.spread_a = -(-(columns_a // 2 + 1) // width)
        self.spread_b = -(-(columns_b // 2 + 1) // width)
        self.piece = 2 * self.spread_a
        self.units = rows_a + rows_b // 2
        self.tokens = round_up(columns_a, 8)
        self.pad_a = round_up(H_A, 16)
        self.pad_b = round_up(H_B, 16)
        self.points_a = self.spread_a * self.pad_a
        self.points = self.points_a + self.spread_b * self.pad_b

    def fits(self):
        return (
            self.columns_a == 2 * self.columns_b
            and self.spread_a == 2 * self.spread_b
            and self.piece % 8 == 0
            and self.rows_b % 2 == 0
            and self.half % 128 == 0
            and self.half % BS == 0
        )

    def spec_a(self):
        last = self.rows_a - 1
        return pl.BlockSpec(
            (1, self.columns_a, self.local), lambda i: (jnp.minimum(i, last), 0, 0)
        )

    def spec_b(self):
        first = self.rows_a
        return pl.BlockSpec(
            (2, self.columns_b, self.local), lambda i: (jnp.maximum(i - first, 0), 0, 0)
        )

    def unit(self, last=None):
        return pl.BlockSpec((1, self.tokens, last or self.local), lambda i: (i, 0, 0))

    def sends(self):
        return pl.BlockSpec((self.width, 1, self.piece, self.half), lambda i: (0, i, 0, 0))

    def table(self, shape):
        first = self.rows_a
        zeros = (0,) * len(shape)
        return pl.BlockSpec((1,) + shape, lambda i: ((i >= first).astype(jnp.int32),) + zeros)

    def exchange_shape(self):
        return jax.ShapeDtypeStruct((self.width, self.units, self.piece, self.half), BF16)

    def units_shape(self, kind):
        return jax.ShapeDtypeStruct((self.units, self.tokens, self.local), kind)

    def load(self, step, a_ref, b_ref, scratch):
        @pl.when(step == 0)
        def _():
            scratch[...] = jnp.zeros_like(scratch)

        @pl.when(step < self.rows_a)
        def _():
            scratch[: self.columns_a] = a_ref[0].astype(F32)

        @pl.when(step >= self.rows_a)
        def _():
            scratch[: self.columns_b] = b_ref[0].astype(F32)
            scratch[self.columns_b : self.columns_a] = b_ref[1].astype(F32)

        return scratch[...]

    def outs(self):
        last, first = self.rows_a - 1, self.rows_a
        return [
            pl.BlockSpec(
                (1, 1, self.columns_a, self.local), lambda i: (jnp.minimum(i, last), 0, 0, 0)
            ),
            pl.BlockSpec(
                (2, 1, self.columns_b, self.local), lambda i: (jnp.maximum(i - first, 0), 0, 0, 0)
            ),
        ]

    def store(self, step, value, a_ref, b_ref):
        @pl.when(step < self.rows_a)
        def _():
            a_ref[0, 0] = value[: self.columns_a].astype(a_ref.dtype)

        @pl.when(step >= self.rows_a)
        def _():
            b_ref[0, 0] = value[: self.columns_b].astype(b_ref.dtype)
            b_ref[1, 0] = value[self.columns_b : self.columns_a].astype(b_ref.dtype)

    def put_sends(self, product, refs):
        for index, ref in enumerate(refs):
            lanes = product[:, index * self.half : (index + 1) * self.half]
            ref[:, 0] = lanes.reshape(self.width, self.piece, self.half).astype(BF16)

    def get_sends(self, refs):
        depth = self.width * self.piece
        return [ref[:, 0].astype(F32).reshape(depth, self.half).astype(BF16) for ref in refs]

    def valid_rows(self, step, counts, shape):
        token = lax.broadcasted_iota(jnp.int32, shape, 0)
        second = (token >= self.columns_b).astype(jnp.int32)
        in_a = (step < counts[0]) & (step < self.rows_a)
        row_b = 2 * (step - self.rows_a) + second
        in_b = (row_b < counts[1]) & (step >= self.rows_a)
        return (in_a | in_b) & (token < self.columns_a)


def first_kernel(plan, xa, xb, gain, bias, table, out0, out1, scratch):
    step = pl.program_id(0)
    value = plan.load(step, xa, xb, scratch)
    standard, _ = layer_norm(value)
    high, low = halves(standard * gain[...] + bias[...])
    spectrum = dot(table[0, 0], high) + (dot(table[0, 0], low) + dot(table[0, 1], high))
    plan.put_sends(spectrum, (out0, out1))


def cotangent_kernel(plan, counts, ca, cb, out, sums, scratch):
    step = pl.program_id(0)
    value = plan.load(step, ca, cb, scratch)
    value = jnp.where(plan.valid_rows(step, counts, value.shape), value, 0.0)
    out[0] = value.astype(BF16)

    @pl.when(step == 0)
    def _():
        sums[...] = jnp.zeros_like(sums)

    sums[...] += row_sums(value)


def middle_kernel(plan, xa, xb, got0, got1, gain, bias, gain2, bias2, table, mid, out, scratch):
    step = pl.program_id(0)
    value = plan.load(step, xa, xb, scratch)
    standard, _ = layer_norm(value)
    back = jnp.concatenate([dot(table[0], part) for part in plan.get_sends((got0, got1))], axis=1)
    middle = value + standard * gain[...] + bias[...] + back
    mid[0] = middle
    standard2, _ = layer_norm(middle)
    out[0] = (standard2 * gain2[...] + bias2[...]).astype(BF16)


def middle_back_kernel(plan, dv, mid, cot, gain2, table, dmid, out0, out1, sums):
    step = pl.program_id(0)
    grad = dv[0].astype(F32)
    standard, scale = layer_norm(mid[0])
    total = cot[0].astype(F32) + layer_norm_back(grad, gain2[...], standard, scale)
    dmid[0] = total
    plan.put_sends(dot(table[0], total.astype(BF16)), (out0, out1))

    @pl.when(step == 0)
    def _():
        sums[...] = jnp.zeros_like(sums)

    sums[...] += row_sums(grad * standard, grad)


def mixed_kernel(
    plan, counts, hidden, weight, bias, mid, dmid, xa, xb, outa, outb, sums, scratch
):
    step = pl.program_id(0)
    standard, _ = layer_norm(plan.load(step, xa, xb, scratch))
    grad = dmid[0]

    @pl.when(step == 0)
    def _():
        sums[...] = jnp.zeros_like(sums)

    sums[...] += row_sums(grad * standard, grad)
    value = mid[0] + dot(hidden[0], weight[...]) + bias[...]
    value = jnp.where(plan.valid_rows(step, counts, value.shape), value, 0.0)
    plan.store(step, value, outa, outb)


def last_kernel(plan, xa, xb, got0, got1, dmid, gain, table, outa, outb, scratch):
    step = pl.program_id(0)
    value = plan.load(step, xa, xb, scratch)
    standard, scale = layer_norm(value)
    back = jnp.concatenate([dot(table[0], part) for part in plan.get_sends((got0, got1))], axis=1)
    grad = back + dmid[0]
    total = dmid[0] + layer_norm_back(grad, gain[...], standard, scale)
    plan.store(step, total, outa, outb)


def unpack(plan, got, part_a, part_b):
    rows_a = plan.rows_a * plan.piece
    rows_b = (plan.units - plan.rows_a) * plan.piece
    for j in range(plan.width):
        value = got[j].astype(F32)
        for part, rows, piece in (
            (part_a, rows_a, value[: plan.rows_a]),
            (part_b, rows_b, value[plan.rows_a :]),
        ):
            for g in range(plan.half // LANES):
                lanes = piece[:, :, g * LANES : (g + 1) * LANES]
                part[g, j * rows : (j + 1) * rows] = lanes.reshape(rows, LANES)


def repack(plan, part_a, part_b, out):
    rows_a = plan.rows_a * plan.piece
    rows_b = (plan.units - plan.rows_a) * plan.piece
    for j in range(plan.width):
        for part, rows, first, last in (
            (part_a, rows_a, 0, plan.rows_a),
            (part_b, rows_b, plan.rows_a, plan.units),
        ):
            for g in range(plan.half // LANES):
                out[j, first:last, :, g * LANES : (g + 1) * LANES] = (
                    part[g, j * rows : (j + 1) * rows]
                    .reshape(last - first, plan.piece, LANES)
                    .astype(BF16)
                )


def grids(plan):
    return (
        (plan.spread_a, plan.pad_a, plan.width * 2 * plan.rows_a, 0, 0),
        (plan.spread_b, plan.pad_b, plan.width * 2 * plan.rows_b, plan.points_a, 1),
    )


def to_points(plan, parts, tables, out, first=None):
    for spread, pad, depth, base, which in grids(plan):
        for f in range(spread):
            lanes = [
                parts[which][g, pl.ds(f, depth, stride=spread), :].astype(BF16)
                for g in range(plan.half // LANES)
            ]
            column = jnp.concatenate(lanes, axis=1)
            product = dot(tables[which][0], column)
            if first is not None:
                product += dot(tables[which][1], column)
                if f == 0:
                    first[which : which + 1] = product[:1]
            out[base + f * pad : base + (f + 1) * pad, :] = jnp.concatenate(
                [product[:pad], product[pad:]], axis=1
            ).astype(out.dtype)


def from_points(plan, points, tables, parts):
    for spread, pad, depth, base, which in grids(plan):
        for f in range(spread):
            value = points[base + f * pad : base + (f + 1) * pad, :]
            column = jnp.concatenate([value[:, : plan.half], value[:, plan.half :]], axis=0)
            product = dot(tables[which][...], column)
            for g in range(plan.half // LANES):
                parts[which][g, pl.ds(f, depth, stride=spread), :] = product[
                    :, g * LANES : (g + 1) * LANES
                ]


def spectral_kernel(
    plan, steps, got, ta, tb, tat, tbt, w1, b1, w2, b2, out, zed, act, slope1, slope2, dc, pa, pb, shrunk
):
    unpack(plan, got, pa, pb)
    dc[...] = jnp.zeros_like(dc)
    to_points(plan, (pa, pb), (ta, tb), zed, dc)
    size = plan.points // steps

    def body(index, carry):
        rows = pl.ds(pl.multiple_of(index * size, size), size)
        pre_one = dot(zed[rows, :], w1[...]) + b1[...]
        cdf = 0.5 * (1.0 + lax.erf(pre_one * ROOT_HALF))
        hidden = (pre_one * cdf).astype(BF16)
        act[rows, :] = hidden
        slope1[rows, :] = (
            cdf + pre_one * jnp.exp(-0.5 * pre_one * pre_one) * (1.0 / ROOT_TWO_PI)
        ).astype(BF16)
        pre_two = dot(hidden, w2[...]) + b2[...]
        bent = jnp.tanh(pre_two * (1.0 / SHRINK))
        shrunk[rows, :] = (pre_two - SHRINK * bent).astype(BF16)
        slope2[rows, :] = (bent * bent).astype(BF16)
        return carry

    lax.fori_loop(0, steps, body, 0)
    from_points(plan, shrunk, (tat, tbt), (pa, pb))
    repack(plan, pa, pb, out)


def spectral_back_kernel(
    plan, steps, got, ta, tb, tat, tbt, w1, w2, slope1, slope2, zed, out, grad1, grad2, sums, pa, pb, work
):
    unpack(plan, got, pa, pb)
    to_points(plan, (pa, pb), (ta, tb), work)
    size = plan.points // steps
    sums[...] = jnp.zeros_like(sums)

    def body(index, carry):
        rows = pl.ds(pl.multiple_of(index * size, size), size)
        two = (work[rows, :].astype(F32) * slope2[rows, :].astype(F32)).astype(BF16)
        grad2[rows, :] = two
        one = (dot_t(two, w2[...]) * slope1[rows, :].astype(F32)).astype(BF16)
        grad1[rows, :] = one
        grad = dot_t(one, w1[...])
        work[rows, :] = grad.astype(BF16)
        sums[...] += row_sums(one.astype(F32), two.astype(F32), grad * zed[rows, :].astype(F32))
        return carry

    lax.fori_loop(0, steps, body, 0)
    for which, start in enumerate((0, plan.points_a)):
        sums[3 + which : 4 + which] = work[start : start + 16, :].astype(F32)[:1]
        sums[5 + which : 6 + which] = zed[start : start + 16, :].astype(F32)[:1]
    from_points(plan, work, (tat, tbt), (pa, pb))
    repack(plan, pa, pb, out)


def pack_kernel(plan, place, products, backs, dcs, norm2, cot, norm1, shift, gain, bias, out):
    half, blocks = plan.half, plan.half // BS
    out[...] = jnp.zeros_like(out)
    for kind in range(2):
        for h in range(2):
            product = products[kind][h]
            for b in range(blocks):
                rows = slice(b * BS, (b + 1) * BS)
                late = slice(half + b * BS, half + (b + 1) * BS)
                real = product[rows, rows] + product[late, late]
                imag = product[rows, late] - product[late, rows]
                lanes = slice(h * half + b * BS, h * half + (b + 1) * BS)
                out[2 * kind * BS : (2 * kind + 1) * BS, lanes] = real
                out[(2 * kind + 1) * BS : (2 * kind + 2) * BS, lanes] = imag
    row = 4 * BS
    for kind in range(2):
        for part in range(2):
            for h in range(2):
                out[row : row + 1, h * half : (h + 1) * half] = backs[h][
                    kind : kind + 1, part * half : (part + 1) * half
                ]
            row += 1
    out[row : row + 2] = norm2[0:2]
    out[row + 2 : row + 3] = cot[0:1]
    row += 3
    first = jnp.where(place[0] == 0, 1.0, 0.0)
    roots = [math.sqrt(H_A * plan.columns_a), math.sqrt(H_B * plan.columns_b)]
    for h in range(2):
        lanes = slice(h * half, (h + 1) * half)
        total = backs[h][2:3, :half] + backs[h][2:3, half:]
        plain = norm1[1:2, lanes]
        for which in range(2):
            grad = backs[h][3 + which : 4 + which, :half] * first
            exact = dcs[h][which : which + 1] - bias[:, lanes] * roots[which]
            total += grad * (exact - backs[h][5 + which : 6 + which, :half])
            plain += grad * roots[which]
        out[row : row + 1, lanes] = norm1[0:1, lanes] + total / gain[:, lanes]
        out[row + 1 : row + 2, lanes] = plain
    row += 2
    for n in range(4):
        out[row + n : row + n + 1] = shift[pl.ds(n ^ place[1], 1), :]


def swap(value, axis, distance):
    size = lax.axis_size(axis)
    return lax.ppermute(value, axis, [(i, i ^ distance) for i in range(size)])


def halve(value, axis, distance):
    size = value.shape[0] // 2
    bit = (lax.axis_index(axis) // distance) % 2
    keep = lax.dynamic_slice_in_dim(value, bit * size, size)
    send = lax.dynamic_slice_in_dim(value, (1 - bit) * size, size)
    return keep, send


def join(value, axis, distance):
    other = swap(value, axis, distance)
    bit = (lax.axis_index(axis) // distance) % 2
    return jnp.where(
        bit == 0, jnp.concatenate([value, other]), jnp.concatenate([other, value])
    )


def add_up(value, links, kind):
    for axis, distance in links:
        keep, send = halve(value, axis, distance)
        value = keep + swap(send.astype(kind), axis, distance).astype(F32)
    value = value.astype(kind)
    for axis, distance in reversed(links):
        value = join(value, axis, distance)
    return value


def powers(size):
    return [1 << k for k in range(size.bit_length() - 1)]


def fast_device(
    plan,
    field_a,
    field_b,
    cotangent_a,
    cotangent_b,
    offsets_a,
    offsets_b,
    first_gain,
    first_bias,
    inner_weight,
    inner_bias,
    outer_weight,
    outer_bias,
    second_gain,
    second_norm_bias,
    expand_weight,
    expand_bias,
    reduce_weight,
    reduce_bias,
):
    width, local, half = plan.width, plan.local, plan.half
    blocks = half // BS
    tokens, units = plan.tokens, plan.units
    myself = lax.axis_index("wide")
    xa = field_a.reshape(plan.rows_a, plan.columns_a, local)
    xb = field_b.reshape(plan.rows_b, plan.columns_b, local)
    ca = cotangent_a.reshape(plan.rows_a, plan.columns_a, local)
    cb = cotangent_b.reshape(plan.rows_b, plan.columns_b, local)
    gain1 = first_gain.astype(F32)[None]
    bias1 = first_bias.astype(F32)[None]
    gain2 = second_gain.astype(F32)[None]
    bias2 = second_norm_bias.astype(F32)[None]
    tables = [
        column_tables(plan.columns_a, plan.spread_a, width, 1, tokens),
        column_tables(plan.columns_b, plan.spread_b, width, 2, tokens),
    ]
    forward = np.stack([pair[0] for pair in tables])
    inverse = np.stack([pair[1] for pair in tables])
    depth = width * plan.piece
    fwd_w_t = jnp.asarray(forward.transpose(0, 2, 1).astype(jnp.bfloat16))
    inv_w_t = jnp.asarray(inverse.astype(jnp.bfloat16))
    inv_w = jnp.asarray(inverse.transpose(0, 2, 1).astype(jnp.bfloat16))
    fine = forward.astype(jnp.bfloat16)
    rest = (forward - fine.astype(np.float64)).astype(jnp.bfloat16)
    fwd_w = jnp.asarray(np.stack([fine, rest], axis=1))
    vector = pl.BlockSpec((1, local), lambda i: (0, 0))
    sums_spec = pl.BlockSpec((PAD, local), lambda i: (0, 0))
    sums_shape = jax.ShapeDtypeStruct((PAD, local), F32)
    scratch = pltpu.VMEM((tokens, local), F32)
    counts = jnp.stack(
        [offsets_a[myself + 1] - offsets_a[myself], offsets_b[myself + 1] - offsets_b[myself]]
    )
    count_spec = pl.BlockSpec(memory_space=pltpu.SMEM)

    def exchange(parts):
        return [lax.all_to_all(part, "wide", 0, 0, tiled=True) for part in parts]

    sends = call(
        functools.partial(first_kernel, plan),
        (units,),
        [plan.spec_a(), plan.spec_b(), vector, vector, plan.table((2, depth, tokens))],
        [plan.sends(), plan.sends()],
        [plan.exchange_shape()] * 2,
        [scratch],
    )(xa, xb, gain1, bias1, fwd_w)
    arrived = exchange(sends)

    own = (expand_weight, expand_bias, reduce_weight)
    far = tuple(swap(part, "narrow", 2) for part in own)
    near = tuple(swap(part, "narrow", 1) for part in own)
    cross = tuple(swap(part, "narrow", 1) for part in far)
    chunks = (own, near, far, cross)
    expand = jnp.concatenate([chunk[0] for chunk in chunks], axis=1)
    expand_b = jnp.concatenate([chunk[1] for chunk in chunks]).astype(F32)
    reduce = jnp.concatenate([chunk[2] for chunk in chunks], axis=0)

    cot, cot_sums = call(
        functools.partial(cotangent_kernel, plan),
        (units,),
        [count_spec, plan.spec_a(), plan.spec_b()],
        [plan.unit(), sums_spec],
        [plan.units_shape(BF16), sums_shape],
        [scratch],
    )(counts, ca, cb)
    cot_rows = cot.reshape(units * tokens, local)
    grad_hidden = dot_t(cot_rows, reduce).astype(BF16)

    table = []
    for offsets, height, rows, padded in (
        (offsets_a, H_A, plan.rows_a, plan.pad_a),
        (offsets_b, H_B, plan.rows_b, plan.pad_b),
    ):
        line, valid = row_slots(offsets, rows, width)
        table.append(jnp.stack(halves(row_table(height, line, valid, padded))))
    row_tables = (table[0], table[1], table[0][0].T, table[1][0].T)
    ones = [half_weight(inner_weight, h, blocks) for h in range(2)]
    twos = [half_weight(outer_weight, h, blocks) for h in range(2)]
    shift1 = inner_bias.astype(F32).reshape(2, 2, half)
    shift2 = outer_bias.astype(F32).reshape(2, 2, half)
    points_shape = jax.ShapeDtypeStruct((plan.points, 2 * half), BF16)
    points_spec = pl.BlockSpec((plan.points, 2 * half), lambda: (0, 0))
    exchange_spec = pl.BlockSpec((width, units, plan.piece, half), lambda: (0, 0, 0, 0))
    parts_scratch = [
        pltpu.VMEM((half // LANES, width * plan.rows_a * plan.piece, LANES), F32),
        pltpu.VMEM((half // LANES, width * (units - plan.rows_a) * plan.piece, LANES), F32),
        pltpu.VMEM((plan.points, 2 * half), BF16),
    ]
    steps = 5 if plan.points % 80 == 0 else 1
    kept, outgoing = [], []
    ready = ((far[0], far[2], cot), (expand, reduce))
    for h in range(2):
        operands = (
            arrived[h],
            *row_tables,
            ones[h],
            shift1[:, h].reshape(1, 2 * half),
            twos[h],
            shift2[:, h].reshape(1, 2 * half),
        )
        got = call(
            functools.partial(spectral_kernel, plan, steps),
            (),
            [whole(item) for item in operands],
            [exchange_spec] + [points_spec] * 4 + [pl.BlockSpec((PAD, half), lambda: (0, 0))],
            [plan.exchange_shape()] + [points_shape] * 4 + [jax.ShapeDtypeStruct((PAD, half), F32)],
            parts_scratch,
            after=len(ready[h]),
        )(*operands, *ready[h])
        outgoing.append(got[0])
        kept.append(got[1:])
    returned = exchange(outgoing)

    middle, normed = call(
        functools.partial(middle_kernel, plan),
        (units,),
        [plan.spec_a(), plan.spec_b(), plan.sends(), plan.sends()]
        + [vector] * 4
        + [plan.table((tokens, depth))],
        [plan.unit(), plan.unit()],
        [plan.units_shape(F32), plan.units_shape(BF16)],
        [scratch],
        after=1,
    )(xa, xb, *returned, gain1, bias1, gain2, bias2, inv_w, grad_hidden)
    rows = normed.reshape(units * tokens, local)
    pre = dot(rows, expand) + expand_b
    cdf = 0.5 * (1.0 + lax.erf(pre * ROOT_HALF))
    hidden = (pre * cdf).astype(BF16)
    slope = cdf + pre * jnp.exp(-0.5 * pre * pre) / ROOT_TWO_PI
    grad_pre = (grad_hidden.astype(F32) * slope).astype(BF16)
    grad_rows = dot_t(grad_pre, expand).astype(BF16)

    dmid, send0, send1, norm2_sums = call(
        functools.partial(middle_back_kernel, plan),
        (units,),
        [plan.unit(), plan.unit(), plan.unit(), vector, plan.table((depth, tokens))],
        [plan.unit(), plan.sends(), plan.sends(), sums_spec],
        [plan.units_shape(F32), plan.exchange_shape(), plan.exchange_shape(), sums_shape],
    )(grad_rows.reshape(units, tokens, local), middle, cot, gain2, inv_w_t)
    arrived = exchange((send0, send1))

    hidden_units = hidden.reshape(units, tokens, -1)
    hidden_size = hidden.shape[-1]
    over_tokens = (((0,), (0,)), ((), ()))
    grad_reduce = lax.dot_general(hidden, cot_rows, over_tokens, preferred_element_type=F32)
    grad_expand = lax.dot_general(rows, grad_pre, over_tokens, preferred_element_type=F32)
    grad_expand_b = jnp.sum(grad_pre.astype(F32), 0)
    own_units = hidden_size // 4
    shares = [
        (
            grad_reduce[k * own_units : (k + 1) * own_units],
            grad_expand[:, k * own_units : (k + 1) * own_units],
        )
        for k in range(4)
    ]

    def add_from(target, source, distance):
        return tuple(
            t + swap(s.astype(BF16), "narrow", distance).astype(F32)
            for t, s in zip(target, source, strict=True)
        )

    outgoing, products, backs = [], ([], []), []
    for h in range(2):
        zed, act, slope1, slope2, _ = kept[h]
        operands = (
            arrived[h],
            *row_tables,
            ones[h],
            twos[h],
            slope1,
            slope2,
            zed,
        )
        out, grad1, grad2, sums = call(
            functools.partial(spectral_back_kernel, plan, steps),
            (),
            [whole(item) for item in operands],
            [exchange_spec, points_spec, points_spec, pl.BlockSpec((PAD, 2 * half), lambda: (0, 0))],
            [
                plan.exchange_shape(),
                points_shape,
                points_shape,
                jax.ShapeDtypeStruct((PAD, 2 * half), F32),
            ],
            parts_scratch,
        )(*operands)
        outgoing.append(out)
        backs.append(sums)
        for index, (left, right) in enumerate(((zed, grad1), (act, grad2))):
            products[index].append(
                lax.dot_general(left, right, over_tokens, preferred_element_type=F32)
            )
    returned = exchange(outgoing)
    mixed_a, mixed_b, norm1_sums = call(
        functools.partial(mixed_kernel, plan),
        (units,),
        [
            count_spec,
            plan.unit(hidden_size),
            pl.BlockSpec((hidden_size, local), lambda i: (0, 0)),
            vector,
            plan.unit(),
            plan.unit(),
            plan.spec_a(),
            plan.spec_b(),
        ],
        [*plan.outs(), sums_spec],
        [
            jax.ShapeDtypeStruct(field_a.shape, BF16),
            jax.ShapeDtypeStruct(field_b.shape, BF16),
            sums_shape,
        ],
        [scratch],
        after=1,
    )(counts, hidden_units, reduce, reduce_bias.astype(F32)[None], middle, dmid, xa, xb, grad1)
    sum_own = add_from(shares[0], shares[1], 1)
    sum_far = add_from(shares[2], shares[3], 1)
    sum_own = add_from(sum_own, sum_far, 2)
    wide_links = [("wide", d) for d in powers(width)]
    mlp_sums = add_up(jnp.concatenate(sum_own), wide_links, BF16).astype(F32)


    grad_a, grad_b = call(
        functools.partial(last_kernel, plan),
        (units,),
        [plan.spec_a(), plan.spec_b(), plan.sends(), plan.sends(), plan.unit(), vector]
        + [plan.table((tokens, depth))],
        plan.outs(),
        [
            jax.ShapeDtypeStruct(field_a.shape, F32),
            jax.ShapeDtypeStruct(field_b.shape, F32),
        ],
        [scratch],
    )(xa, xb, *returned, dmid, gain1, fwd_w_t)

    place = jnp.stack([myself, lax.axis_index("narrow")])
    flat = (
        *products[0],
        *products[1],
        *backs,
        kept[0][4],
        kept[1][4],
        norm2_sums,
        cot_sums,
        norm1_sums,
        grad_expand_b.reshape(4, -1),
        gain1,
        bias1,
    )

    def pack_body(place, *refs):
        pack_kernel(
            plan, place, (refs[0:2], refs[2:4]), refs[4:6], refs[6:8], *refs[8:]
        )

    links = [("narrow", d) for d in powers(4)] + wide_links
    rows = round_up(4 * BS + 13, 8 << len(links))
    pack = call(
        pack_body,
        (),
        [count_spec] + [whole(item) for item in flat],
        pl.BlockSpec((rows, local), lambda: (0, 0)),
        jax.ShapeDtypeStruct((rows, local), F32),
    )(place, *flat)
    pack = add_up(pack, links, F32)
    matrices = pack[: 4 * BS].reshape(2, 2, BS, local)
    small = pack[4 * BS : 4 * BS + 13]
    own_row = lax.dynamic_slice_in_dim(small, 9 + place[1], 1)[0]
    own_depth = mlp_sums.shape[0] // 2
    return (
        mixed_a,
        mixed_b,
        grad_a,
        grad_b,
        small[7],
        small[8],
        matrices[0],
        small[0:2],
        matrices[1],
        small[2:4],
        small[4],
        small[5],
        mlp_sums[own_depth:],
        own_row,
        mlp_sums[:own_depth],
        small[6],
    )


def choose(field_a, field_b, *rest):
    plan = Plan(
        lax.axis_size("wide"),
        field_a.shape[0],
        field_a.shape[2],
        field_b.shape[0],
        field_b.shape[2],
        field_a.shape[3],
    )
    alone = field_a.shape[1] == 1 and field_b.shape[1] == 1
    if plan.fits() and alone and lax.axis_size("narrow") == 4:
        return fast_device(plan, field_a, field_b, *rest)
    return general_device(field_a, field_b, *rest)


def solution(mesh):
    placed = (
        P("wide", "narrow", None, None),
        P("wide", "narrow", None, None),
        P("wide", "narrow", None, None),
        P("wide", "narrow", None, None),
        P(),
        P(),
        P(),
        P(),
        P(),
        P(),
        P(),
        P(),
        P(),
        P(),
        P(None, "narrow"),
        P("narrow"),
        P("narrow", None),
        P(),
    )
    return jax.shard_map(
        choose,
        mesh=mesh,
        in_specs=placed,
        out_specs=(
            P("wide", "narrow", None, None),
            P("wide", "narrow", None, None),
            P("wide", "narrow", None, None),
            P("wide", "narrow", None, None),
            P(),
            P(),
            P(),
            P(),
            P(),
            P(),
            P(),
            P(),
            P(None, "narrow"),
            P("narrow"),
            P("narrow", None),
            P(),
        ),
        check_vma=False,
    )
```

```python
import functools
import math

import jax
import jax.numpy as jnp
import numpy as np
from jax import lax
from jax.experimental import pallas as pl
from jax.experimental.pallas import tpu as pltpu
from jax.sharding import PartitionSpec as P

NBL = 8
BS = 96
H_A = 90
H_B = 45


EPSILON = 1e-05
SHRINK = 0.01
HIGH = lax.Precision.HIGHEST
ROOT_HALF = 0.7071067811865476
ROOT_TWO_PI = 2.5066282746310002


def gelu_value(value):
    return 0.5 * value * (1.0 + lax.erf(value * ROOT_HALF))


def gelu_slope(value):
    return (
        0.5 * (1.0 + lax.erf(value * ROOT_HALF))
        + value * jnp.exp(-0.5 * value * value) / ROOT_TWO_PI
    )


def shrink_value(value):
    return value - SHRINK * jnp.tanh(value / SHRINK)


def shrink_slope(value):
    bent = jnp.tanh(value / SHRINK)
    return bent * bent


def phase(left, right, length):
    turns = left * right % length
    return turns.astype(jnp.float32) * (2.0 * math.pi / length)


def row_slots(offsets, depth, width):
    offset = jnp.arange(depth, dtype=jnp.int32)
    begin = offsets[:width]
    counts = offsets[1:] - begin
    line = (begin[:, None] + offset[None, :]).reshape(-1)
    valid = (offset[None, :] < counts[:, None]).reshape(-1).astype(jnp.float32)
    return (line, valid)


def column_slots(freqs, spread, width):
    edges = jnp.arange(width + 1, dtype=jnp.int32) * freqs // width
    offset = jnp.arange(spread, dtype=jnp.int32)
    begin = edges[:width]
    valid = (offset[None, :] < (edges[1:] - begin)[:, None]).reshape(-1).astype(jnp.float32)
    return ((begin[:, None] + offset[None, :]).reshape(-1), valid)


def forward_w_table(columns, freq, valid, width, spread):
    angle = phase(jnp.arange(columns, dtype=jnp.int32)[:, None], freq[None, :], columns)
    scale = valid[None, :] / math.sqrt(columns)
    table = jnp.stack([jnp.cos(angle) * scale, -jnp.sin(angle) * scale], axis=1)
    return table.reshape(columns, 2, width, spread)


def inverse_w_table(columns, freq, valid, width, spread):
    angle = phase(freq[:, None], jnp.arange(columns, dtype=jnp.int32)[None, :], columns)
    edge = (freq == 0) | (2 * freq == columns)
    weight = jnp.where(edge, 1.0, 2.0) * valid / math.sqrt(columns)
    real = jnp.cos(angle) * weight[:, None]
    imag = jnp.where(edge[:, None], 0.0, -jnp.sin(angle)) * weight[:, None]
    return jnp.stack([real, imag], axis=1).reshape(width, spread, 2, columns)


def forward_h_table(height, line, valid):
    angle = phase(jnp.arange(height, dtype=jnp.int32)[:, None], line[None, :], height)
    scale = valid[None, :] / math.sqrt(height)
    cosine = jnp.cos(angle) * scale
    sine = jnp.sin(angle) * scale
    upper = jnp.stack([cosine, sine], axis=-1)
    lower = jnp.stack([-sine, cosine], axis=-1)
    return jnp.stack([upper, lower], axis=1)


def inverse_h_table(height, line, valid):
    angle = phase(line[:, None], jnp.arange(height, dtype=jnp.int32)[None, :], height)
    scale = valid[:, None] / math.sqrt(height)
    cosine = jnp.cos(angle) * scale
    sine = jnp.sin(angle) * scale
    upper = jnp.stack([cosine, -sine], axis=-1)
    lower = jnp.stack([sine, cosine], axis=-1)
    return jnp.stack([upper, lower], axis=1)


def complex_weight(weight):
    blocked = weight.reshape(2, BS, NBL, BS).transpose(0, 2, 1, 3)
    return jnp.stack([jnp.stack([blocked[0], blocked[1]]), jnp.stack([-blocked[1], blocked[0]])])


def fold_weight(grad):
    folded = jnp.stack([grad[0, 0] + grad[1, 1], grad[0, 1] - grad[1, 0]])
    return folded.transpose(0, 2, 1, 3).reshape(2, BS, NBL * BS)


def general_device(
    field_a,
    field_b,
    cotangent_a,
    cotangent_b,
    offsets_a,
    offsets_b,
    first_gain,
    first_bias,
    inner_weight,
    inner_bias,
    outer_weight,
    outer_bias,
    second_gain,
    second_norm_bias,
    expand_weight,
    expand_bias,
    reduce_weight,
    reduce_bias,
):
    width = lax.axis_size("wide")
    myself = lax.axis_index("wide")
    local = field_a.shape[-1]
    layouts = []
    for field, offsets, height in ((field_a, offsets_a, H_A), (field_b, offsets_b, H_B)):
        depth, snaps, columns = (field.shape[0], field.shape[1], field.shape[2])
        freqs = columns // 2 + 1
        spread = (freqs + width - 1) // width
        line, row_valid = row_slots(offsets, depth, width)
        freq, freq_valid = column_slots(freqs, spread, width)
        layouts.append(
            (
                depth,
                snaps,
                columns,
                spread,
                height,
                forward_w_table(columns, freq, freq_valid, width, spread),
                inverse_w_table(columns, freq, freq_valid, width, spread),
                forward_h_table(height, line, row_valid),
                inverse_h_table(height, line, row_valid),
                lax.dynamic_slice_in_dim(row_valid, myself * depth, depth),
            )
        )
    token_count = layouts[0][0] * layouts[0][1] * layouts[0][2]
    point_count = layouts[0][4] * layouts[0][1] * layouts[0][3]

    def to_grids(tokens):
        return [
            tokens[:token_count].reshape(
                layouts[0][0], layouts[0][1], layouts[0][2], tokens.shape[-1]
            ),
            tokens[token_count:].reshape(
                layouts[1][0], layouts[1][1], layouts[1][2], tokens.shape[-1]
            ),
        ]

    def to_tokens(parts):
        return jnp.concatenate([piece.reshape(-1, piece.shape[-1]) for piece in parts])

    def to_spectra(points):
        pieces = (points[:point_count], points[point_count:])
        return [
            pieces[index].reshape(layouts[index][4], layouts[index][1], layouts[index][3], 2, local)
            for index in range(2)
        ]

    def to_sends(parts):
        return [
            parts[index].reshape(
                width, layouts[index][0], layouts[index][1], layouts[index][3], 2, local
            )
            for index in range(2)
        ]

    mask = to_tokens(
        [
            jnp.broadcast_to(lay[9][:, None, None, None], (lay[0], lay[1], lay[2], 1))
            for lay in layouts
        ]
    )
    first_norm_gain = first_gain.astype(jnp.float32)
    first_norm_bias = first_bias.astype(jnp.float32)
    bias_out = reduce_bias.astype(jnp.float32)
    weight_one = complex_weight(inner_weight)
    weight_two = complex_weight(outer_weight)
    shift_one = inner_bias.astype(jnp.float32).reshape(2, NBL, BS)
    shift_two = outer_bias.astype(jnp.float32).reshape(2, NBL, BS)
    source = jnp.concatenate([field_a.reshape(-1, local), field_b.reshape(-1, local)]).astype(
        jnp.float32
    )
    mean_one = jnp.mean(source, axis=1, keepdims=True)
    first_centered_input = source - mean_one
    first_inverse_deviation = lax.rsqrt(
        jnp.mean(first_centered_input * first_centered_input, axis=1, keepdims=True) + EPSILON
    )
    first_standardized = first_centered_input * first_inverse_deviation
    normalized_rows = first_standardized * first_norm_gain + first_norm_bias
    normed_parts = to_grids(normalized_rows)
    sends = [
        jnp.einsum(
            "rswc,wtjk->jrsktc", normed_parts[index], layouts[index][5], precision=HIGH
        ).astype(jnp.bfloat16)
        for index in range(2)
    ]
    arrived = (
        lax.all_to_all(sends[0], "wide", split_axis=0, concat_axis=1, tiled=True),
        lax.all_to_all(sends[1], "wide", split_axis=0, concat_axis=1, tiled=True),
    )
    spectra = [
        jnp.einsum(
            "kumt,msqtc->ksquc",
            layouts[index][7],
            arrived[index][0].astype(jnp.float32),
            precision=HIGH,
        )
        for index in range(2)
    ]
    zed = jnp.concatenate([piece.reshape(-1, 2, NBL, BS) for piece in spectra]).astype(jnp.bfloat16)
    pre_one = (
        jnp.einsum("pcbi,cdbio->pdbo", zed, weight_one, preferred_element_type=jnp.float32)
        + shift_one
    )
    act_one = gelu_value(pre_one).astype(jnp.bfloat16)
    pre_two = (
        jnp.einsum("pcbi,cdbio->pdbo", act_one, weight_two, preferred_element_type=jnp.float32)
        + shift_two
    )
    shrunk = to_spectra(shrink_value(pre_two))
    outgoing = to_sends(
        [
            jnp.einsum(
                "mukt,ksqtc->msquc", layouts[index][8], shrunk[index], precision=HIGH
            ).astype(jnp.bfloat16)
            for index in range(2)
        ]
    )
    returned = (
        lax.all_to_all(outgoing[0], "wide", split_axis=0, concat_axis=1, tiled=True),
        lax.all_to_all(outgoing[1], "wide", split_axis=0, concat_axis=1, tiled=True),
    )
    field_parts = to_grids(source)
    middle_parts = []
    for index in range(2):
        lay = layouts[index]
        received = (
            returned[index][0].reshape(width, lay[0], lay[1], lay[3], 2, local).astype(jnp.float32)
        )
        middle_parts.append(
            jnp.einsum("jrsktc,jktw->rswc", received, lay[6], precision=HIGH)
            + normed_parts[index]
            + field_parts[index]
        )
    middle = to_tokens(middle_parts)
    mean_two = jnp.mean(middle, axis=1, keepdims=True)
    second_centered_input = middle - mean_two
    second_inverse_deviation = lax.rsqrt(
        jnp.mean(second_centered_input * second_centered_input, axis=1, keepdims=True) + EPSILON
    )
    second_standardized = second_centered_input * second_inverse_deviation
    second_norm_gain = second_gain.astype(jnp.float32)
    input_rows = (
        second_standardized * second_norm_gain + second_norm_bias.astype(jnp.float32)
    ).astype(jnp.bfloat16)
    full_inputs = lax.all_gather(input_rows, "narrow", axis=0, tiled=True)
    pre_three = jnp.dot(
        full_inputs, expand_weight, preferred_element_type=jnp.float32
    ) + expand_bias.astype(jnp.float32)
    act_three = gelu_value(pre_three).astype(jnp.bfloat16)
    partial_value = jnp.dot(act_three, reduce_weight, preferred_element_type=jnp.float32)
    mixed = (
        lax.psum_scatter(
            partial_value.astype(jnp.bfloat16), "narrow", scatter_dimension=0, tiled=True
        ).astype(jnp.float32)
        + bias_out
    )
    result = to_grids((middle + mixed) * mask)
    upstream = jnp.concatenate([cotangent_a.reshape(-1, local), cotangent_b.reshape(-1, local)])
    upstream = jnp.where(mask > 0.0, upstream, jnp.zeros_like(upstream))
    upstream_f = upstream.astype(jnp.float32)
    grad_out_b = jnp.sum(upstream_f, 0)
    full_upstream = lax.all_gather(upstream, "narrow", axis=0, tiled=True)
    grad_act = jnp.einsum(
        "td,fd->tf", full_upstream, reduce_weight, preferred_element_type=jnp.float32
    )
    grad_pre = (grad_act * gelu_slope(pre_three)).astype(jnp.bfloat16)
    grad_reduce = jnp.einsum(
        "tf,td->fd", act_three, full_upstream, preferred_element_type=jnp.float32
    )
    grad_expand = jnp.einsum("td,tf->df", full_inputs, grad_pre, preferred_element_type=jnp.float32)
    grad_expand_b = jnp.sum(grad_pre.astype(jnp.float32), 0)
    grad_terms = jnp.einsum(
        "tf,df->td", grad_pre, expand_weight, preferred_element_type=jnp.float32
    )
    input_gradient = lax.psum_scatter(
        grad_terms.astype(jnp.bfloat16), "narrow", scatter_dimension=0, tiled=True
    ).astype(jnp.float32)
    scaled_rows = input_gradient * second_norm_gain
    gradient_second_norm_gain = jnp.sum(input_gradient * second_standardized, 0)
    grad_bias_two = jnp.sum(input_gradient, 0)
    grad_full = second_inverse_deviation * (
        scaled_rows
        - jnp.mean(scaled_rows, axis=1, keepdims=True)
        - second_standardized * jnp.mean(scaled_rows * second_standardized, axis=1, keepdims=True)
    )
    grad_middle = grad_full + upstream_f
    grad_parts = to_grids(grad_middle)
    sends = [
        jnp.einsum(
            "rswc,jktw->jrsktc", grad_parts[index], layouts[index][6], precision=HIGH
        ).astype(jnp.bfloat16)
        for index in range(2)
    ]
    arrived = (
        lax.all_to_all(sends[0], "wide", split_axis=0, concat_axis=1, tiled=True),
        lax.all_to_all(sends[1], "wide", split_axis=0, concat_axis=1, tiled=True),
    )
    grad_points = jnp.concatenate(
        [
            jnp.einsum(
                "mukt,msquc->ksqtc",
                layouts[index][8],
                arrived[index][0].astype(jnp.float32),
                precision=HIGH,
            ).reshape(-1, 2, NBL, BS)
            for index in range(2)
        ]
    )
    grad_two = (grad_points * shrink_slope(pre_two)).astype(jnp.bfloat16)
    grad_hidden = jnp.einsum(
        "pdbo,cdbio->pcbi", grad_two, weight_two, preferred_element_type=jnp.float32
    )
    grad_weight_two = fold_weight(
        jnp.einsum("pcbi,pdbo->cdbio", act_one, grad_two, preferred_element_type=jnp.float32)
    )
    grad_shift_two = jnp.sum(grad_two.astype(jnp.float32), 0).reshape(2, -1)
    grad_one = (grad_hidden * gelu_slope(pre_one)).astype(jnp.bfloat16)
    grad_zed = jnp.einsum(
        "pdbo,cdbio->pcbi", grad_one, weight_one, preferred_element_type=jnp.float32
    )
    grad_weight_one = fold_weight(
        jnp.einsum("pcbi,pdbo->cdbio", zed, grad_one, preferred_element_type=jnp.float32)
    )
    grad_shift_one = jnp.sum(grad_one.astype(jnp.float32), 0).reshape(2, -1)
    grad_spectra = to_spectra(grad_zed)
    outgoing = to_sends(
        [
            jnp.einsum(
                "kumt,ksquc->msqtc", layouts[index][7], grad_spectra[index], precision=HIGH
            ).astype(jnp.bfloat16)
            for index in range(2)
        ]
    )
    returned = (
        lax.all_to_all(outgoing[0], "wide", split_axis=0, concat_axis=1, tiled=True),
        lax.all_to_all(outgoing[1], "wide", split_axis=0, concat_axis=1, tiled=True),
    )
    grad_normed_parts = []
    for index in range(2):
        lay = layouts[index]
        received = (
            returned[index][0].reshape(width, lay[0], lay[1], lay[3], 2, local).astype(jnp.float32)
        )
        grad_normed_parts.append(
            jnp.einsum("jrsktc,wtjk->rswc", received, lay[5], precision=HIGH) + grad_parts[index]
        )
    normalized_gradient = to_tokens(grad_normed_parts)
    scaled_rows = normalized_gradient * first_norm_gain
    grad_source = (
        first_inverse_deviation
        * (
            scaled_rows
            - jnp.mean(scaled_rows, axis=1, keepdims=True)
            - first_standardized * jnp.mean(scaled_rows * first_standardized, axis=1, keepdims=True)
        )
        + grad_middle
    )
    grad_fields = to_grids(grad_source * mask)
    gradient_first_norm_gain = jnp.sum(normalized_gradient * first_standardized, 0)
    grad_bias_one = jnp.sum(normalized_gradient, 0)
    mlp_sums = lax.psum((grad_expand, grad_expand_b, grad_reduce), "wide")
    shared = lax.psum(
        (
            grad_weight_one,
            grad_shift_one,
            grad_weight_two,
            grad_shift_two,
            gradient_first_norm_gain,
            grad_bias_one,
            gradient_second_norm_gain,
            grad_bias_two,
            grad_out_b,
        ),
        ("wide", "narrow"),
    )
    return (
        result[0].astype(jnp.bfloat16),
        result[1].astype(jnp.bfloat16),
        grad_fields[0],
        grad_fields[1],
        shared[4],
        shared[5],
        shared[0],
        shared[1],
        shared[2],
        shared[3],
        shared[6],
        shared[7],
        mlp_sums[0],
        mlp_sums[1],
        mlp_sums[2],
        shared[8],
    )


F32 = jnp.float32
BF16 = jnp.bfloat16
MIB = 1024 * 1024
PAD = 8
LANES = 128
CHUNK = 256
NARROW = 4


def halves(value):
    high = lax.reduce_precision(value, 8, 7)
    return high.astype(BF16), (value - high).astype(BF16)


def round_up(value, unit):
    return -(-value // unit) * unit


def call(kernel, grid, in_specs, out_specs, out_shape, scratch=(), limit=56, after=0):
    first = len(in_specs)

    def body(*refs):
        kernel(*refs[:first], *refs[first + after :])

    return pl.pallas_call(
        body,
        grid=grid,
        in_specs=in_specs + [pl.BlockSpec(memory_space=pl.ANY)] * after,
        out_specs=out_specs,
        out_shape=out_shape,
        scratch_shapes=list(scratch),
        compiler_params=pltpu.CompilerParams(vmem_limit_bytes=limit * MIB),
    )


def whole(array):
    zeros = (0,) * len(array.shape)
    return pl.BlockSpec(array.shape, lambda *_: zeros)


def dot(left, right):
    return jnp.dot(left, right, preferred_element_type=F32)


def dot_t(left, right):
    return lax.dot_general(left, right, (((1,), (1,)), ((), ())), preferred_element_type=F32)


def column_tables(columns, spread, width, repeat, tokens):
    freqs = columns // 2 + 1
    freq = np.arange(width * spread)
    valid = (freq < freqs).astype(np.float64)
    angle = 2.0 * np.pi * (np.outer(freq, np.arange(columns)) % columns) / columns
    scale = valid[:, None] / math.sqrt(columns)
    weight = np.where((freq == 0) | (2 * freq == columns), 1.0, 2.0)[:, None]
    parts = np.stack([np.cos(angle) * scale, -np.sin(angle) * scale], axis=1)
    parts = parts.reshape(width, spread, 2, columns).transpose(0, 2, 1, 3)
    heavy = np.broadcast_to(weight.reshape(width, 1, spread, 1), parts.shape)
    forward = np.zeros((width, repeat, 2, spread, tokens))
    inverse = np.zeros((width, repeat, 2, spread, tokens))
    for index in range(repeat):
        span = slice(index * columns, (index + 1) * columns)
        forward[:, index, :, :, span] = parts
        inverse[:, index, :, :, span] = parts * heavy
    return forward.reshape(-1, tokens), inverse.reshape(-1, tokens)


def row_table(height, line, valid, padded):
    angle = phase(jnp.arange(padded, dtype=jnp.int32)[:, None], line[None, :], height)
    inside = (jnp.arange(padded) < height).astype(F32)[:, None]
    scale = inside * valid[None, :] / math.sqrt(height)
    cosine = jnp.cos(angle) * scale
    sine = jnp.sin(angle) * scale
    upper = jnp.stack([cosine, sine], axis=-1)
    lower = jnp.stack([-sine, cosine], axis=-1)
    return jnp.stack([upper, lower]).reshape(2 * padded, -1)


def layer_norm(value):
    mean = jnp.mean(value, axis=1, keepdims=True)
    centred = value - mean
    scale = lax.rsqrt(jnp.mean(centred * centred, axis=1, keepdims=True) + EPSILON)
    return centred * scale, scale


def layer_norm_back(grad, gain, standard, scale):
    scaled = grad * gain
    return scale * (
        scaled
        - jnp.mean(scaled, axis=1, keepdims=True)
        - standard * jnp.mean(scaled * standard, axis=1, keepdims=True)
    )


def row_sums(*values):
    rows = [jnp.sum(value, axis=0, keepdims=True) for value in values]
    blank = jnp.zeros((PAD - len(rows), rows[0].shape[1]), F32)
    return jnp.concatenate(rows + [blank], axis=0)


class Plan:
    def __init__(self, width, rows_a, columns_a, rows_b, columns_b, local):
        self.width = width
        self.rows_a, self.columns_a = rows_a, columns_a
        self.rows_b, self.columns_b = rows_b, columns_b
        self.local = local
        self.half = local // 2
        self.spread_a = -(-(columns_a // 2 + 1) // width)
        self.spread_b = -(-(columns_b // 2 + 1) // width)
        self.piece = 2 * self.spread_a
        self.units = rows_a + rows_b // 2
        self.group = max(1, math.gcd(rows_a, rows_b // 2))
        self.steps_a = rows_a // self.group
        self.steps = self.units // self.group
        self.tokens = round_up(columns_a, 16)
        self.pad_a = round_up(H_A, 16)
        self.pad_b = round_up(H_B, 16)
        self.points_a = self.spread_a * self.pad_a
        self.points = self.points_a + self.spread_b * self.pad_b

    def fits(self):
        return (
            self.columns_a == 2 * self.columns_b
            and self.spread_a == 2 * self.spread_b
            and self.piece % 8 == 0
            and self.rows_b % 2 == 0
            and self.half % 128 == 0
            and self.half % BS == 0
        )

    def spec_a(self):
        last = self.steps_a - 1
        return pl.BlockSpec(
            (self.group, self.columns_a, self.local), lambda i: (jnp.minimum(i, last), 0, 0)
        )

    def spec_b(self):
        first = self.steps_a
        return pl.BlockSpec(
            (2 * self.group, self.columns_b, self.local),
            lambda i: (jnp.maximum(i - first, 0), 0, 0),
        )

    def rows(self):
        return pl.BlockSpec((self.group * self.tokens, self.local), lambda i: (i, 0))

    def chunks(self):
        return pl.BlockSpec((NARROW, self.group * self.tokens, self.local), lambda i: (0, i, 0))

    def sends(self):
        return pl.BlockSpec(
            (self.width, self.group, self.piece, self.half), lambda i: (0, i, 0, 0)
        )

    def table(self, shape):
        first = self.steps_a
        zeros = (0,) * len(shape)
        return pl.BlockSpec((1,) + shape, lambda i: ((i >= first).astype(jnp.int32),) + zeros)

    def exchange_shape(self):
        return jax.ShapeDtypeStruct((self.width, self.units, self.piece, self.half), BF16)

    def full_sends(self):
        return pl.BlockSpec(
            (self.width, self.group, self.piece, self.local), lambda i: (0, i, 0, 0)
        )

    def full_shape(self):
        return jax.ShapeDtypeStruct((self.width, self.units, self.piece, self.local), BF16)

    def rows_shape(self, kind):
        return jax.ShapeDtypeStruct((self.units * self.tokens, self.local), kind)

    def chunks_shape(self):
        return jax.ShapeDtypeStruct((NARROW, self.units * self.tokens, self.local), BF16)

    def scratch(self):
        return pltpu.VMEM((self.group * self.tokens, self.local), F32)

    def load(self, step, a_ref, b_ref, scratch):
        @pl.when(step == 0)
        def _():
            scratch[...] = jnp.zeros_like(scratch)

        @pl.when(step < self.steps_a)
        def _():
            for u in range(self.group):
                base = u * self.tokens
                scratch[base : base + self.columns_a] = a_ref[u].astype(F32)

        @pl.when(step >= self.steps_a)
        def _():
            for u in range(self.group):
                base = u * self.tokens
                middle = base + self.columns_b
                scratch[base:middle] = b_ref[2 * u].astype(F32)
                scratch[middle : base + self.columns_a] = b_ref[2 * u + 1].astype(F32)

        return scratch[...]

    def parts(self, value):
        return [value[u * self.tokens : (u + 1) * self.tokens] for u in range(self.group)]

    def outs(self):
        last, first = self.steps_a - 1, self.steps_a
        return [
            pl.BlockSpec(
                (self.group, 1, self.columns_a, self.local),
                lambda i: (jnp.minimum(i, last), 0, 0, 0),
            ),
            pl.BlockSpec(
                (2 * self.group, 1, self.columns_b, self.local),
                lambda i: (jnp.maximum(i - first, 0), 0, 0, 0),
            ),
        ]

    def flat_outs(self):
        last, first = self.steps_a - 1, self.steps_a
        return [
            pl.BlockSpec(
                (self.group, self.columns_a, 1, self.local),
                lambda i: (jnp.minimum(i, last), 0, 0, 0),
            ),
            pl.BlockSpec(
                (2 * self.group, self.columns_b, 1, self.local),
                lambda i: (jnp.maximum(i - first, 0), 0, 0, 0),
            ),
        ]

    def store(self, step, value, a_ref, b_ref):
        units = self.parts(value)

        @pl.when(step < self.steps_a)
        def _():
            for u in range(self.group):
                a_ref[u, 0] = units[u][: self.columns_a].astype(a_ref.dtype)

        @pl.when(step >= self.steps_a)
        def _():
            for u in range(self.group):
                b_ref[2 * u, 0] = units[u][: self.columns_b].astype(b_ref.dtype)
                b_ref[2 * u + 1, 0] = units[u][self.columns_b : self.columns_a].astype(b_ref.dtype)

    def store_flat(self, step, value, a_ref, b_ref):
        units = self.parts(value)

        @pl.when(step < self.steps_a)
        def _():
            for u in range(self.group):
                a_ref[u, :, 0, :] = units[u][: self.columns_a]

        @pl.when(step >= self.steps_a)
        def _():
            for u in range(self.group):
                b_ref[2 * u, :, 0, :] = units[u][: self.columns_b]
                b_ref[2 * u + 1, :, 0, :] = units[u][self.columns_b : self.columns_a]

    def put_sends(self, product, unit, refs):
        size = self.local // len(refs)
        for index, ref in enumerate(refs):
            lanes = product[:, index * size : (index + 1) * size]
            ref[:, unit] = lanes.reshape(self.width, self.piece, size).astype(BF16)

    def from_sends(self, table, refs):
        depth = self.width * self.piece
        units = []
        for u in range(self.group):
            size = self.local // len(refs)
            parts = [ref[:, u].astype(F32).reshape(depth, size).astype(BF16) for ref in refs]
            units.append(jnp.concatenate([dot(table, part) for part in parts], axis=1))
        return jnp.concatenate(units, axis=0)

    def valid_rows(self, step, counts, shape):
        row = lax.broadcasted_iota(jnp.int32, shape, 0)
        inside = row >= 0
        used = row < 0
        for u in range(self.group):
            token = row - u * self.tokens
            here = (token >= 0) & (token < self.columns_a)
            in_a = (step < self.steps_a) & (step * self.group + u < counts[0])
            pair = 2 * ((step - self.steps_a) * self.group + u)
            in_b0 = (step >= self.steps_a) & (pair < counts[1])
            in_b1 = (step >= self.steps_a) & (pair + 1 < counts[1])
            first = (in_a | in_b0).astype(jnp.int32)
            second = (in_a | in_b1).astype(jnp.int32)
            flag = jnp.where(token < self.columns_b, first, second)
            used = used | (here & (flag > 0))
        return used


def first_kernel(plan, xa, xb, gain, bias, table, out0, out1, scratch):
    step = pl.program_id(0)
    standard, _ = layer_norm(plan.load(step, xa, xb, scratch))
    for u, part in enumerate(plan.parts(standard * gain[...] + bias[...])):
        high, low = halves(part)
        spectrum = dot(table[0, 0], high) + (dot(table[0, 0], low) + dot(table[0, 1], high))
        plan.put_sends(spectrum, u, (out0, out1))


def cotangent_kernel(plan, counts, ca, cb, out, sums, scratch):
    step = pl.program_id(0)
    value = plan.load(step, ca, cb, scratch)
    value = jnp.where(plan.valid_rows(step, counts, value.shape), value, 0.0)
    out[...] = value.astype(BF16)

    @pl.when(step == 0)
    def _():
        sums[...] = jnp.zeros_like(sums)

    sums[...] += row_sums(value)


def gelu_both(value):
    bell = jnp.exp(-0.5 * value * value)
    cdf = 0.5 * (1.0 + lax.erf(value * ROOT_HALF))
    return value * cdf, cdf + value * bell * (1.0 / ROOT_TWO_PI)


def hidden_kernel(cot, w0, w1, w2, w3, out):
    for k, weight in enumerate((w0, w1, w2, w3)):
        out[k] = dot_t(cot[...], weight[...]).astype(BF16)


def middle_kernel(
    plan, xa, xb, got0, got1, gain, bias, gain2, bias2, inv, inv_t, w0, w1, w2, w3, shift, back,
    cot, mid, rows, hidden, grad_pre, dmid, out, sums, shift_sums, scratch,
):
    step = pl.program_id(0)

    @pl.when(step == 0)
    def _():
        sums[...] = jnp.zeros_like(sums)
        shift_sums[...] = jnp.zeros_like(shift_sums)

    value = plan.load(step, xa, xb, scratch)
    standard, _ = layer_norm(value)
    middle = value + standard * gain[...] + bias[...]
    middle += plan.from_sends(inv[0], (got0, got1))
    mid[...] = middle
    standard, scale = layer_norm(middle)
    flat = (standard * gain2[...] + bias2[...]).astype(BF16)
    rows[...] = flat
    weights = (w0, w1, w2, w3)
    grad = None
    for k, weight in enumerate(weights):
        for start in range(0, plan.local, CHUNK):
            lanes = slice(start, start + CHUNK)
            act, slope = gelu_both(dot(flat, weight[:, lanes]) + shift[k : k + 1, lanes])
            hidden[k, :, lanes] = act.astype(BF16)
            pre = back[k, :, lanes].astype(F32) * slope
            grad_pre[k, :, lanes] = pre.astype(BF16)
            shift_sums[k, :1, lanes] += jnp.sum(pre, axis=0, keepdims=True)
        part = dot_t(grad_pre[k], weight[...])
        grad = part if grad is None else grad + part
    sums[...] += row_sums(grad * standard, grad)
    result = cot[...].astype(F32) + layer_norm_back(grad, gain2[...], standard, scale)
    dmid[...] = result
    for u, part in enumerate(plan.parts(result)):
        plan.put_sends(dot(inv_t[0], part.astype(BF16)), u, (out,))


def mixed_kernel(
    plan, counts, hidden, w0, w1, w2, w3, bias, mid, dmid, xa, xb, outa, outb, sums, scratch
):
    step = pl.program_id(0)
    standard, _ = layer_norm(plan.load(step, xa, xb, scratch))
    grad = dmid[...]

    @pl.when(step == 0)
    def _():
        sums[...] = jnp.zeros_like(sums)

    sums[...] += row_sums(grad * standard, grad)
    value = mid[...] + bias[...]
    for k, weight in enumerate((w0, w1, w2, w3)):
        value += dot(hidden[k], weight[...])
    value = jnp.where(plan.valid_rows(step, counts, value.shape), value, 0.0)
    plan.store(step, value, outa, outb)


def products(plan, chunked, plain, first, chunk_left, got=None):
    count, local = plain.shape
    square = (1, local, local)
    chunk = pl.BlockSpec((1, count, local), lambda i: (2 * i + first, 0, 0))
    flat = pl.BlockSpec((count, local), lambda i: (0, 0))
    each = pl.BlockSpec(square, lambda i: (i, 0, 0))
    whole_out = pl.BlockSpec((local, local), lambda i: (0, 0))
    one = jax.ShapeDtypeStruct((local, local), BF16)

    def kernel(chunk_ref, plain_ref, *refs):
        pair = (chunk_ref[0], plain_ref[...])
        value = lax.dot_general(
            *(pair if chunk_left else pair[::-1]),
            (((0,), (0,)), ((), ())),
            preferred_element_type=F32,
        )
        if got is None:
            refs[0][0] = value.astype(BF16)
            return
        value += refs[0][0].astype(F32)
        for k in range(2):

            @pl.when(pl.program_id(0) == k)
            def _(k=k):
                refs[1 + k][...] = value.astype(BF16)

    if got is None:
        return call(
            kernel, (2,), [chunk, flat], each, jax.ShapeDtypeStruct((2, local, local), BF16)
        )(chunked, plain)
    return call(kernel, (2,), [chunk, flat, each], [whole_out] * 2, [one] * 2)(
        chunked, plain, got
    )


def last_kernel(plan, xa, xb, got, dmid, gain, table, outa, outb, scratch):
    step = pl.program_id(0)
    standard, scale = layer_norm(plan.load(step, xa, xb, scratch))
    passed = dmid[...]
    grad = plan.from_sends(table[0], (got,)) + passed
    total = passed + layer_norm_back(grad, gain[...], standard, scale)
    plan.store_flat(step, total, outa, outb)


def weights_kernel(plan, inner, outer, inner0, inner1, outer0, outer1):
    half = plan.half
    for weight, outs in ((inner, (inner0, inner1)), (outer, (outer0, outer1))):
        parts = [weight[k].astype(F32) for k in range(2)]
        for h, out in enumerate(outs):
            out[...] = jnp.zeros_like(out)
            for b in range(half // BS):
                lanes = slice(h * half + b * BS, h * half + (b + 1) * BS)
                near = slice(b * BS, (b + 1) * BS)
                late = slice(half + b * BS, half + (b + 1) * BS)
                real, imag = parts[0][:, lanes].astype(BF16), parts[1][:, lanes].astype(BF16)
                out[near, near] = real
                out[late, late] = real
                out[near, late] = imag
                out[late, near] = -imag


def nothing(*refs):
    return None


def hold(value, *before):
    anywhere = pl.BlockSpec(memory_space=pl.ANY)
    return pl.pallas_call(
        nothing,
        in_specs=[anywhere] * (1 + len(before)),
        out_specs=anywhere,
        out_shape=jax.ShapeDtypeStruct(value.shape, value.dtype),
        input_output_aliases={0: 0},
    )(value, *before)


def bit_of(place, link):
    return (place[link[0]] // link[1]) % 2


def fold_kernel(link, place, left, right, keep, send):
    total = left[...].astype(F32) + right[...].astype(F32)
    size = keep.shape[-2]
    near, far = total[..., :size, :], total[..., size:, :]
    bit = bit_of(place, link)

    @pl.when(bit == 0)
    def _():
        keep[...] = near.astype(keep.dtype)
        send[...] = far.astype(send.dtype)

    @pl.when(bit == 1)
    def _():
        keep[...] = far.astype(keep.dtype)
        send[...] = near.astype(send.dtype)


SMEM = pl.BlockSpec(memory_space=pltpu.SMEM)


def flat_call(kernel, place, operands, shapes, before=()):
    def spec(item):
        zeros = (0,) * len(item.shape)
        return pl.BlockSpec(item.shape, lambda: zeros)

    return call(
        kernel,
        (),
        [SMEM] + [spec(item) for item in operands],
        [spec(item) for item in shapes],
        list(shapes),
        after=len(before),
    )(place, *operands, *before)


def fold(place, link, left, right, *before):
    shape = left.shape[:-2] + (left.shape[-2] // 2, left.shape[-1])
    half = jax.ShapeDtypeStruct(shape, left.dtype)
    return flat_call(
        functools.partial(fold_kernel, link), place, (left, right), (half, half), before
    )


def add_pairs(place, lefts, rights, *before):
    count = len(lefts)

    def kernel(_, *refs):
        for k in range(count):
            value = refs[k][...].astype(F32) + refs[count + k][...].astype(F32)
            refs[2 * count + k][...] = value.astype(BF16)

    shapes = [jax.ShapeDtypeStruct(item.shape, BF16) for item in lefts]
    return flat_call(kernel, place, (*lefts, *rights), shapes, before)


def total(place, parts, *before, kind=None):
    def kernel(_, *refs):
        values = [ref[...].astype(F32) for ref in refs[:-1]]
        while len(values) > 1:
            values = [a + b for a, b in zip(values[::2], values[1::2], strict=True)]
        refs[-1][...] = values[0].astype(refs[-1].dtype)

    return flat_call(
        kernel, place, parts, [jax.ShapeDtypeStruct(parts[0].shape, kind or parts[0].dtype)], before
    )[0]


def join(place, link, mine, other, *before, kind=None):
    size = mine.shape[-2]
    shape = mine.shape[:-2] + (2 * size, mine.shape[-1])

    def kernel(place, mine, other, out):
        bit = bit_of(place, link)

        def put(low, high):
            out[..., :size, :] = low[...].astype(out.dtype)
            out[..., size:, :] = high[...].astype(out.dtype)

        @pl.when(bit == 0)
        def _():
            put(mine, other)

        @pl.when(bit == 1)
        def _():
            put(other, mine)

    return flat_call(
        kernel, place, (mine, other), [jax.ShapeDtypeStruct(shape, kind or mine.dtype)], before
    )[0]


def last_join(place, link, mine, other):
    size, local = mine.shape

    def kernel(place, mine, other, inner, outer, small, whole_pack):
        bit = bit_of(place, link)
        whole_pack[pl.ds(pl.multiple_of(bit * size, size), size), :] = mine[...].astype(F32)
        whole_pack[pl.ds(pl.multiple_of((1 - bit) * size, size), size), :] = other[...].astype(F32)
        for k in range(2):
            inner[k] = whole_pack[k * BS : (k + 1) * BS]
            outer[k] = whole_pack[(2 + k) * BS : (3 + k) * BS]
        small[...] = whole_pack[4 * BS : 4 * BS + small.shape[0]]

    def spec(item):
        zeros = (0,) * len(item.shape)
        return pl.BlockSpec(item.shape, lambda: zeros)

    matrix = jax.ShapeDtypeStruct((2, BS, local), F32)
    shapes = [matrix, matrix, jax.ShapeDtypeStruct((16, local), F32)]
    return call(
        kernel,
        (),
        [SMEM, spec(mine), spec(other)],
        [spec(item) for item in shapes],
        shapes,
        [pltpu.VMEM((2 * size, local), F32)],
    )(place, mine, other)


def unpack(plan, got, part_a, part_b):
    rows_a = plan.rows_a * plan.piece
    rows_b = (plan.units - plan.rows_a) * plan.piece
    for j in range(plan.width):
        value = got[j].astype(F32)
        for part, rows, piece in (
            (part_a, rows_a, value[: plan.rows_a]),
            (part_b, rows_b, value[plan.rows_a :]),
        ):
            for g in range(plan.half // LANES):
                lanes = piece[:, :, g * LANES : (g + 1) * LANES]
                part[g, j * rows : (j + 1) * rows] = lanes.reshape(rows, LANES)


def repack(plan, part_a, part_b, out):
    rows_a = plan.rows_a * plan.piece
    rows_b = (plan.units - plan.rows_a) * plan.piece
    for j in range(plan.width):
        for part, rows, first, last in (
            (part_a, rows_a, 0, plan.rows_a),
            (part_b, rows_b, plan.rows_a, plan.units),
        ):
            for g in range(plan.half // LANES):
                out[j, first:last, :, g * LANES : (g + 1) * LANES] = (
                    part[g, j * rows : (j + 1) * rows]
                    .reshape(last - first, plan.piece, LANES)
                    .astype(BF16)
                )


def grids(plan):
    return (
        (plan.spread_a, plan.pad_a, plan.width * 2 * plan.rows_a, 0, 0),
        (plan.spread_b, plan.pad_b, plan.width * 2 * plan.rows_b, plan.points_a, 1),
    )


def to_points(plan, parts, tables, out, first=None):
    for spread, pad, depth, base, which in grids(plan):
        for f in range(spread):
            lanes = [
                parts[which][g, pl.ds(f, depth, stride=spread), :].astype(BF16)
                for g in range(plan.half // LANES)
            ]
            column = jnp.concatenate(lanes, axis=1)
            product = dot(tables[which][0], column)
            if first is not None:
                product += dot(tables[which][1], column)
                if f == 0:
                    first[which : which + 1] = product[:1]
            out[base + f * pad : base + (f + 1) * pad, :] = jnp.concatenate(
                [product[:pad], product[pad:]], axis=1
            ).astype(out.dtype)


def from_points(plan, points, tables, parts):
    for spread, pad, depth, base, which in grids(plan):
        for f in range(spread):
            value = points[base + f * pad : base + (f + 1) * pad, :]
            column = jnp.concatenate([value[:, : plan.half], value[:, plan.half :]], axis=0)
            product = dot(tables[which][...], column)
            for g in range(plan.half // LANES):
                parts[which][g, pl.ds(f, depth, stride=spread), :] = product[
                    :, g * LANES : (g + 1) * LANES
                ]


def spectral_kernel(
    plan, steps, got, ta, tb, tat, tbt, w1, b1, w2, b2, out, zed, act, slope1, slope2, dc, pa, pb, shrunk
):
    unpack(plan, got, pa, pb)
    dc[...] = jnp.zeros_like(dc)
    to_points(plan, (pa, pb), (ta, tb), zed, dc)
    size = plan.points // steps

    def body(index, carry):
        rows = pl.ds(pl.multiple_of(index * size, size), size)
        pre_one = dot(zed[rows, :], w1[...]) + b1[...]
        cdf = 0.5 * (1.0 + lax.erf(pre_one * ROOT_HALF))
        hidden = (pre_one * cdf).astype(BF16)
        act[rows, :] = hidden
        slope1[rows, :] = (
            cdf + pre_one * jnp.exp(-0.5 * pre_one * pre_one) * (1.0 / ROOT_TWO_PI)
        ).astype(BF16)
        pre_two = dot(hidden, w2[...]) + b2[...]
        bent = jnp.tanh(pre_two * (1.0 / SHRINK))
        shrunk[rows, :] = (pre_two - SHRINK * bent).astype(BF16)
        slope2[rows, :] = (bent * bent).astype(BF16)
        return carry

    lax.fori_loop(0, steps, body, 0)
    from_points(plan, shrunk, (tat, tbt), (pa, pb))
    repack(plan, pa, pb, out)


def spectral_back_kernel(
    plan, steps, skip, got, ta, tb, tat, tbt, w1, w2, slope1, slope2, zed, *refs
):
    out, grad1, grad2, sums, pa, pb, work = refs[skip:]
    unpack(plan, got, pa, pb)
    to_points(plan, (pa, pb), (ta, tb), work)
    size = plan.points // steps
    sums[...] = jnp.zeros_like(sums)

    def body(index, carry):
        rows = pl.ds(pl.multiple_of(index * size, size), size)
        two = (work[rows, :].astype(F32) * slope2[rows, :].astype(F32)).astype(BF16)
        grad2[rows, :] = two
        one = (dot_t(two, w2[...]) * slope1[rows, :].astype(F32)).astype(BF16)
        grad1[rows, :] = one
        grad = dot_t(one, w1[...])
        work[rows, :] = grad.astype(BF16)
        sums[...] += row_sums(one.astype(F32), two.astype(F32), grad * zed[rows, :].astype(F32))
        return carry

    lax.fori_loop(0, steps, body, 0)
    for which, start in enumerate((0, plan.points_a)):
        sums[3 + which : 4 + which] = work[start : start + 16, :].astype(F32)[:1]
        sums[5 + which : 6 + which] = zed[start : start + 16, :].astype(F32)[:1]
    from_points(plan, work, (tat, tbt), (pa, pb))
    repack(plan, pa, pb, out)


def pack_kernel(
    plan, place, products, backs, dcs, norm2, cot, norm1, shift, gain, bias, keep, send, out
):
    half, blocks = plan.half, plan.half // BS
    out[...] = jnp.zeros_like(out)
    for kind in range(2):
        for h in range(2):
            product = products[kind][h]
            for b in range(blocks):
                rows = slice(b * BS, (b + 1) * BS)
                late = slice(half + b * BS, half + (b + 1) * BS)
                real = product[rows, rows] + product[late, late]
                imag = product[rows, late] - product[late, rows]
                lanes = slice(h * half + b * BS, h * half + (b + 1) * BS)
                out[2 * kind * BS : (2 * kind + 1) * BS, lanes] = real
                out[(2 * kind + 1) * BS : (2 * kind + 2) * BS, lanes] = imag
    row = 4 * BS
    for kind in range(2):
        for part in range(2):
            for h in range(2):
                out[row : row + 1, h * half : (h + 1) * half] = backs[h][
                    kind : kind + 1, part * half : (part + 1) * half
                ]
            row += 1
    out[row : row + 2] = norm2[0:2]
    out[row + 2 : row + 3] = cot[0:1]
    row += 3
    first = jnp.where(place[0] == 0, 1.0, 0.0)
    roots = [math.sqrt(H_A * plan.columns_a), math.sqrt(H_B * plan.columns_b)]
    for h in range(2):
        lanes = slice(h * half, (h + 1) * half)
        total = backs[h][2:3, :half] + backs[h][2:3, half:]
        plain = norm1[1:2, lanes]
        for which in range(2):
            grad = backs[h][3 + which : 4 + which, :half] * first
            exact = dcs[h][which : which + 1] - bias[:, lanes] * roots[which]
            total += grad * (exact - backs[h][5 + which : 6 + which, :half])
            plain += grad * roots[which]
        out[row : row + 1, lanes] = norm1[0:1, lanes] + total / gain[:, lanes]
        out[row + 1 : row + 2, lanes] = plain
    row += 2
    for n in range(4):
        out[row + n : row + n + 1] = shift[n ^ place[1], :1]
    size = keep.shape[0]
    mine = pl.multiple_of((place[1] % 2) * size, size)
    keep[...] = out[pl.ds(mine, size), :]
    send[...] = out[pl.ds(size - mine, size), :]


def swap(value, axis, distance):
    size = lax.axis_size(axis)
    return lax.ppermute(value, axis, [(i, i ^ distance) for i in range(size)])


def fast_device(
    plan,
    field_a,
    field_b,
    cotangent_a,
    cotangent_b,
    offsets_a,
    offsets_b,
    first_gain,
    first_bias,
    inner_weight,
    inner_bias,
    outer_weight,
    outer_bias,
    second_gain,
    second_norm_bias,
    expand_weight,
    expand_bias,
    reduce_weight,
    reduce_bias,
):
    width, local, half = plan.width, plan.local, plan.half
    tokens, units = plan.tokens, plan.units
    myself = lax.axis_index("wide")
    xa = field_a.reshape(plan.rows_a, plan.columns_a, local)
    xb = field_b.reshape(plan.rows_b, plan.columns_b, local)
    ca = cotangent_a.reshape(plan.rows_a, plan.columns_a, local)
    cb = cotangent_b.reshape(plan.rows_b, plan.columns_b, local)
    gain1 = first_gain.astype(F32)[None]
    bias1 = first_bias.astype(F32)[None]
    gain2 = second_gain.astype(F32)[None]
    bias2 = second_norm_bias.astype(F32)[None]
    tables = [
        column_tables(plan.columns_a, plan.spread_a, width, 1, tokens),
        column_tables(plan.columns_b, plan.spread_b, width, 2, tokens),
    ]
    forward = np.stack([pair[0] for pair in tables])
    inverse = np.stack([pair[1] for pair in tables])
    depth = width * plan.piece
    fwd_w_t = jnp.asarray(forward.transpose(0, 2, 1).astype(jnp.bfloat16))
    inv_w_t = jnp.asarray(inverse.astype(jnp.bfloat16))
    inv_w = jnp.asarray(inverse.transpose(0, 2, 1).astype(jnp.bfloat16))
    fine = forward.astype(jnp.bfloat16)
    rest = (forward - fine.astype(np.float64)).astype(jnp.bfloat16)
    fwd_w = jnp.asarray(np.stack([fine, rest], axis=1))
    vector = pl.BlockSpec((1, local), lambda i: (0, 0))
    sums_spec = pl.BlockSpec((PAD, local), lambda i: (0, 0))
    sums_shape = jax.ShapeDtypeStruct((PAD, local), F32)
    scratch = plan.scratch()
    counts = jnp.stack(
        [offsets_a[myself + 1] - offsets_a[myself], offsets_b[myself + 1] - offsets_b[myself]]
    )
    count_spec = pl.BlockSpec(memory_space=pltpu.SMEM)

    def exchange(parts):
        return [lax.all_to_all(part, "wide", 0, 0, tiled=True) for part in parts]

    sends = call(
        functools.partial(first_kernel, plan),
        (plan.steps,),
        [plan.spec_a(), plan.spec_b(), vector, vector, plan.table((2, depth, tokens))],
        [plan.sends(), plan.sends()],
        [plan.exchange_shape()] * 2,
        [scratch],
    )(xa, xb, gain1, bias1, fwd_w)

    own = (expand_weight, expand_bias, reduce_weight)
    far = tuple(swap(part, "narrow", 2) for part in own)
    near = tuple(swap(part, "narrow", 1) for part in own)
    cross = tuple(swap(part, "narrow", 1) for part in far)
    chunks = (own, near, far, cross)
    expand = [chunk[0] for chunk in chunks]
    expand_b = jnp.stack([chunk[1] for chunk in chunks]).astype(F32)
    reduce = [chunk[2] for chunk in chunks]
    square = pl.BlockSpec(own[0].shape, lambda i: (0, 0), pipeline_mode=pl.Buffered(1))

    cot, cot_sums = call(
        functools.partial(cotangent_kernel, plan),
        (plan.steps,),
        [count_spec, plan.spec_a(), plan.spec_b()],
        [plan.rows(), sums_spec],
        [plan.rows_shape(BF16), sums_shape],
        [scratch],
    )(counts, ca, cb)
    block_shape = jax.ShapeDtypeStruct((2 * half, 2 * half), BF16)
    block_spec = pl.BlockSpec((2 * half, 2 * half), lambda: (0, 0))
    *ones, two0, two1 = call(
        functools.partial(weights_kernel, plan),
        (),
        [whole(inner_weight), whole(outer_weight)],
        [block_spec] * 4,
        [block_shape] * 4,
    )(inner_weight, outer_weight)
    twos = (two0, two1)

    table = []
    for offsets, height, rows, padded in (
        (offsets_a, H_A, plan.rows_a, plan.pad_a),
        (offsets_b, H_B, plan.rows_b, plan.pad_b),
    ):
        line, valid = row_slots(offsets, rows, width)
        table.append(jnp.stack(halves(row_table(height, line, valid, padded))))
    row_tables = (table[0], table[1], table[0][0].T, table[1][0].T)
    arrived = exchange([sends[0], hold(sends[1], *ones, cot, *row_tables, far[0], far[2])])
    shift1 = inner_bias.astype(F32).reshape(2, 2, half)
    shift2 = outer_bias.astype(F32).reshape(2, 2, half)
    points_shape = jax.ShapeDtypeStruct((plan.points, 2 * half), BF16)
    points_spec = pl.BlockSpec((plan.points, 2 * half), lambda: (0, 0))
    exchange_spec = pl.BlockSpec((width, units, plan.piece, half), lambda: (0, 0, 0, 0))
    parts_scratch = [
        pltpu.VMEM((half // LANES, width * plan.rows_a * plan.piece, LANES), F32),
        pltpu.VMEM((half // LANES, width * (units - plan.rows_a) * plan.piece, LANES), F32),
        pltpu.VMEM((plan.points, 2 * half), BF16),
    ]
    steps = 5 if plan.points % 80 == 0 else 1
    kept, outgoing = [], []
    ready = ((), (near[0], near[2], cross[0], cross[2], expand_b))
    for h in range(2):
        operands = (
            arrived[h],
            *row_tables,
            ones[h],
            shift1[:, h].reshape(1, 2 * half),
            twos[h],
            shift2[:, h].reshape(1, 2 * half),
        )
        got = call(
            functools.partial(spectral_kernel, plan, steps),
            (),
            [whole(item) for item in operands],
            [exchange_spec] + [points_spec] * 4 + [pl.BlockSpec((PAD, half), lambda: (0, 0))],
            [plan.exchange_shape()] + [points_shape] * 4 + [jax.ShapeDtypeStruct((PAD, half), F32)],
            parts_scratch,
            after=len(ready[h]),
        )(*operands, *ready[h])
        outgoing.append(got[0])
        kept.append(got[1:])
    returned = exchange(outgoing)
    grad_hidden = call(
        hidden_kernel,
        (plan.steps,),
        [plan.rows()] + [square] * 4,
        plan.chunks(),
        plan.chunks_shape(),
        after=1,
    )(cot, *reduce, returned[0])

    (
        middle, rows, hidden, grad_pre, dmid, send, norm2_sums, shift_sums
    ) = call(
        functools.partial(middle_kernel, plan),
        (plan.steps,),
        [plan.spec_a(), plan.spec_b(), plan.sends(), plan.sends()]
        + [vector] * 4
        + [plan.table((tokens, depth)), plan.table((depth, tokens))]
        + [square] * 4
        + [
            pl.BlockSpec(expand_b.shape, lambda i: (0, 0)),
            plan.chunks(),
            plan.rows(),
        ],
        [
            plan.rows(),
            plan.rows(),
            plan.chunks(),
            plan.chunks(),
            plan.rows(),
            plan.full_sends(),
            sums_spec,
            pl.BlockSpec((NARROW, PAD, local), lambda i: (0, 0, 0)),
        ],
        [
            plan.rows_shape(F32),
            plan.rows_shape(BF16),
            plan.chunks_shape(),
            plan.chunks_shape(),
            plan.rows_shape(F32),
            plan.full_shape(),
            sums_shape,
            jax.ShapeDtypeStruct((NARROW, PAD, local), F32),
        ],
        [scratch],
        limit=60,
    )(
        xa, xb, *returned, gain1, bias1, gain2, bias2, inv_w, inv_w_t, *expand, expand_b,
        grad_hidden, cot,
    )
    place = jnp.stack([myself, lax.axis_index("narrow")])
    row_link = ("wide", 1)
    axes = ("wide", "narrow")

    def over(value, link):
        return swap(value, *link)

    def at(link):
        return axes.index(link[0]), link[1]

    core_link, column_link = ("narrow", 1), ("narrow", 2)
    reduce_got = over(products(plan, hidden, cot, 1, True), core_link)
    expand_got = over(products(plan, grad_pre, rows, 1, False), core_link)
    reduce_keep, reduce_send = products(plan, hidden, cot, 0, True, reduce_got)
    expand_keep, expand_send = products(plan, grad_pre, rows, 0, False, expand_got)
    reduce_got = over(reduce_send, column_link)
    expand_got = over(expand_send, column_link)
    (arrived,) = exchange([send])

    mixed_a, mixed_b, norm1_sums = call(
        functools.partial(mixed_kernel, plan),
        (plan.steps,),
        [count_spec, plan.chunks()]
        + [square] * 4
        + [vector, plan.rows(), plan.rows(), plan.spec_a(), plan.spec_b()],
        [*plan.outs(), sums_spec],
        [
            jax.ShapeDtypeStruct(field_a.shape, BF16),
            jax.ShapeDtypeStruct(field_b.shape, BF16),
            sums_shape,
        ],
        [scratch],
        after=1,
    )(
        counts, hidden, *reduce, reduce_bias.astype(F32)[None], middle, dmid, xa, xb,
        reduce_send,
    )
    backs = []
    back_shape = jax.ShapeDtypeStruct((PAD, 2 * half), F32)
    weight_sums, pairs = ([], []), []
    over_points = (((0,), (0,)), ((), ()))
    for h in range(2):
        zed, act, slope1, slope2, _ = kept[h]
        operands = (*row_tables, ones[h], twos[h], slope1, slope2, zed)
        block = pl.BlockSpec((width, units, plan.piece, half), lambda i, h=h: (0, 0, 0, h))
        earlier = [mixed_a, expand_send] if h == 0 else [outgoing]
        outgoing, grad1, grad2, sums = pl.pallas_call(
            functools.partial(spectral_back_kernel, plan, steps, len(earlier)),
            grid=(1,),
            in_specs=[block]
            + [whole(item) for item in operands]
            + [pl.BlockSpec(memory_space=pl.ANY)] * len(earlier),
            out_specs=[block] + [whole(points_shape)] * 2 + [whole(back_shape)],
            out_shape=[plan.full_shape(), points_shape, points_shape, back_shape],
            input_output_aliases={1 + len(operands): 0} if h else {},
            scratch_shapes=parts_scratch,
            compiler_params=pltpu.CompilerParams(vmem_limit_bytes=60 * MIB),
        )(arrived, *operands, *earlier)
        backs.append(sums)
        pairs.append(((zed, grad1), (act, grad2)))
    for h in range(2):
        for index, (left, right) in enumerate(pairs[h]):
            if h == 0:
                right = hold(right, outgoing)
            weight_sums[index].append(
                lax.dot_general(left, right, over_points, preferred_element_type=F32)
            )
    reduce_sum_own, expand_sum_own = add_pairs(
        place, (reduce_keep, expand_keep), (reduce_got, expand_got), outgoing
    )
    reduce_sum, expand_sum = lax.psum((reduce_sum_own, expand_sum_own), "wide")

    flat = (
        *weight_sums[0],
        *weight_sums[1],
        *backs,
        kept[0][4],
        kept[1][4],
        norm2_sums,
        cot_sums,
        norm1_sums,
        shift_sums,
        gain1,
        bias1,
    )

    def pack_body(place, *refs):
        pack_kernel(
            plan, place, (refs[0:2], refs[2:4]), refs[4:6], refs[6:8], *refs[8:]
        )

    pack_links = (core_link, column_link, row_link)
    pack_rows = round_up(4 * BS + 13, 8 << (len(pack_links) + 1)) // 2
    pack_half = jax.ShapeDtypeStruct((pack_rows, local), F32)
    pack_keep, pack_send = call(
        pack_body,
        (),
        [count_spec] + [whole(item) for item in flat],
        [pl.BlockSpec((pack_rows, local), lambda: (0, 0))] * 2,
        [pack_half] * 2,
        [pltpu.VMEM((2 * pack_rows, local), F32)],
    )(place, *flat)
    for link in pack_links[1:]:
        before = pack_links[pack_links.index(link) - 1]
        pack_keep, pack_send = fold(place, at(link), pack_keep, over(pack_send, before))
    pack = total(place, (pack_keep, over(pack_send, pack_links[-1])))
    (returned,) = exchange([outgoing])
    pack = hold(pack, returned)
    layers = [over(pack, ("wide", 2 * k)) for k in range(1, width // 2)]

    grad_a, grad_b = call(
        functools.partial(last_kernel, plan),
        (plan.steps,),
        [plan.spec_a(), plan.spec_b(), plan.full_sends(), plan.rows(), vector]
        + [plan.table((tokens, depth))],
        plan.flat_outs(),
        [
            jax.ShapeDtypeStruct((plan.rows_a, plan.columns_a, 1, local), F32),
            jax.ShapeDtypeStruct((plan.rows_b, plan.columns_b, 1, local), F32),
        ],
        [scratch],
    )(xa, xb, returned, dmid, gain1, fwd_w_t)

    pack = total(place, [pack] + layers, grad_a, kind=BF16)
    for link in pack_links[:0:-1]:
        pack = join(place, at(link), pack, over(pack, link))
    inner_grad, outer_grad, small = last_join(place, at(core_link), pack, over(pack, core_link))
    own_row = lax.dynamic_slice_in_dim(small, 9 + place[1], 1)[0]
    return (
        mixed_a,
        mixed_b,
        grad_a.transpose(0, 2, 1, 3),
        grad_b.transpose(0, 2, 1, 3),
        small[7],
        small[8],
        inner_grad,
        small[0:2],
        outer_grad,
        small[2:4],
        small[4],
        small[5],
        expand_sum.astype(F32),
        own_row,
        reduce_sum.astype(F32),
        small[6],
    )


def choose(field_a, field_b, *rest):
    plan = Plan(
        lax.axis_size("wide"),
        field_a.shape[0],
        field_a.shape[2],
        field_b.shape[0],
        field_b.shape[2],
        field_a.shape[3],
    )
    alone = field_a.shape[1] == 1 and field_b.shape[1] == 1
    if plan.fits() and alone and lax.axis_size("narrow") == 4:
        return fast_device(plan, field_a, field_b, *rest)
    return general_device(field_a, field_b, *rest)


def solution(mesh):
    placed = (
        P("wide", "narrow", None, None),
        P("wide", "narrow", None, None),
        P("wide", "narrow", None, None),
        P("wide", "narrow", None, None),
        P(),
        P(),
        P(),
        P(),
        P(),
        P(),
        P(),
        P(),
        P(),
        P(),
        P(None, "narrow"),
        P("narrow"),
        P("narrow", None),
        P(),
    )
    return jax.shard_map(
        choose,
        mesh=mesh,
        in_specs=placed,
        out_specs=(
            P("wide", "narrow", None, None),
            P("wide", "narrow", None, None),
            P("wide", "narrow", None, None),
            P("wide", "narrow", None, None),
            P(),
            P(),
            P(),
            P(),
            P(),
            P(),
            P(),
            P(),
            P(None, "narrow"),
            P("narrow"),
            P("narrow", None),
            P(),
        ),
        check_vma=False,
    )
```

```python
import functools
import math

import jax
import jax.numpy as jnp
import numpy as np
from jax import lax
from jax.experimental import pallas as pl
from jax.experimental.pallas import tpu as pltpu
from jax.sharding import PartitionSpec as P

NBL = 8
BS = 96
H_A = 90
H_B = 45


EPSILON = 1e-05
SHRINK = 0.01
HIGH = lax.Precision.HIGHEST
ROOT_HALF = 0.7071067811865476
ROOT_TWO_PI = 2.5066282746310002


def gelu_value(value):
    return 0.5 * value * (1.0 + lax.erf(value * ROOT_HALF))


def gelu_slope(value):
    return (
        0.5 * (1.0 + lax.erf(value * ROOT_HALF))
        + value * jnp.exp(-0.5 * value * value) / ROOT_TWO_PI
    )


def shrink_value(value):
    return value - SHRINK * jnp.tanh(value / SHRINK)


def shrink_slope(value):
    bent = jnp.tanh(value / SHRINK)
    return bent * bent


def phase(left, right, length):
    turns = left * right % length
    return turns.astype(jnp.float32) * (2.0 * math.pi / length)


def row_slots(offsets, depth, width):
    offset = jnp.arange(depth, dtype=jnp.int32)
    begin = offsets[:width]
    counts = offsets[1:] - begin
    line = (begin[:, None] + offset[None, :]).reshape(-1)
    valid = (offset[None, :] < counts[:, None]).reshape(-1).astype(jnp.float32)
    return (line, valid)


def column_slots(freqs, spread, width):
    edges = jnp.arange(width + 1, dtype=jnp.int32) * freqs // width
    offset = jnp.arange(spread, dtype=jnp.int32)
    begin = edges[:width]
    valid = (offset[None, :] < (edges[1:] - begin)[:, None]).reshape(-1).astype(jnp.float32)
    return ((begin[:, None] + offset[None, :]).reshape(-1), valid)


def forward_w_table(columns, freq, valid, width, spread):
    angle = phase(jnp.arange(columns, dtype=jnp.int32)[:, None], freq[None, :], columns)
    scale = valid[None, :] / math.sqrt(columns)
    table = jnp.stack([jnp.cos(angle) * scale, -jnp.sin(angle) * scale], axis=1)
    return table.reshape(columns, 2, width, spread)


def inverse_w_table(columns, freq, valid, width, spread):
    angle = phase(freq[:, None], jnp.arange(columns, dtype=jnp.int32)[None, :], columns)
    edge = (freq == 0) | (2 * freq == columns)
    weight = jnp.where(edge, 1.0, 2.0) * valid / math.sqrt(columns)
    real = jnp.cos(angle) * weight[:, None]
    imag = jnp.where(edge[:, None], 0.0, -jnp.sin(angle)) * weight[:, None]
    return jnp.stack([real, imag], axis=1).reshape(width, spread, 2, columns)


def forward_h_table(height, line, valid):
    angle = phase(jnp.arange(height, dtype=jnp.int32)[:, None], line[None, :], height)
    scale = valid[None, :] / math.sqrt(height)
    cosine = jnp.cos(angle) * scale
    sine = jnp.sin(angle) * scale
    upper = jnp.stack([cosine, sine], axis=-1)
    lower = jnp.stack([-sine, cosine], axis=-1)
    return jnp.stack([upper, lower], axis=1)


def inverse_h_table(height, line, valid):
    angle = phase(line[:, None], jnp.arange(height, dtype=jnp.int32)[None, :], height)
    scale = valid[:, None] / math.sqrt(height)
    cosine = jnp.cos(angle) * scale
    sine = jnp.sin(angle) * scale
    upper = jnp.stack([cosine, -sine], axis=-1)
    lower = jnp.stack([sine, cosine], axis=-1)
    return jnp.stack([upper, lower], axis=1)


def complex_weight(weight):
    blocked = weight.reshape(2, BS, NBL, BS).transpose(0, 2, 1, 3)
    return jnp.stack([jnp.stack([blocked[0], blocked[1]]), jnp.stack([-blocked[1], blocked[0]])])


def fold_weight(grad):
    folded = jnp.stack([grad[0, 0] + grad[1, 1], grad[0, 1] - grad[1, 0]])
    return folded.transpose(0, 2, 1, 3).reshape(2, BS, NBL * BS)


def general_device(
    field_a,
    field_b,
    cotangent_a,
    cotangent_b,
    offsets_a,
    offsets_b,
    first_gain,
    first_bias,
    inner_weight,
    inner_bias,
    outer_weight,
    outer_bias,
    second_gain,
    second_norm_bias,
    expand_weight,
    expand_bias,
    reduce_weight,
    reduce_bias,
):
    width = lax.axis_size("wide")
    myself = lax.axis_index("wide")
    local = field_a.shape[-1]
    layouts = []
    for field, offsets, height in ((field_a, offsets_a, H_A), (field_b, offsets_b, H_B)):
        depth, snaps, columns = (field.shape[0], field.shape[1], field.shape[2])
        freqs = columns // 2 + 1
        spread = (freqs + width - 1) // width
        line, row_valid = row_slots(offsets, depth, width)
        freq, freq_valid = column_slots(freqs, spread, width)
        layouts.append(
            (
                depth,
                snaps,
                columns,
                spread,
                height,
                forward_w_table(columns, freq, freq_valid, width, spread),
                inverse_w_table(columns, freq, freq_valid, width, spread),
                forward_h_table(height, line, row_valid),
                inverse_h_table(height, line, row_valid),
                lax.dynamic_slice_in_dim(row_valid, myself * depth, depth),
            )
        )
    token_count = layouts[0][0] * layouts[0][1] * layouts[0][2]
    point_count = layouts[0][4] * layouts[0][1] * layouts[0][3]

    def to_grids(tokens):
        return [
            tokens[:token_count].reshape(
                layouts[0][0], layouts[0][1], layouts[0][2], tokens.shape[-1]
            ),
            tokens[token_count:].reshape(
                layouts[1][0], layouts[1][1], layouts[1][2], tokens.shape[-1]
            ),
        ]

    def to_tokens(parts):
        return jnp.concatenate([piece.reshape(-1, piece.shape[-1]) for piece in parts])

    def to_spectra(points):
        pieces = (points[:point_count], points[point_count:])
        return [
            pieces[index].reshape(layouts[index][4], layouts[index][1], layouts[index][3], 2, local)
            for index in range(2)
        ]

    def to_sends(parts):
        return [
            parts[index].reshape(
                width, layouts[index][0], layouts[index][1], layouts[index][3], 2, local
            )
            for index in range(2)
        ]

    mask = to_tokens(
        [
            jnp.broadcast_to(lay[9][:, None, None, None], (lay[0], lay[1], lay[2], 1))
            for lay in layouts
        ]
    )
    first_norm_gain = first_gain.astype(jnp.float32)
    first_norm_bias = first_bias.astype(jnp.float32)
    bias_out = reduce_bias.astype(jnp.float32)
    weight_one = complex_weight(inner_weight)
    weight_two = complex_weight(outer_weight)
    shift_one = inner_bias.astype(jnp.float32).reshape(2, NBL, BS)
    shift_two = outer_bias.astype(jnp.float32).reshape(2, NBL, BS)
    source = jnp.concatenate([field_a.reshape(-1, local), field_b.reshape(-1, local)]).astype(
        jnp.float32
    )
    mean_one = jnp.mean(source, axis=1, keepdims=True)
    first_centered_input = source - mean_one
    first_inverse_deviation = lax.rsqrt(
        jnp.mean(first_centered_input * first_centered_input, axis=1, keepdims=True) + EPSILON
    )
    first_standardized = first_centered_input * first_inverse_deviation
    normalized_rows = first_standardized * first_norm_gain + first_norm_bias
    normed_parts = to_grids(normalized_rows)
    sends = [
        jnp.einsum(
            "rswc,wtjk->jrsktc", normed_parts[index], layouts[index][5], precision=HIGH
        ).astype(jnp.bfloat16)
        for index in range(2)
    ]
    arrived = (
        lax.all_to_all(sends[0], "wide", split_axis=0, concat_axis=1, tiled=True),
        lax.all_to_all(sends[1], "wide", split_axis=0, concat_axis=1, tiled=True),
    )
    spectra = [
        jnp.einsum(
            "kumt,msqtc->ksquc",
            layouts[index][7],
            arrived[index][0].astype(jnp.float32),
            precision=HIGH,
        )
        for index in range(2)
    ]
    zed = jnp.concatenate([piece.reshape(-1, 2, NBL, BS) for piece in spectra]).astype(jnp.bfloat16)
    pre_one = (
        jnp.einsum("pcbi,cdbio->pdbo", zed, weight_one, preferred_element_type=jnp.float32)
        + shift_one
    )
    act_one = gelu_value(pre_one).astype(jnp.bfloat16)
    pre_two = (
        jnp.einsum("pcbi,cdbio->pdbo", act_one, weight_two, preferred_element_type=jnp.float32)
        + shift_two
    )
    shrunk = to_spectra(shrink_value(pre_two))
    outgoing = to_sends(
        [
            jnp.einsum(
                "mukt,ksqtc->msquc", layouts[index][8], shrunk[index], precision=HIGH
            ).astype(jnp.bfloat16)
            for index in range(2)
        ]
    )
    returned = (
        lax.all_to_all(outgoing[0], "wide", split_axis=0, concat_axis=1, tiled=True),
        lax.all_to_all(outgoing[1], "wide", split_axis=0, concat_axis=1, tiled=True),
    )
    field_parts = to_grids(source)
    middle_parts = []
    for index in range(2):
        lay = layouts[index]
        received = (
            returned[index][0].reshape(width, lay[0], lay[1], lay[3], 2, local).astype(jnp.float32)
        )
        middle_parts.append(
            jnp.einsum("jrsktc,jktw->rswc", received, lay[6], precision=HIGH)
            + normed_parts[index]
            + field_parts[index]
        )
    middle = to_tokens(middle_parts)
    mean_two = jnp.mean(middle, axis=1, keepdims=True)
    second_centered_input = middle - mean_two
    second_inverse_deviation = lax.rsqrt(
        jnp.mean(second_centered_input * second_centered_input, axis=1, keepdims=True) + EPSILON
    )
    second_standardized = second_centered_input * second_inverse_deviation
    second_norm_gain = second_gain.astype(jnp.float32)
    input_rows = (
        second_standardized * second_norm_gain + second_norm_bias.astype(jnp.float32)
    ).astype(jnp.bfloat16)
    full_inputs = lax.all_gather(input_rows, "narrow", axis=0, tiled=True)
    pre_three = jnp.dot(
        full_inputs, expand_weight, preferred_element_type=jnp.float32
    ) + expand_bias.astype(jnp.float32)
    act_three = gelu_value(pre_three).astype(jnp.bfloat16)
    partial_value = jnp.dot(act_three, reduce_weight, preferred_element_type=jnp.float32)
    mixed = (
        lax.psum_scatter(
            partial_value.astype(jnp.bfloat16), "narrow", scatter_dimension=0, tiled=True
        ).astype(jnp.float32)
        + bias_out
    )
    result = to_grids((middle + mixed) * mask)
    upstream = jnp.concatenate([cotangent_a.reshape(-1, local), cotangent_b.reshape(-1, local)])
    upstream = jnp.where(mask > 0.0, upstream, jnp.zeros_like(upstream))
    upstream_f = upstream.astype(jnp.float32)
    grad_out_b = jnp.sum(upstream_f, 0)
    full_upstream = lax.all_gather(upstream, "narrow", axis=0, tiled=True)
    grad_act = jnp.einsum(
        "td,fd->tf", full_upstream, reduce_weight, preferred_element_type=jnp.float32
    )
    grad_pre = (grad_act * gelu_slope(pre_three)).astype(jnp.bfloat16)
    grad_reduce = jnp.einsum(
        "tf,td->fd", act_three, full_upstream, preferred_element_type=jnp.float32
    )
    grad_expand = jnp.einsum("td,tf->df", full_inputs, grad_pre, preferred_element_type=jnp.float32)
    grad_expand_b = jnp.sum(grad_pre.astype(jnp.float32), 0)
    grad_terms = jnp.einsum(
        "tf,df->td", grad_pre, expand_weight, preferred_element_type=jnp.float32
    )
    input_gradient = lax.psum_scatter(
        grad_terms.astype(jnp.bfloat16), "narrow", scatter_dimension=0, tiled=True
    ).astype(jnp.float32)
    scaled_rows = input_gradient * second_norm_gain
    gradient_second_norm_gain = jnp.sum(input_gradient * second_standardized, 0)
    grad_bias_two = jnp.sum(input_gradient, 0)
    grad_full = second_inverse_deviation * (
        scaled_rows
        - jnp.mean(scaled_rows, axis=1, keepdims=True)
        - second_standardized * jnp.mean(scaled_rows * second_standardized, axis=1, keepdims=True)
    )
    grad_middle = grad_full + upstream_f
    grad_parts = to_grids(grad_middle)
    sends = [
        jnp.einsum(
            "rswc,jktw->jrsktc", grad_parts[index], layouts[index][6], precision=HIGH
        ).astype(jnp.bfloat16)
        for index in range(2)
    ]
    arrived = (
        lax.all_to_all(sends[0], "wide", split_axis=0, concat_axis=1, tiled=True),
        lax.all_to_all(sends[1], "wide", split_axis=0, concat_axis=1, tiled=True),
    )
    grad_points = jnp.concatenate(
        [
            jnp.einsum(
                "mukt,msquc->ksqtc",
                layouts[index][8],
                arrived[index][0].astype(jnp.float32),
                precision=HIGH,
            ).reshape(-1, 2, NBL, BS)
            for index in range(2)
        ]
    )
    grad_two = (grad_points * shrink_slope(pre_two)).astype(jnp.bfloat16)
    grad_hidden = jnp.einsum(
        "pdbo,cdbio->pcbi", grad_two, weight_two, preferred_element_type=jnp.float32
    )
    grad_weight_two = fold_weight(
        jnp.einsum("pcbi,pdbo->cdbio", act_one, grad_two, preferred_element_type=jnp.float32)
    )
    grad_shift_two = jnp.sum(grad_two.astype(jnp.float32), 0).reshape(2, -1)
    grad_one = (grad_hidden * gelu_slope(pre_one)).astype(jnp.bfloat16)
    grad_zed = jnp.einsum(
        "pdbo,cdbio->pcbi", grad_one, weight_one, preferred_element_type=jnp.float32
    )
    grad_weight_one = fold_weight(
        jnp.einsum("pcbi,pdbo->cdbio", zed, grad_one, preferred_element_type=jnp.float32)
    )
    grad_shift_one = jnp.sum(grad_one.astype(jnp.float32), 0).reshape(2, -1)
    grad_spectra = to_spectra(grad_zed)
    outgoing = to_sends(
        [
            jnp.einsum(
                "kumt,ksquc->msqtc", layouts[index][7], grad_spectra[index], precision=HIGH
            ).astype(jnp.bfloat16)
            for index in range(2)
        ]
    )
    returned = (
        lax.all_to_all(outgoing[0], "wide", split_axis=0, concat_axis=1, tiled=True),
        lax.all_to_all(outgoing[1], "wide", split_axis=0, concat_axis=1, tiled=True),
    )
    grad_normed_parts = []
    for index in range(2):
        lay = layouts[index]
        received = (
            returned[index][0].reshape(width, lay[0], lay[1], lay[3], 2, local).astype(jnp.float32)
        )
        grad_normed_parts.append(
            jnp.einsum("jrsktc,wtjk->rswc", received, lay[5], precision=HIGH) + grad_parts[index]
        )
    normalized_gradient = to_tokens(grad_normed_parts)
    scaled_rows = normalized_gradient * first_norm_gain
    grad_source = (
        first_inverse_deviation
        * (
            scaled_rows
            - jnp.mean(scaled_rows, axis=1, keepdims=True)
            - first_standardized * jnp.mean(scaled_rows * first_standardized, axis=1, keepdims=True)
        )
        + grad_middle
    )
    grad_fields = to_grids(grad_source * mask)
    gradient_first_norm_gain = jnp.sum(normalized_gradient * first_standardized, 0)
    grad_bias_one = jnp.sum(normalized_gradient, 0)
    mlp_sums = lax.psum((grad_expand, grad_expand_b, grad_reduce), "wide")
    shared = lax.psum(
        (
            grad_weight_one,
            grad_shift_one,
            grad_weight_two,
            grad_shift_two,
            gradient_first_norm_gain,
            grad_bias_one,
            gradient_second_norm_gain,
            grad_bias_two,
            grad_out_b,
        ),
        ("wide", "narrow"),
    )
    return (
        result[0].astype(jnp.bfloat16),
        result[1].astype(jnp.bfloat16),
        grad_fields[0],
        grad_fields[1],
        shared[4],
        shared[5],
        shared[0],
        shared[1],
        shared[2],
        shared[3],
        shared[6],
        shared[7],
        mlp_sums[0],
        mlp_sums[1],
        mlp_sums[2],
        shared[8],
    )


F32 = jnp.float32
BF16 = jnp.bfloat16
MIB = 1024 * 1024
PAD = 8
LANES = 128
CHUNK = 256
NARROW = 4


def halves(value):
    high = lax.reduce_precision(value, 8, 7)
    return high.astype(BF16), (value - high).astype(BF16)


def round_up(value, unit):
    return -(-value // unit) * unit


def call(kernel, grid, in_specs, out_specs, out_shape, scratch=(), limit=56, after=0):
    first = len(in_specs)

    def body(*refs):
        kernel(*refs[:first], *refs[first + after :])

    return pl.pallas_call(
        body,
        grid=grid,
        in_specs=in_specs + [pl.BlockSpec(memory_space=pl.ANY)] * after,
        out_specs=out_specs,
        out_shape=out_shape,
        scratch_shapes=list(scratch),
        compiler_params=pltpu.CompilerParams(vmem_limit_bytes=limit * MIB),
    )


def whole(array):
    zeros = (0,) * len(array.shape)
    return pl.BlockSpec(array.shape, lambda *_: zeros)


def dot(left, right):
    return jnp.dot(left, right, preferred_element_type=F32)


def dot_t(left, right):
    return lax.dot_general(left, right, (((1,), (1,)), ((), ())), preferred_element_type=F32)


def column_tables(columns, spread, width, repeat, tokens):
    freqs = columns // 2 + 1
    freq = np.arange(width * spread)
    valid = (freq < freqs).astype(np.float64)
    angle = 2.0 * np.pi * (np.outer(freq, np.arange(columns)) % columns) / columns
    scale = valid[:, None] / math.sqrt(columns)
    weight = np.where((freq == 0) | (2 * freq == columns), 1.0, 2.0)[:, None]
    parts = np.stack([np.cos(angle) * scale, -np.sin(angle) * scale], axis=1)
    parts = parts.reshape(width, spread, 2, columns).transpose(0, 2, 1, 3)
    heavy = np.broadcast_to(weight.reshape(width, 1, spread, 1), parts.shape)
    forward = np.zeros((width, repeat, 2, spread, tokens))
    inverse = np.zeros((width, repeat, 2, spread, tokens))
    for index in range(repeat):
        span = slice(index * columns, (index + 1) * columns)
        forward[:, index, :, :, span] = parts
        inverse[:, index, :, :, span] = parts * heavy
    return forward.reshape(-1, tokens), inverse.reshape(-1, tokens)


def row_table(height, line, valid, padded):
    angle = phase(jnp.arange(padded, dtype=jnp.int32)[:, None], line[None, :], height)
    inside = (jnp.arange(padded) < height).astype(F32)[:, None]
    scale = inside * valid[None, :] / math.sqrt(height)
    cosine = jnp.cos(angle) * scale
    sine = jnp.sin(angle) * scale
    upper = jnp.stack([cosine, sine], axis=-1)
    lower = jnp.stack([-sine, cosine], axis=-1)
    return jnp.stack([upper, lower]).reshape(2 * padded, -1)


def layer_norm(value):
    mean = jnp.mean(value, axis=1, keepdims=True)
    centred = value - mean
    scale = lax.rsqrt(jnp.mean(centred * centred, axis=1, keepdims=True) + EPSILON)
    return centred * scale, scale


def layer_norm_back(grad, gain, standard, scale):
    scaled = grad * gain
    return scale * (
        scaled
        - jnp.mean(scaled, axis=1, keepdims=True)
        - standard * jnp.mean(scaled * standard, axis=1, keepdims=True)
    )


def row_sums(*values):
    rows = [jnp.sum(value, axis=0, keepdims=True) for value in values]
    blank = jnp.zeros((PAD - len(rows), rows[0].shape[1]), F32)
    return jnp.concatenate(rows + [blank], axis=0)


class Plan:
    def __init__(self, width, rows_a, columns_a, rows_b, columns_b, local):
        self.width = width
        self.rows_a, self.columns_a = rows_a, columns_a
        self.rows_b, self.columns_b = rows_b, columns_b
        self.local = local
        self.half = local // 2
        self.spread_a = -(-(columns_a // 2 + 1) // width)
        self.spread_b = -(-(columns_b // 2 + 1) // width)
        self.piece = 2 * self.spread_a
        self.units = rows_a + rows_b // 2
        self.group = max(1, math.gcd(rows_a, rows_b // 2))
        self.steps_a = rows_a // self.group
        self.steps = self.units // self.group
        self.tokens = round_up(columns_a, 16)
        self.pad_a = round_up(H_A, 16)
        self.pad_b = round_up(H_B, 16)
        self.points_a = self.spread_a * self.pad_a
        self.points = self.points_a + self.spread_b * self.pad_b

    def fits(self):
        return (
            self.columns_a == 2 * self.columns_b
            and self.spread_a == 2 * self.spread_b
            and self.piece % 8 == 0
            and self.rows_b % 2 == 0
            and self.half % 128 == 0
            and self.half % BS == 0
        )

    def spec_a(self):
        last = self.steps_a - 1
        return pl.BlockSpec(
            (self.group, self.columns_a, self.local), lambda i: (jnp.minimum(i, last), 0, 0)
        )

    def spec_b(self):
        first = self.steps_a
        return pl.BlockSpec(
            (2 * self.group, self.columns_b, self.local),
            lambda i: (jnp.maximum(i - first, 0), 0, 0),
        )

    def rows(self):
        return pl.BlockSpec((self.group * self.tokens, self.local), lambda i: (i, 0))

    def chunks(self):
        return pl.BlockSpec((NARROW, self.group * self.tokens, self.local), lambda i: (0, i, 0))

    def sends(self):
        return pl.BlockSpec(
            (self.width, self.group, self.piece, self.half), lambda i: (0, i, 0, 0)
        )

    def table(self, shape):
        first = self.steps_a
        zeros = (0,) * len(shape)
        return pl.BlockSpec((1,) + shape, lambda i: ((i >= first).astype(jnp.int32),) + zeros)

    def exchange_shape(self):
        return jax.ShapeDtypeStruct((self.width, self.units, self.piece, self.half), BF16)

    def full_sends(self):
        return pl.BlockSpec(
            (self.width, self.group, self.piece, self.local), lambda i: (0, i, 0, 0)
        )

    def full_shape(self):
        return jax.ShapeDtypeStruct((self.width, self.units, self.piece, self.local), BF16)

    def rows_shape(self, kind):
        return jax.ShapeDtypeStruct((self.units * self.tokens, self.local), kind)

    def chunks_shape(self):
        return jax.ShapeDtypeStruct((NARROW, self.units * self.tokens, self.local), BF16)

    def scratch(self):
        return pltpu.VMEM((self.group * self.tokens, self.local), F32)

    def load(self, step, a_ref, b_ref, scratch):
        @pl.when(step == 0)
        def _():
            scratch[...] = jnp.zeros_like(scratch)

        @pl.when(step < self.steps_a)
        def _():
            for u in range(self.group):
                base = u * self.tokens
                scratch[base : base + self.columns_a] = a_ref[u].astype(F32)

        @pl.when(step >= self.steps_a)
        def _():
            for u in range(self.group):
                base = u * self.tokens
                middle = base + self.columns_b
                scratch[base:middle] = b_ref[2 * u].astype(F32)
                scratch[middle : base + self.columns_a] = b_ref[2 * u + 1].astype(F32)

        return scratch[...]

    def parts(self, value):
        return [value[u * self.tokens : (u + 1) * self.tokens] for u in range(self.group)]

    def outs(self):
        last, first = self.steps_a - 1, self.steps_a
        return [
            pl.BlockSpec(
                (self.group, 1, self.columns_a, self.local),
                lambda i: (jnp.minimum(i, last), 0, 0, 0),
            ),
            pl.BlockSpec(
                (2 * self.group, 1, self.columns_b, self.local),
                lambda i: (jnp.maximum(i - first, 0), 0, 0, 0),
            ),
        ]

    def flat_outs(self):
        last, first = self.steps_a - 1, self.steps_a
        return [
            pl.BlockSpec(
                (self.group, self.columns_a, 1, self.local),
                lambda i: (jnp.minimum(i, last), 0, 0, 0),
            ),
            pl.BlockSpec(
                (2 * self.group, self.columns_b, 1, self.local),
                lambda i: (jnp.maximum(i - first, 0), 0, 0, 0),
            ),
        ]

    def store(self, step, value, a_ref, b_ref):
        units = self.parts(value)

        @pl.when(step < self.steps_a)
        def _():
            for u in range(self.group):
                a_ref[u, 0] = units[u][: self.columns_a].astype(a_ref.dtype)

        @pl.when(step >= self.steps_a)
        def _():
            for u in range(self.group):
                b_ref[2 * u, 0] = units[u][: self.columns_b].astype(b_ref.dtype)
                b_ref[2 * u + 1, 0] = units[u][self.columns_b : self.columns_a].astype(b_ref.dtype)

    def store_flat(self, step, value, a_ref, b_ref):
        units = self.parts(value)

        @pl.when(step < self.steps_a)
        def _():
            for u in range(self.group):
                a_ref[u, :, 0, :] = units[u][: self.columns_a]

        @pl.when(step >= self.steps_a)
        def _():
            for u in range(self.group):
                b_ref[2 * u, :, 0, :] = units[u][: self.columns_b]
                b_ref[2 * u + 1, :, 0, :] = units[u][self.columns_b : self.columns_a]

    def put_sends(self, product, unit, refs):
        size = self.local // len(refs)
        for index, ref in enumerate(refs):
            lanes = product[:, index * size : (index + 1) * size]
            ref[:, unit] = lanes.reshape(self.width, self.piece, size).astype(BF16)

    def from_sends(self, table, refs):
        depth = self.width * self.piece
        units = []
        for u in range(self.group):
            size = self.local // len(refs)
            parts = [ref[:, u].astype(F32).reshape(depth, size).astype(BF16) for ref in refs]
            units.append(jnp.concatenate([dot(table, part) for part in parts], axis=1))
        return jnp.concatenate(units, axis=0)

    def valid_rows(self, step, counts, shape):
        row = lax.broadcasted_iota(jnp.int32, shape, 0)
        inside = row >= 0
        used = row < 0
        for u in range(self.group):
            token = row - u * self.tokens
            here = (token >= 0) & (token < self.columns_a)
            in_a = (step < self.steps_a) & (step * self.group + u < counts[0])
            pair = 2 * ((step - self.steps_a) * self.group + u)
            in_b0 = (step >= self.steps_a) & (pair < counts[1])
            in_b1 = (step >= self.steps_a) & (pair + 1 < counts[1])
            first = (in_a | in_b0).astype(jnp.int32)
            second = (in_a | in_b1).astype(jnp.int32)
            flag = jnp.where(token < self.columns_b, first, second)
            used = used | (here & (flag > 0))
        return used


def first_kernel(plan, xa, xb, gain, bias, table, out0, out1, scratch):
    step = pl.program_id(0)
    standard, _ = layer_norm(plan.load(step, xa, xb, scratch))
    scale, shift = (ref[...].astype(F32).reshape(1, plan.local) for ref in (gain, bias))
    for u, part in enumerate(plan.parts(standard * scale + shift)):
        high, low = halves(part)
        spectrum = dot(table[0, 0], high) + (dot(table[0, 0], low) + dot(table[0, 1], high))
        plan.put_sends(spectrum, u, (out0, out1))


def cotangent_kernel(plan, counts, ca, cb, out, sums, scratch):
    step = pl.program_id(0)
    value = plan.load(step, ca, cb, scratch)
    value = jnp.where(plan.valid_rows(step, counts, value.shape), value, 0.0)
    out[...] = value.astype(BF16)

    @pl.when(step == 0)
    def _():
        sums[...] = jnp.zeros_like(sums)

    sums[...] += row_sums(value)


def gelu_both(value):
    bell = jnp.exp(-0.5 * value * value)
    cdf = 0.5 * (1.0 + lax.erf(value * ROOT_HALF))
    return value * cdf, cdf + value * bell * (1.0 / ROOT_TWO_PI)


def hidden_kernel(cot, w0, w1, w2, w3, out):
    for k, weight in enumerate((w0, w1, w2, w3)):
        out[k] = dot_t(cot[...], weight[...]).astype(BF16)


def middle_kernel(
    plan, xa, xb, got0, got1, gain, bias, gain2, bias2, inv, inv_t, w0, w1, w2, w3, shift, back,
    cot, mid, rows, hidden, grad_pre, dmid, out, sums, shift_sums, scratch,
):
    step = pl.program_id(0)

    @pl.when(step == 0)
    def _():
        sums[...] = jnp.zeros_like(sums)
        shift_sums[...] = jnp.zeros_like(shift_sums)

    value = plan.load(step, xa, xb, scratch)
    standard, _ = layer_norm(value)
    middle = value + standard * gain[...] + bias[...]
    middle += plan.from_sends(inv[0], (got0, got1))
    mid[...] = middle
    standard, scale = layer_norm(middle)
    flat = (standard * gain2[...] + bias2[...]).astype(BF16)
    rows[...] = flat
    weights = (w0, w1, w2, w3)
    grad = None
    for k, weight in enumerate(weights):
        for start in range(0, plan.local, CHUNK):
            lanes = slice(start, start + CHUNK)
            act, slope = gelu_both(dot(flat, weight[:, lanes]) + shift[k : k + 1, lanes])
            hidden[k, :, lanes] = act.astype(BF16)
            pre = back[k, :, lanes].astype(F32) * slope
            grad_pre[k, :, lanes] = pre.astype(BF16)
            shift_sums[k, :1, lanes] += jnp.sum(pre, axis=0, keepdims=True)
        part = dot_t(grad_pre[k], weight[...])
        grad = part if grad is None else grad + part
    sums[...] += row_sums(grad * standard, grad)
    result = cot[...].astype(F32) + layer_norm_back(grad, gain2[...], standard, scale)
    dmid[...] = result
    for u, part in enumerate(plan.parts(result)):
        plan.put_sends(dot(inv_t[0], part.astype(BF16)), u, (out,))


def mixed_kernel(
    plan, counts, hidden, w0, w1, w2, w3, bias, mid, dmid, xa, xb, outa, outb, sums, scratch
):
    step = pl.program_id(0)
    standard, _ = layer_norm(plan.load(step, xa, xb, scratch))
    grad = dmid[...]

    @pl.when(step == 0)
    def _():
        sums[...] = jnp.zeros_like(sums)

    sums[...] += row_sums(grad * standard, grad)
    value = mid[...] + bias[...]
    for k, weight in enumerate((w0, w1, w2, w3)):
        value += dot(hidden[k], weight[...])
    value = jnp.where(plan.valid_rows(step, counts, value.shape), value, 0.0)
    plan.store(step, value, outa, outb)


def products(plan, chunked, plain, first, chunk_left, got=None):
    count, local = plain.shape
    square = (1, local, local)
    chunk = pl.BlockSpec((1, count, local), lambda i: (2 * i + first, 0, 0))
    flat = pl.BlockSpec((count, local), lambda i: (0, 0))
    each = pl.BlockSpec(square, lambda i: (i, 0, 0))
    whole_out = pl.BlockSpec((local, local), lambda i: (0, 0))
    one = jax.ShapeDtypeStruct((local, local), BF16)

    def kernel(chunk_ref, plain_ref, *refs):
        pair = (chunk_ref[0], plain_ref[...])
        value = lax.dot_general(
            *(pair if chunk_left else pair[::-1]),
            (((0,), (0,)), ((), ())),
            preferred_element_type=F32,
        )
        if got is None:
            refs[0][0] = value.astype(BF16)
            return
        value += refs[0][0].astype(F32)
        for k in range(2):

            @pl.when(pl.program_id(0) == k)
            def _(k=k):
                refs[1 + k][...] = value.astype(BF16)

    if got is None:
        return call(
            kernel, (2,), [chunk, flat], each, jax.ShapeDtypeStruct((2, local, local), BF16)
        )(chunked, plain)
    return call(kernel, (2,), [chunk, flat, each], [whole_out] * 2, [one] * 2)(
        chunked, plain, got
    )


def last_kernel(plan, xa, xb, got, dmid, gain, table, outa, outb, scratch):
    step = pl.program_id(0)
    standard, scale = layer_norm(plan.load(step, xa, xb, scratch))
    passed = dmid[...]
    grad = plan.from_sends(table[0], (got,)) + passed
    total = passed + layer_norm_back(grad, gain[...], standard, scale)
    plan.store_flat(step, total, outa, outb)


def weights_kernel(plan, inner, outer, inner0, inner1, outer0, outer1):
    half = plan.half
    for weight, outs in ((inner, (inner0, inner1)), (outer, (outer0, outer1))):
        parts = [weight[k].astype(F32) for k in range(2)]
        for h, out in enumerate(outs):
            out[...] = jnp.zeros_like(out)
            for b in range(half // BS):
                lanes = slice(h * half + b * BS, h * half + (b + 1) * BS)
                near = slice(b * BS, (b + 1) * BS)
                late = slice(half + b * BS, half + (b + 1) * BS)
                real, imag = parts[0][:, lanes].astype(BF16), parts[1][:, lanes].astype(BF16)
                out[near, near] = real
                out[late, late] = real
                out[near, late] = imag
                out[late, near] = -imag


def nothing(*refs):
    return None


def hold(value, *before):
    anywhere = pl.BlockSpec(memory_space=pl.ANY)
    return pl.pallas_call(
        nothing,
        in_specs=[anywhere] * (1 + len(before)),
        out_specs=anywhere,
        out_shape=jax.ShapeDtypeStruct(value.shape, value.dtype),
        input_output_aliases={0: 0},
    )(value, *before)


def bit_of(place, link):
    return (place[link[0]] // link[1]) % 2


def fold_kernel(link, place, left, right, keep, send):
    total = left[...].astype(F32) + right[...].astype(F32)
    size = keep.shape[-2]
    near, far = total[..., :size, :], total[..., size:, :]
    bit = bit_of(place, link)

    @pl.when(bit == 0)
    def _():
        keep[...] = near.astype(keep.dtype)
        send[...] = far.astype(send.dtype)

    @pl.when(bit == 1)
    def _():
        keep[...] = far.astype(keep.dtype)
        send[...] = near.astype(send.dtype)


SMEM = pl.BlockSpec(memory_space=pltpu.SMEM)


def flat_call(kernel, place, operands, shapes, before=()):
    def spec(item):
        zeros = (0,) * len(item.shape)
        return pl.BlockSpec(item.shape, lambda: zeros)

    return call(
        kernel,
        (),
        [SMEM] + [spec(item) for item in operands],
        [spec(item) for item in shapes],
        list(shapes),
        after=len(before),
    )(place, *operands, *before)


def fold(place, link, left, right, *before):
    shape = left.shape[:-2] + (left.shape[-2] // 2, left.shape[-1])
    half = jax.ShapeDtypeStruct(shape, left.dtype)
    return flat_call(
        functools.partial(fold_kernel, link), place, (left, right), (half, half), before
    )


def both_fold(place, link, lefts, rights, *before):
    rows, local = lefts[0].shape
    half = jax.ShapeDtypeStruct((2, rows // 2, local), lefts[0].dtype)

    def kernel(place, left0, left1, right0, right1, keep, send):
        for k, (left, right) in enumerate(((left0, right0), (left1, right1))):
            fold_kernel(link, place, left, right, keep.at[k], send.at[k])

    return flat_call(kernel, place, (*lefts, *rights), (half, half), before)


def corners(place, links, pieces, *before):
    _, size, local = pieces[0].shape
    shape = jax.ShapeDtypeStruct((4 * size, local), F32)

    def kernel(place, *refs):
        outer, inner = (bit_of(place, link) for link in links)
        for k, piece in enumerate(refs[:4]):
            start = 2 * (outer ^ (k % 2)) + (inner ^ (k // 2))
            rows = pl.ds(pl.multiple_of(start * size, size), size)
            for j, out in enumerate(refs[4:]):
                out[rows, :] = piece[j].astype(F32)

    return flat_call(kernel, place, pieces, (shape, shape), before)


def total(place, parts, *before, kind=None):
    def kernel(_, *refs):
        values = [ref[...].astype(F32) for ref in refs[:-1]]
        while len(values) > 1:
            values = [a + b for a, b in zip(values[::2], values[1::2], strict=True)]
        refs[-1][...] = values[0].astype(refs[-1].dtype)

    return flat_call(
        kernel, place, parts, [jax.ShapeDtypeStruct(parts[0].shape, kind or parts[0].dtype)], before
    )[0]


def join(place, link, mine, other, *before, kind=None):
    size = mine.shape[-2]
    shape = mine.shape[:-2] + (2 * size, mine.shape[-1])

    def kernel(place, mine, other, out):
        bit = bit_of(place, link)

        def put(low, high):
            out[..., :size, :] = low[...].astype(out.dtype)
            out[..., size:, :] = high[...].astype(out.dtype)

        @pl.when(bit == 0)
        def _():
            put(mine, other)

        @pl.when(bit == 1)
        def _():
            put(other, mine)

    return flat_call(
        kernel, place, (mine, other), [jax.ShapeDtypeStruct(shape, kind or mine.dtype)], before
    )[0]


def last_join(place, link, mine, other, *before):
    size, local = mine.shape

    def kernel(place, mine, other, inner, outer, small, whole_pack):
        bit = bit_of(place, link)
        whole_pack[pl.ds(pl.multiple_of(bit * size, size), size), :] = mine[...].astype(F32)
        whole_pack[pl.ds(pl.multiple_of((1 - bit) * size, size), size), :] = other[...].astype(F32)
        for k in range(2):
            inner[k] = whole_pack[k * BS : (k + 1) * BS]
            outer[k] = whole_pack[(2 + k) * BS : (3 + k) * BS]
        small[...] = whole_pack[4 * BS : 4 * BS + small.shape[0]]

    def spec(item):
        zeros = (0,) * len(item.shape)
        return pl.BlockSpec(item.shape, lambda: zeros)

    matrix = jax.ShapeDtypeStruct((2, BS, local), F32)
    shapes = [matrix, matrix, jax.ShapeDtypeStruct((16, local), F32)]
    return call(
        kernel,
        (),
        [SMEM, spec(mine), spec(other)],
        [spec(item) for item in shapes],
        shapes,
        [pltpu.VMEM((2 * size, local), F32)],
        after=len(before),
    )(place, mine, other, *before)


def unpack(plan, got, part_a, part_b):
    rows_a = plan.rows_a * plan.piece
    rows_b = (plan.units - plan.rows_a) * plan.piece
    for j in range(plan.width):
        value = got[j].astype(F32)
        for part, rows, piece in (
            (part_a, rows_a, value[: plan.rows_a]),
            (part_b, rows_b, value[plan.rows_a :]),
        ):
            for g in range(plan.half // LANES):
                lanes = piece[:, :, g * LANES : (g + 1) * LANES]
                part[g, j * rows : (j + 1) * rows] = lanes.reshape(rows, LANES)


def repack(plan, part_a, part_b, out):
    rows_a = plan.rows_a * plan.piece
    rows_b = (plan.units - plan.rows_a) * plan.piece
    for j in range(plan.width):
        for part, rows, first, last in (
            (part_a, rows_a, 0, plan.rows_a),
            (part_b, rows_b, plan.rows_a, plan.units),
        ):
            for g in range(plan.half // LANES):
                out[j, first:last, :, g * LANES : (g + 1) * LANES] = (
                    part[g, j * rows : (j + 1) * rows]
                    .reshape(last - first, plan.piece, LANES)
                    .astype(BF16)
                )


def grids(plan):
    return (
        (plan.spread_a, plan.pad_a, plan.width * 2 * plan.rows_a, 0, 0),
        (plan.spread_b, plan.pad_b, plan.width * 2 * plan.rows_b, plan.points_a, 1),
    )


def to_points(plan, parts, tables, out, first=None):
    for spread, pad, depth, base, which in grids(plan):
        for f in range(spread):
            lanes = [
                parts[which][g, pl.ds(f, depth, stride=spread), :].astype(BF16)
                for g in range(plan.half // LANES)
            ]
            column = jnp.concatenate(lanes, axis=1)
            product = dot(tables[which][0], column)
            if first is not None:
                product += dot(tables[which][1], column)
                if f == 0:
                    first[which : which + 1] = product[:1]
            out[base + f * pad : base + (f + 1) * pad, :] = jnp.concatenate(
                [product[:pad], product[pad:]], axis=1
            ).astype(out.dtype)


def from_points(plan, points, tables, parts):
    for spread, pad, depth, base, which in grids(plan):
        for f in range(spread):
            value = points[base + f * pad : base + (f + 1) * pad, :]
            column = jnp.concatenate([value[:, : plan.half], value[:, plan.half :]], axis=0)
            product = dot(tables[which][...], column)
            for g in range(plan.half // LANES):
                parts[which][g, pl.ds(f, depth, stride=spread), :] = product[
                    :, g * LANES : (g + 1) * LANES
                ]


def spectral_kernel(
    plan, steps, got, ta, tb, tat, tbt, w1, b1, w2, b2, out, zed, act, slope1, slope2, dc, pa, pb, shrunk
):
    unpack(plan, got, pa, pb)
    dc[...] = jnp.zeros_like(dc)
    to_points(plan, (pa, pb), (ta, tb), zed, dc)
    size = plan.points // steps

    def body(index, carry):
        rows = pl.ds(pl.multiple_of(index * size, size), size)
        pre_one = dot(zed[rows, :], w1[...]) + b1[...]
        cdf = 0.5 * (1.0 + lax.erf(pre_one * ROOT_HALF))
        hidden = (pre_one * cdf).astype(BF16)
        act[rows, :] = hidden
        slope1[rows, :] = (
            cdf + pre_one * jnp.exp(-0.5 * pre_one * pre_one) * (1.0 / ROOT_TWO_PI)
        ).astype(BF16)
        pre_two = dot(hidden, w2[...]) + b2[...]
        bent = jnp.tanh(pre_two * (1.0 / SHRINK))
        shrunk[rows, :] = (pre_two - SHRINK * bent).astype(BF16)
        slope2[rows, :] = (bent * bent).astype(BF16)
        return carry

    lax.fori_loop(0, steps, body, 0)
    from_points(plan, shrunk, (tat, tbt), (pa, pb))
    repack(plan, pa, pb, out)


def spectral_back_kernel(
    plan, steps, skip, got, ta, tb, tat, tbt, w1, w2, slope1, slope2, zed, *refs
):
    out, grad1, grad2, sums, pa, pb, work = refs[skip:]
    unpack(plan, got, pa, pb)
    to_points(plan, (pa, pb), (ta, tb), work)
    size = plan.points // steps
    sums[...] = jnp.zeros_like(sums)

    def body(index, carry):
        rows = pl.ds(pl.multiple_of(index * size, size), size)
        two = (work[rows, :].astype(F32) * slope2[rows, :].astype(F32)).astype(BF16)
        grad2[rows, :] = two
        one = (dot_t(two, w2[...]) * slope1[rows, :].astype(F32)).astype(BF16)
        grad1[rows, :] = one
        grad = dot_t(one, w1[...])
        work[rows, :] = grad.astype(BF16)
        sums[...] += row_sums(one.astype(F32), two.astype(F32), grad * zed[rows, :].astype(F32))
        return carry

    lax.fori_loop(0, steps, body, 0)
    for which, start in enumerate((0, plan.points_a)):
        sums[3 + which : 4 + which] = work[start : start + 16, :].astype(F32)[:1]
        sums[5 + which : 6 + which] = zed[start : start + 16, :].astype(F32)[:1]
    from_points(plan, work, (tat, tbt), (pa, pb))
    repack(plan, pa, pb, out)


def pack_kernel(
    plan, place, products, backs, dcs, norm2, cot, norm1, shift, gain, bias, keep, send, out
):
    half, blocks = plan.half, plan.half // BS
    out[...] = jnp.zeros_like(out)
    for kind in range(2):
        for h in range(2):
            product = products[kind][h]
            for b in range(blocks):
                rows = slice(b * BS, (b + 1) * BS)
                late = slice(half + b * BS, half + (b + 1) * BS)
                real = product[rows, rows] + product[late, late]
                imag = product[rows, late] - product[late, rows]
                lanes = slice(h * half + b * BS, h * half + (b + 1) * BS)
                out[2 * kind * BS : (2 * kind + 1) * BS, lanes] = real
                out[(2 * kind + 1) * BS : (2 * kind + 2) * BS, lanes] = imag
    row = 4 * BS
    for kind in range(2):
        for part in range(2):
            for h in range(2):
                out[row : row + 1, h * half : (h + 1) * half] = backs[h][
                    kind : kind + 1, part * half : (part + 1) * half
                ]
            row += 1
    out[row : row + 2] = norm2[0:2]
    out[row + 2 : row + 3] = cot[0:1]
    row += 3
    first = jnp.where(place[0] == 0, 1.0, 0.0)
    roots = [math.sqrt(H_A * plan.columns_a), math.sqrt(H_B * plan.columns_b)]
    for h in range(2):
        lanes = slice(h * half, (h + 1) * half)
        total = backs[h][2:3, :half] + backs[h][2:3, half:]
        plain = norm1[1:2, lanes]
        for which in range(2):
            grad = backs[h][3 + which : 4 + which, :half] * first
            exact = dcs[h][which : which + 1] - bias[:, lanes] * roots[which]
            total += grad * (exact - backs[h][5 + which : 6 + which, :half])
            plain += grad * roots[which]
        out[row : row + 1, lanes] = norm1[0:1, lanes] + total / gain[:, lanes]
        out[row + 1 : row + 2, lanes] = plain
    row += 2
    for n in range(4):
        out[row + n : row + n + 1] = shift[n ^ place[1], :1]
    size = keep.shape[0]
    mine = pl.multiple_of((place[1] % 2) * size, size)
    keep[...] = out[pl.ds(mine, size), :]
    send[...] = out[pl.ds(size - mine, size), :]


def swap(value, axis, distance):
    size = lax.axis_size(axis)
    return lax.ppermute(value, axis, [(i, i ^ distance) for i in range(size)])


def fast_device(
    plan,
    field_a,
    field_b,
    cotangent_a,
    cotangent_b,
    offsets_a,
    offsets_b,
    first_gain,
    first_bias,
    inner_weight,
    inner_bias,
    outer_weight,
    outer_bias,
    second_gain,
    second_norm_bias,
    expand_weight,
    expand_bias,
    reduce_weight,
    reduce_bias,
):
    width, local, half = plan.width, plan.local, plan.half
    tokens, units = plan.tokens, plan.units
    myself = lax.axis_index("wide")
    xa = field_a.reshape(plan.rows_a, plan.columns_a, local)
    xb = field_b.reshape(plan.rows_b, plan.columns_b, local)
    ca = cotangent_a.reshape(plan.rows_a, plan.columns_a, local)
    cb = cotangent_b.reshape(plan.rows_b, plan.columns_b, local)
    gain1 = first_gain.astype(F32)[None]
    bias1 = first_bias.astype(F32)[None]
    gain2 = second_gain.astype(F32)[None]
    bias2 = second_norm_bias.astype(F32)[None]
    tables = [
        column_tables(plan.columns_a, plan.spread_a, width, 1, tokens),
        column_tables(plan.columns_b, plan.spread_b, width, 2, tokens),
    ]
    forward = np.stack([pair[0] for pair in tables])
    inverse = np.stack([pair[1] for pair in tables])
    depth = width * plan.piece
    fwd_w_t = jnp.asarray(forward.transpose(0, 2, 1).astype(jnp.bfloat16))
    inv_w_t = jnp.asarray(inverse.astype(jnp.bfloat16))
    inv_w = jnp.asarray(inverse.transpose(0, 2, 1).astype(jnp.bfloat16))
    fine = forward.astype(jnp.bfloat16)
    rest = (forward - fine.astype(np.float64)).astype(jnp.bfloat16)
    fwd_w = jnp.asarray(np.stack([fine, rest], axis=1))
    vector = pl.BlockSpec((1, local), lambda i: (0, 0))
    plain = pl.BlockSpec((local,), lambda i: (0,))
    sums_spec = pl.BlockSpec((PAD, local), lambda i: (0, 0))
    sums_shape = jax.ShapeDtypeStruct((PAD, local), F32)
    scratch = plan.scratch()
    counts = jnp.stack(
        [offsets_a[myself + 1] - offsets_a[myself], offsets_b[myself + 1] - offsets_b[myself]]
    )
    count_spec = pl.BlockSpec(memory_space=pltpu.SMEM)

    def exchange(parts):
        return [lax.all_to_all(part, "wide", 0, 0, tiled=True) for part in parts]

    sends = call(
        functools.partial(first_kernel, plan),
        (plan.steps,),
        [plan.spec_a(), plan.spec_b(), plain, plain, plan.table((2, depth, tokens))],
        [plan.sends(), plan.sends()],
        [plan.exchange_shape()] * 2,
        [scratch],
    )(xa, xb, first_gain, first_bias, fwd_w)

    own = (expand_weight, expand_bias, reduce_weight)
    far = tuple(swap(part, "narrow", 2) for part in own)
    near = tuple(swap(part, "narrow", 1) for part in own)
    cross = tuple(swap(part, "narrow", 1) for part in far)
    chunks = (own, near, far, cross)
    expand = [chunk[0] for chunk in chunks]
    expand_b = jnp.stack([chunk[1] for chunk in chunks]).astype(F32)
    reduce = [chunk[2] for chunk in chunks]
    square = pl.BlockSpec(own[0].shape, lambda i: (0, 0), pipeline_mode=pl.Buffered(1))

    cot, cot_sums = call(
        functools.partial(cotangent_kernel, plan),
        (plan.steps,),
        [count_spec, plan.spec_a(), plan.spec_b()],
        [plan.rows(), sums_spec],
        [plan.rows_shape(BF16), sums_shape],
        [scratch],
    )(counts, ca, cb)
    block_shape = jax.ShapeDtypeStruct((2 * half, 2 * half), BF16)
    block_spec = pl.BlockSpec((2 * half, 2 * half), lambda: (0, 0))
    *ones, two0, two1 = call(
        functools.partial(weights_kernel, plan),
        (),
        [whole(inner_weight), whole(outer_weight)],
        [block_spec] * 4,
        [block_shape] * 4,
    )(inner_weight, outer_weight)
    twos = (two0, two1)

    table = []
    for offsets, height, rows, padded in (
        (offsets_a, H_A, plan.rows_a, plan.pad_a),
        (offsets_b, H_B, plan.rows_b, plan.pad_b),
    ):
        line, valid = row_slots(offsets, rows, width)
        table.append(jnp.stack(halves(row_table(height, line, valid, padded))))
    row_tables = (table[0], table[1], table[0][0].T, table[1][0].T)
    arrived = exchange([sends[0], hold(sends[1], *ones, cot, *row_tables, far[0], far[2])])
    shift1 = inner_bias.astype(F32).reshape(2, 2, half)
    shift2 = outer_bias.astype(F32).reshape(2, 2, half)
    points_shape = jax.ShapeDtypeStruct((plan.points, 2 * half), BF16)
    points_spec = pl.BlockSpec((plan.points, 2 * half), lambda: (0, 0))
    exchange_spec = pl.BlockSpec((width, units, plan.piece, half), lambda: (0, 0, 0, 0))
    parts_scratch = [
        pltpu.VMEM((half // LANES, width * plan.rows_a * plan.piece, LANES), F32),
        pltpu.VMEM((half // LANES, width * (units - plan.rows_a) * plan.piece, LANES), F32),
        pltpu.VMEM((plan.points, 2 * half), BF16),
    ]
    steps = 5 if plan.points % 80 == 0 else 1
    kept, outgoing = [], []
    ready = ((), (near[0], near[2], cross[0], cross[2], expand_b))
    for h in range(2):
        operands = (
            arrived[h],
            *row_tables,
            ones[h],
            shift1[:, h].reshape(1, 2 * half),
            twos[h],
            shift2[:, h].reshape(1, 2 * half),
        )
        got = call(
            functools.partial(spectral_kernel, plan, steps),
            (),
            [whole(item) for item in operands],
            [exchange_spec] + [points_spec] * 4 + [pl.BlockSpec((PAD, half), lambda: (0, 0))],
            [plan.exchange_shape()] + [points_shape] * 4 + [jax.ShapeDtypeStruct((PAD, half), F32)],
            parts_scratch,
            after=len(ready[h]),
        )(*operands, *ready[h])
        outgoing.append(got[0])
        kept.append(got[1:])
    returned = exchange(outgoing)
    grad_hidden = call(
        hidden_kernel,
        (plan.steps,),
        [plan.rows()] + [square] * 4,
        plan.chunks(),
        plan.chunks_shape(),
        after=1,
    )(cot, *reduce, returned[0])

    (
        middle, rows, hidden, grad_pre, dmid, send, norm2_sums, shift_sums
    ) = call(
        functools.partial(middle_kernel, plan),
        (plan.steps,),
        [plan.spec_a(), plan.spec_b(), plan.sends(), plan.sends()]
        + [vector] * 4
        + [plan.table((tokens, depth)), plan.table((depth, tokens))]
        + [square] * 4
        + [
            pl.BlockSpec(expand_b.shape, lambda i: (0, 0)),
            plan.chunks(),
            plan.rows(),
        ],
        [
            plan.rows(),
            plan.rows(),
            plan.chunks(),
            plan.chunks(),
            plan.rows(),
            plan.full_sends(),
            sums_spec,
            pl.BlockSpec((NARROW, PAD, local), lambda i: (0, 0, 0)),
        ],
        [
            plan.rows_shape(F32),
            plan.rows_shape(BF16),
            plan.chunks_shape(),
            plan.chunks_shape(),
            plan.rows_shape(F32),
            plan.full_shape(),
            sums_shape,
            jax.ShapeDtypeStruct((NARROW, PAD, local), F32),
        ],
        [scratch],
        limit=60,
    )(
        xa, xb, *returned, gain1, bias1, gain2, bias2, inv_w, inv_w_t, *expand, expand_b,
        grad_hidden, cot,
    )
    place = jnp.stack([myself, lax.axis_index("narrow")])
    row_link, low_link, high_link = ("wide", 1), ("wide", 2), ("wide", 4)
    axes = ("wide", "narrow")

    def over(value, link):
        return swap(value, *link)

    def at(link):
        return axes.index(link[0]), link[1]

    core_link, column_link = ("narrow", 1), ("narrow", 2)
    reduce_got = over(products(plan, hidden, cot, 1, True), core_link)
    expand_got = over(products(plan, grad_pre, rows, 1, False), core_link)
    reduce_keep, reduce_send = products(plan, hidden, cot, 0, True, reduce_got)
    expand_keep, expand_send = products(plan, grad_pre, rows, 0, False, expand_got)
    reduce_got = over(reduce_send, column_link)
    expand_got = over(expand_send, column_link)
    (arrived,) = exchange([send])

    mixed_a, mixed_b, norm1_sums = call(
        functools.partial(mixed_kernel, plan),
        (plan.steps,),
        [count_spec, plan.chunks()]
        + [square] * 4
        + [vector, plan.rows(), plan.rows(), plan.spec_a(), plan.spec_b()],
        [*plan.outs(), sums_spec],
        [
            jax.ShapeDtypeStruct(field_a.shape, BF16),
            jax.ShapeDtypeStruct(field_b.shape, BF16),
            sums_shape,
        ],
        [scratch],
        after=1,
    )(
        counts, hidden, *reduce, reduce_bias.astype(F32)[None], middle, dmid, xa, xb,
        reduce_send,
    )
    keep, send = both_fold(
        place,
        at(row_link),
        (reduce_keep, expand_keep),
        (reduce_got, expand_got),
        mixed_a,
    )
    row_got = over(send, row_link)

    backs = []
    back_shape = jax.ShapeDtypeStruct((PAD, 2 * half), F32)
    weight_sums, pairs = ([], []), []
    over_points = (((0,), (0,)), ((), ()))
    for h in range(2):
        zed, act, slope1, slope2, _ = kept[h]
        operands = (*row_tables, ones[h], twos[h], slope1, slope2, zed)
        block = pl.BlockSpec((width, units, plan.piece, half), lambda i, h=h: (0, 0, 0, h))
        earlier = [keep] if h == 0 else [outgoing]
        outgoing, grad1, grad2, sums = pl.pallas_call(
            functools.partial(spectral_back_kernel, plan, steps, len(earlier)),
            grid=(1,),
            in_specs=[block]
            + [whole(item) for item in operands]
            + [pl.BlockSpec(memory_space=pl.ANY)] * len(earlier),
            out_specs=[block] + [whole(points_shape)] * 2 + [whole(back_shape)],
            out_shape=[plan.full_shape(), points_shape, points_shape, back_shape],
            input_output_aliases={1 + len(operands): 0} if h else {},
            scratch_shapes=parts_scratch,
            compiler_params=pltpu.CompilerParams(vmem_limit_bytes=60 * MIB),
        )(arrived, *operands, *earlier)
        backs.append(sums)
        pairs.append(((zed, grad1), (act, grad2)))
    for h in range(2):
        for index, (left, right) in enumerate(pairs[h]):
            if h == 0:
                right = hold(right, sums)
            weight_sums[index].append(
                lax.dot_general(left, right, over_points, preferred_element_type=F32)
            )
    keep, send = fold(place, at(low_link), keep, row_got, sums)
    outgoing = hold(outgoing, send)
    flat = (
        *weight_sums[0],
        *weight_sums[1],
        *backs,
        kept[0][4],
        kept[1][4],
        norm2_sums,
        cot_sums,
        norm1_sums,
        shift_sums,
        gain1,
        bias1,
    )

    def pack_body(place, *refs):
        pack_kernel(
            plan, place, (refs[0:2], refs[2:4]), refs[4:6], refs[6:8], *refs[8:]
        )

    pack_links = (core_link, column_link, row_link)
    pack_rows = round_up(4 * BS + 13, 8 << (len(pack_links) + 1)) // 2
    pack_half = jax.ShapeDtypeStruct((pack_rows, local), F32)
    pack_keep, pack_send = call(
        pack_body,
        (),
        [count_spec] + [whole(item) for item in flat],
        [pl.BlockSpec((pack_rows, local), lambda: (0, 0))] * 2,
        [pack_half] * 2,
        [pltpu.VMEM((2 * pack_rows, local), F32)],
    )(place, *flat)
    pack_keep, pack_send = fold(place, at(column_link), pack_keep, over(pack_send, core_link))
    pack_keep, pack_send = fold(place, at(row_link), pack_keep, over(pack_send, column_link))
    keep, send = fold(place, at(high_link), keep, over(send, low_link), pack_send)
    shared = total(place, (keep, over(send, high_link)))
    high_got = over(shared, high_link)

    pack = total(place, (pack_keep, over(pack_send, pack_links[-1])))
    (returned,) = exchange([outgoing])
    layers = [over(pack, ("wide", 2 * k)) for k in range(1, width // 2)]

    grad_a, grad_b = call(
        functools.partial(last_kernel, plan),
        (plan.steps,),
        [plan.spec_a(), plan.spec_b(), plan.full_sends(), plan.rows(), vector]
        + [plan.table((tokens, depth))],
        plan.flat_outs(),
        [
            jax.ShapeDtypeStruct((plan.rows_a, plan.columns_a, 1, local), F32),
            jax.ShapeDtypeStruct((plan.rows_b, plan.columns_b, 1, local), F32),
        ],
        [scratch],
        after=2,
    )(xa, xb, returned, dmid, gain1, fwd_w_t, pack, shared)

    shared = join(place, at(high_link), shared, high_got, grad_a)
    low_got = over(shared, low_link)
    row_got = over(shared, row_link)
    reduce_sum, expand_sum = corners(
        place,
        (at(row_link), at(low_link)),
        (shared, row_got, low_got, over(low_got, row_link)),
    )
    pack = total(place, [pack] + layers, grad_a, kind=BF16)
    pack = join(place, at(row_link), pack, over(pack, row_link), row_got)
    pack = join(place, at(column_link), pack, over(pack, column_link), low_got)
    inner_grad, outer_grad, small = last_join(
        place, at(core_link), pack, over(pack, core_link), reduce_sum
    )
    own_row = lax.dynamic_slice_in_dim(small, 9 + place[1], 1)[0]
    return (
        mixed_a,
        mixed_b,
        grad_a.transpose(0, 2, 1, 3),
        grad_b.transpose(0, 2, 1, 3),
        small[7],
        small[8],
        inner_grad,
        small[0:2],
        outer_grad,
        small[2:4],
        small[4],
        small[5],
        expand_sum,
        own_row,
        reduce_sum,
        small[6],
    )


def choose(field_a, field_b, *rest):
    plan = Plan(
        lax.axis_size("wide"),
        field_a.shape[0],
        field_a.shape[2],
        field_b.shape[0],
        field_b.shape[2],
        field_a.shape[3],
    )
    alone = field_a.shape[1] == 1 and field_b.shape[1] == 1
    if plan.fits() and alone and lax.axis_size("narrow") == 4:
        return fast_device(plan, field_a, field_b, *rest)
    return general_device(field_a, field_b, *rest)


def solution(mesh):
    placed = (
        P("wide", "narrow", None, None),
        P("wide", "narrow", None, None),
        P("wide", "narrow", None, None),
        P("wide", "narrow", None, None),
        P(),
        P(),
        P(),
        P(),
        P(),
        P(),
        P(),
        P(),
        P(),
        P(),
        P(None, "narrow"),
        P("narrow"),
        P("narrow", None),
        P(),
    )
    return jax.shard_map(
        choose,
        mesh=mesh,
        in_specs=placed,
        out_specs=(
            P("wide", "narrow", None, None),
            P("wide", "narrow", None, None),
            P("wide", "narrow", None, None),
            P("wide", "narrow", None, None),
            P(),
            P(),
            P(),
            P(),
            P(),
            P(),
            P(),
            P(),
            P(None, "narrow"),
            P("narrow"),
            P("narrow", None),
            P(),
        ),
        check_vma=False,
    )
```

```python
import functools
import math

import jax
import jax.numpy as jnp
import numpy as np
from jax import lax
from jax.experimental import pallas as pl
from jax.experimental.pallas import tpu as pltpu
from jax.sharding import PartitionSpec as P

NBL = 8
BS = 96
H_A = 90
H_B = 45


EPSILON = 1e-05
SHRINK = 0.01
HIGH = lax.Precision.HIGHEST
ROOT_HALF = 0.7071067811865476
ROOT_TWO_PI = 2.5066282746310002


def gelu_value(value):
    return 0.5 * value * (1.0 + lax.erf(value * ROOT_HALF))


def gelu_slope(value):
    return (
        0.5 * (1.0 + lax.erf(value * ROOT_HALF))
        + value * jnp.exp(-0.5 * value * value) / ROOT_TWO_PI
    )


def shrink_value(value):
    return value - SHRINK * jnp.tanh(value / SHRINK)


def shrink_slope(value):
    bent = jnp.tanh(value / SHRINK)
    return bent * bent


def phase(left, right, length):
    turns = left * right % length
    return turns.astype(jnp.float32) * (2.0 * math.pi / length)


def row_slots(offsets, depth, width):
    offset = jnp.arange(depth, dtype=jnp.int32)
    begin = offsets[:width]
    counts = offsets[1:] - begin
    line = (begin[:, None] + offset[None, :]).reshape(-1)
    valid = (offset[None, :] < counts[:, None]).reshape(-1).astype(jnp.float32)
    return (line, valid)


def column_slots(freqs, spread, width):
    edges = jnp.arange(width + 1, dtype=jnp.int32) * freqs // width
    offset = jnp.arange(spread, dtype=jnp.int32)
    begin = edges[:width]
    valid = (offset[None, :] < (edges[1:] - begin)[:, None]).reshape(-1).astype(jnp.float32)
    return ((begin[:, None] + offset[None, :]).reshape(-1), valid)


def forward_w_table(columns, freq, valid, width, spread):
    angle = phase(jnp.arange(columns, dtype=jnp.int32)[:, None], freq[None, :], columns)
    scale = valid[None, :] / math.sqrt(columns)
    table = jnp.stack([jnp.cos(angle) * scale, -jnp.sin(angle) * scale], axis=1)
    return table.reshape(columns, 2, width, spread)


def inverse_w_table(columns, freq, valid, width, spread):
    angle = phase(freq[:, None], jnp.arange(columns, dtype=jnp.int32)[None, :], columns)
    edge = (freq == 0) | (2 * freq == columns)
    weight = jnp.where(edge, 1.0, 2.0) * valid / math.sqrt(columns)
    real = jnp.cos(angle) * weight[:, None]
    imag = jnp.where(edge[:, None], 0.0, -jnp.sin(angle)) * weight[:, None]
    return jnp.stack([real, imag], axis=1).reshape(width, spread, 2, columns)


def forward_h_table(height, line, valid):
    angle = phase(jnp.arange(height, dtype=jnp.int32)[:, None], line[None, :], height)
    scale = valid[None, :] / math.sqrt(height)
    cosine = jnp.cos(angle) * scale
    sine = jnp.sin(angle) * scale
    upper = jnp.stack([cosine, sine], axis=-1)
    lower = jnp.stack([-sine, cosine], axis=-1)
    return jnp.stack([upper, lower], axis=1)


def inverse_h_table(height, line, valid):
    angle = phase(line[:, None], jnp.arange(height, dtype=jnp.int32)[None, :], height)
    scale = valid[:, None] / math.sqrt(height)
    cosine = jnp.cos(angle) * scale
    sine = jnp.sin(angle) * scale
    upper = jnp.stack([cosine, -sine], axis=-1)
    lower = jnp.stack([sine, cosine], axis=-1)
    return jnp.stack([upper, lower], axis=1)


def complex_weight(weight):
    blocked = weight.reshape(2, BS, NBL, BS).transpose(0, 2, 1, 3)
    return jnp.stack([jnp.stack([blocked[0], blocked[1]]), jnp.stack([-blocked[1], blocked[0]])])


def fold_weight(grad):
    folded = jnp.stack([grad[0, 0] + grad[1, 1], grad[0, 1] - grad[1, 0]])
    return folded.transpose(0, 2, 1, 3).reshape(2, BS, NBL * BS)


def general_device(
    field_a,
    field_b,
    cotangent_a,
    cotangent_b,
    offsets_a,
    offsets_b,
    first_gain,
    first_bias,
    inner_weight,
    inner_bias,
    outer_weight,
    outer_bias,
    second_gain,
    second_norm_bias,
    expand_weight,
    expand_bias,
    reduce_weight,
    reduce_bias,
):
    width = lax.axis_size("wide")
    myself = lax.axis_index("wide")
    local = field_a.shape[-1]
    layouts = []
    for field, offsets, height in ((field_a, offsets_a, H_A), (field_b, offsets_b, H_B)):
        depth, snaps, columns = (field.shape[0], field.shape[1], field.shape[2])
        freqs = columns // 2 + 1
        spread = (freqs + width - 1) // width
        line, row_valid = row_slots(offsets, depth, width)
        freq, freq_valid = column_slots(freqs, spread, width)
        layouts.append(
            (
                depth,
                snaps,
                columns,
                spread,
                height,
                forward_w_table(columns, freq, freq_valid, width, spread),
                inverse_w_table(columns, freq, freq_valid, width, spread),
                forward_h_table(height, line, row_valid),
                inverse_h_table(height, line, row_valid),
                lax.dynamic_slice_in_dim(row_valid, myself * depth, depth),
            )
        )
    token_count = layouts[0][0] * layouts[0][1] * layouts[0][2]
    point_count = layouts[0][4] * layouts[0][1] * layouts[0][3]

    def to_grids(tokens):
        return [
            tokens[:token_count].reshape(
                layouts[0][0], layouts[0][1], layouts[0][2], tokens.shape[-1]
            ),
            tokens[token_count:].reshape(
                layouts[1][0], layouts[1][1], layouts[1][2], tokens.shape[-1]
            ),
        ]

    def to_tokens(parts):
        return jnp.concatenate([piece.reshape(-1, piece.shape[-1]) for piece in parts])

    def to_spectra(points):
        pieces = (points[:point_count], points[point_count:])
        return [
            pieces[index].reshape(layouts[index][4], layouts[index][1], layouts[index][3], 2, local)
            for index in range(2)
        ]

    def to_sends(parts):
        return [
            parts[index].reshape(
                width, layouts[index][0], layouts[index][1], layouts[index][3], 2, local
            )
            for index in range(2)
        ]

    mask = to_tokens(
        [
            jnp.broadcast_to(lay[9][:, None, None, None], (lay[0], lay[1], lay[2], 1))
            for lay in layouts
        ]
    )
    first_norm_gain = first_gain.astype(jnp.float32)
    first_norm_bias = first_bias.astype(jnp.float32)
    bias_out = reduce_bias.astype(jnp.float32)
    weight_one = complex_weight(inner_weight)
    weight_two = complex_weight(outer_weight)
    shift_one = inner_bias.astype(jnp.float32).reshape(2, NBL, BS)
    shift_two = outer_bias.astype(jnp.float32).reshape(2, NBL, BS)
    source = jnp.concatenate([field_a.reshape(-1, local), field_b.reshape(-1, local)]).astype(
        jnp.float32
    )
    mean_one = jnp.mean(source, axis=1, keepdims=True)
    first_centered_input = source - mean_one
    first_inverse_deviation = lax.rsqrt(
        jnp.mean(first_centered_input * first_centered_input, axis=1, keepdims=True) + EPSILON
    )
    first_standardized = first_centered_input * first_inverse_deviation
    normalized_rows = first_standardized * first_norm_gain + first_norm_bias
    normed_parts = to_grids(normalized_rows)
    sends = [
        jnp.einsum(
            "rswc,wtjk->jrsktc", normed_parts[index], layouts[index][5], precision=HIGH
        ).astype(jnp.bfloat16)
        for index in range(2)
    ]
    arrived = (
        lax.all_to_all(sends[0], "wide", split_axis=0, concat_axis=1, tiled=True),
        lax.all_to_all(sends[1], "wide", split_axis=0, concat_axis=1, tiled=True),
    )
    spectra = [
        jnp.einsum(
            "kumt,msqtc->ksquc",
            layouts[index][7],
            arrived[index][0].astype(jnp.float32),
            precision=HIGH,
        )
        for index in range(2)
    ]
    zed = jnp.concatenate([piece.reshape(-1, 2, NBL, BS) for piece in spectra]).astype(jnp.bfloat16)
    pre_one = (
        jnp.einsum("pcbi,cdbio->pdbo", zed, weight_one, preferred_element_type=jnp.float32)
        + shift_one
    )
    act_one = gelu_value(pre_one).astype(jnp.bfloat16)
    pre_two = (
        jnp.einsum("pcbi,cdbio->pdbo", act_one, weight_two, preferred_element_type=jnp.float32)
        + shift_two
    )
    shrunk = to_spectra(shrink_value(pre_two))
    outgoing = to_sends(
        [
            jnp.einsum(
                "mukt,ksqtc->msquc", layouts[index][8], shrunk[index], precision=HIGH
            ).astype(jnp.bfloat16)
            for index in range(2)
        ]
    )
    returned = (
        lax.all_to_all(outgoing[0], "wide", split_axis=0, concat_axis=1, tiled=True),
        lax.all_to_all(outgoing[1], "wide", split_axis=0, concat_axis=1, tiled=True),
    )
    field_parts = to_grids(source)
    middle_parts = []
    for index in range(2):
        lay = layouts[index]
        received = (
            returned[index][0].reshape(width, lay[0], lay[1], lay[3], 2, local).astype(jnp.float32)
        )
        middle_parts.append(
            jnp.einsum("jrsktc,jktw->rswc", received, lay[6], precision=HIGH)
            + normed_parts[index]
            + field_parts[index]
        )
    middle = to_tokens(middle_parts)
    mean_two = jnp.mean(middle, axis=1, keepdims=True)
    second_centered_input = middle - mean_two
    second_inverse_deviation = lax.rsqrt(
        jnp.mean(second_centered_input * second_centered_input, axis=1, keepdims=True) + EPSILON
    )
    second_standardized = second_centered_input * second_inverse_deviation
    second_norm_gain = second_gain.astype(jnp.float32)
    input_rows = (
        second_standardized * second_norm_gain + second_norm_bias.astype(jnp.float32)
    ).astype(jnp.bfloat16)
    full_inputs = lax.all_gather(input_rows, "narrow", axis=0, tiled=True)
    pre_three = jnp.dot(
        full_inputs, expand_weight, preferred_element_type=jnp.float32
    ) + expand_bias.astype(jnp.float32)
    act_three = gelu_value(pre_three).astype(jnp.bfloat16)
    partial_value = jnp.dot(act_three, reduce_weight, preferred_element_type=jnp.float32)
    mixed = (
        lax.psum_scatter(
            partial_value.astype(jnp.bfloat16), "narrow", scatter_dimension=0, tiled=True
        ).astype(jnp.float32)
        + bias_out
    )
    result = to_grids((middle + mixed) * mask)
    upstream = jnp.concatenate([cotangent_a.reshape(-1, local), cotangent_b.reshape(-1, local)])
    upstream = jnp.where(mask > 0.0, upstream, jnp.zeros_like(upstream))
    upstream_f = upstream.astype(jnp.float32)
    grad_out_b = jnp.sum(upstream_f, 0)
    full_upstream = lax.all_gather(upstream, "narrow", axis=0, tiled=True)
    grad_act = jnp.einsum(
        "td,fd->tf", full_upstream, reduce_weight, preferred_element_type=jnp.float32
    )
    grad_pre = (grad_act * gelu_slope(pre_three)).astype(jnp.bfloat16)
    grad_reduce = jnp.einsum(
        "tf,td->fd", act_three, full_upstream, preferred_element_type=jnp.float32
    )
    grad_expand = jnp.einsum("td,tf->df", full_inputs, grad_pre, preferred_element_type=jnp.float32)
    grad_expand_b = jnp.sum(grad_pre.astype(jnp.float32), 0)
    grad_terms = jnp.einsum(
        "tf,df->td", grad_pre, expand_weight, preferred_element_type=jnp.float32
    )
    input_gradient = lax.psum_scatter(
        grad_terms.astype(jnp.bfloat16), "narrow", scatter_dimension=0, tiled=True
    ).astype(jnp.float32)
    scaled_rows = input_gradient * second_norm_gain
    gradient_second_norm_gain = jnp.sum(input_gradient * second_standardized, 0)
    grad_bias_two = jnp.sum(input_gradient, 0)
    grad_full = second_inverse_deviation * (
        scaled_rows
        - jnp.mean(scaled_rows, axis=1, keepdims=True)
        - second_standardized * jnp.mean(scaled_rows * second_standardized, axis=1, keepdims=True)
    )
    grad_middle = grad_full + upstream_f
    grad_parts = to_grids(grad_middle)
    sends = [
        jnp.einsum(
            "rswc,jktw->jrsktc", grad_parts[index], layouts[index][6], precision=HIGH
        ).astype(jnp.bfloat16)
        for index in range(2)
    ]
    arrived = (
        lax.all_to_all(sends[0], "wide", split_axis=0, concat_axis=1, tiled=True),
        lax.all_to_all(sends[1], "wide", split_axis=0, concat_axis=1, tiled=True),
    )
    grad_points = jnp.concatenate(
        [
            jnp.einsum(
                "mukt,msquc->ksqtc",
                layouts[index][8],
                arrived[index][0].astype(jnp.float32),
                precision=HIGH,
            ).reshape(-1, 2, NBL, BS)
            for index in range(2)
        ]
    )
    grad_two = (grad_points * shrink_slope(pre_two)).astype(jnp.bfloat16)
    grad_hidden = jnp.einsum(
        "pdbo,cdbio->pcbi", grad_two, weight_two, preferred_element_type=jnp.float32
    )
    grad_weight_two = fold_weight(
        jnp.einsum("pcbi,pdbo->cdbio", act_one, grad_two, preferred_element_type=jnp.float32)
    )
    grad_shift_two = jnp.sum(grad_two.astype(jnp.float32), 0).reshape(2, -1)
    grad_one = (grad_hidden * gelu_slope(pre_one)).astype(jnp.bfloat16)
    grad_zed = jnp.einsum(
        "pdbo,cdbio->pcbi", grad_one, weight_one, preferred_element_type=jnp.float32
    )
    grad_weight_one = fold_weight(
        jnp.einsum("pcbi,pdbo->cdbio", zed, grad_one, preferred_element_type=jnp.float32)
    )
    grad_shift_one = jnp.sum(grad_one.astype(jnp.float32), 0).reshape(2, -1)
    grad_spectra = to_spectra(grad_zed)
    outgoing = to_sends(
        [
            jnp.einsum(
                "kumt,ksquc->msqtc", layouts[index][7], grad_spectra[index], precision=HIGH
            ).astype(jnp.bfloat16)
            for index in range(2)
        ]
    )
    returned = (
        lax.all_to_all(outgoing[0], "wide", split_axis=0, concat_axis=1, tiled=True),
        lax.all_to_all(outgoing[1], "wide", split_axis=0, concat_axis=1, tiled=True),
    )
    grad_normed_parts = []
    for index in range(2):
        lay = layouts[index]
        received = (
            returned[index][0].reshape(width, lay[0], lay[1], lay[3], 2, local).astype(jnp.float32)
        )
        grad_normed_parts.append(
            jnp.einsum("jrsktc,wtjk->rswc", received, lay[5], precision=HIGH) + grad_parts[index]
        )
    normalized_gradient = to_tokens(grad_normed_parts)
    scaled_rows = normalized_gradient * first_norm_gain
    grad_source = (
        first_inverse_deviation
        * (
            scaled_rows
            - jnp.mean(scaled_rows, axis=1, keepdims=True)
            - first_standardized * jnp.mean(scaled_rows * first_standardized, axis=1, keepdims=True)
        )
        + grad_middle
    )
    grad_fields = to_grids(grad_source * mask)
    gradient_first_norm_gain = jnp.sum(normalized_gradient * first_standardized, 0)
    grad_bias_one = jnp.sum(normalized_gradient, 0)
    mlp_sums = lax.psum((grad_expand, grad_expand_b, grad_reduce), "wide")
    shared = lax.psum(
        (
            grad_weight_one,
            grad_shift_one,
            grad_weight_two,
            grad_shift_two,
            gradient_first_norm_gain,
            grad_bias_one,
            gradient_second_norm_gain,
            grad_bias_two,
            grad_out_b,
        ),
        ("wide", "narrow"),
    )
    return (
        result[0].astype(jnp.bfloat16),
        result[1].astype(jnp.bfloat16),
        grad_fields[0],
        grad_fields[1],
        shared[4],
        shared[5],
        shared[0],
        shared[1],
        shared[2],
        shared[3],
        shared[6],
        shared[7],
        mlp_sums[0],
        mlp_sums[1],
        mlp_sums[2],
        shared[8],
    )


F32 = jnp.float32
BF16 = jnp.bfloat16
MIB = 1024 * 1024
PAD = 8
LANES = 128
CHUNK = 256
NARROW = 4


def halves(value):
    high = lax.reduce_precision(value, 8, 7)
    return high.astype(BF16), (value - high).astype(BF16)


def round_up(value, unit):
    return -(-value // unit) * unit


def call(kernel, grid, in_specs, out_specs, out_shape, scratch=(), limit=56, after=0):
    first = len(in_specs)

    def body(*refs):
        kernel(*refs[:first], *refs[first + after :])

    return pl.pallas_call(
        body,
        grid=grid,
        in_specs=in_specs + [pl.BlockSpec(memory_space=pl.ANY)] * after,
        out_specs=out_specs,
        out_shape=out_shape,
        scratch_shapes=list(scratch),
        compiler_params=pltpu.CompilerParams(vmem_limit_bytes=limit * MIB),
    )


def whole(array):
    zeros = (0,) * len(array.shape)
    return pl.BlockSpec(array.shape, lambda *_: zeros)


def dot(left, right):
    return jnp.dot(left, right, preferred_element_type=F32)


def dot_t(left, right):
    return lax.dot_general(left, right, (((1,), (1,)), ((), ())), preferred_element_type=F32)


def column_tables(columns, spread, width, repeat, tokens):
    freqs = columns // 2 + 1
    freq = np.arange(width * spread)
    valid = (freq < freqs).astype(np.float64)
    angle = 2.0 * np.pi * (np.outer(freq, np.arange(columns)) % columns) / columns
    scale = valid[:, None] / math.sqrt(columns)
    weight = np.where((freq == 0) | (2 * freq == columns), 1.0, 2.0)[:, None]
    parts = np.stack([np.cos(angle) * scale, -np.sin(angle) * scale], axis=1)
    parts = parts.reshape(width, spread, 2, columns).transpose(0, 2, 1, 3)
    heavy = np.broadcast_to(weight.reshape(width, 1, spread, 1), parts.shape)
    forward = np.zeros((width, repeat, 2, spread, tokens))
    inverse = np.zeros((width, repeat, 2, spread, tokens))
    for index in range(repeat):
        span = slice(index * columns, (index + 1) * columns)
        forward[:, index, :, :, span] = parts
        inverse[:, index, :, :, span] = parts * heavy
    return forward.reshape(-1, tokens), inverse.reshape(-1, tokens)


def row_table(height, line, valid, padded):
    angle = phase(jnp.arange(padded, dtype=jnp.int32)[:, None], line[None, :], height)
    inside = (jnp.arange(padded) < height).astype(F32)[:, None]
    scale = inside * valid[None, :] / math.sqrt(height)
    cosine = jnp.cos(angle) * scale
    sine = jnp.sin(angle) * scale
    upper = jnp.stack([cosine, sine], axis=-1)
    lower = jnp.stack([-sine, cosine], axis=-1)
    return jnp.stack([upper, lower]).reshape(2 * padded, -1)


def layer_norm(value):
    mean = jnp.mean(value, axis=1, keepdims=True)
    centred = value - mean
    scale = lax.rsqrt(jnp.mean(centred * centred, axis=1, keepdims=True) + EPSILON)
    return centred * scale, scale


def layer_norm_back(grad, gain, standard, scale):
    scaled = grad * gain
    return scale * (
        scaled
        - jnp.mean(scaled, axis=1, keepdims=True)
        - standard * jnp.mean(scaled * standard, axis=1, keepdims=True)
    )


def row_sums(*values):
    rows = [jnp.sum(value, axis=0, keepdims=True) for value in values]
    blank = jnp.zeros((PAD - len(rows), rows[0].shape[1]), F32)
    return jnp.concatenate(rows + [blank], axis=0)


class Plan:
    def __init__(self, width, rows_a, columns_a, rows_b, columns_b, local):
        self.width = width
        self.rows_a, self.columns_a = rows_a, columns_a
        self.rows_b, self.columns_b = rows_b, columns_b
        self.local = local
        self.half = local // 2
        self.spread_a = -(-(columns_a // 2 + 1) // width)
        self.spread_b = -(-(columns_b // 2 + 1) // width)
        self.piece = 2 * self.spread_a
        self.units = rows_a + rows_b // 2
        self.group = max(1, math.gcd(rows_a, rows_b // 2))
        self.steps_a = rows_a // self.group
        self.steps = self.units // self.group
        self.tokens = round_up(columns_a, 16)
        self.pad_a = round_up(H_A, 16)
        self.pad_b = round_up(H_B, 16)
        self.points_a = self.spread_a * self.pad_a
        self.points = self.points_a + self.spread_b * self.pad_b

    def fits(self):
        return (
            self.columns_a == 2 * self.columns_b
            and self.spread_a == 2 * self.spread_b
            and self.piece % 8 == 0
            and self.rows_b % 2 == 0
            and self.half % 128 == 0
            and self.half % BS == 0
        )

    def spec_a(self):
        last = self.steps_a - 1
        return pl.BlockSpec(
            (self.group, self.columns_a, self.local), lambda i: (jnp.minimum(i, last), 0, 0)
        )

    def spec_b(self):
        first = self.steps_a
        return pl.BlockSpec(
            (2 * self.group, self.columns_b, self.local),
            lambda i: (jnp.maximum(i - first, 0), 0, 0),
        )

    def rows(self):
        return pl.BlockSpec((self.group * self.tokens, self.local), lambda i: (i, 0))

    def chunks(self):
        return pl.BlockSpec((NARROW, self.group * self.tokens, self.local), lambda i: (0, i, 0))

    def sends(self):
        return pl.BlockSpec(
            (self.width, self.group, self.piece, self.half), lambda i: (0, i, 0, 0)
        )

    def table(self, shape):
        first = self.steps_a
        zeros = (0,) * len(shape)
        return pl.BlockSpec((1,) + shape, lambda i: ((i >= first).astype(jnp.int32),) + zeros)

    def exchange_shape(self):
        return jax.ShapeDtypeStruct((self.width, self.units, self.piece, self.half), BF16)

    def full_sends(self):
        return pl.BlockSpec(
            (self.width, self.group, self.piece, self.local), lambda i: (0, i, 0, 0)
        )

    def full_shape(self):
        return jax.ShapeDtypeStruct((self.width, self.units, self.piece, self.local), BF16)

    def rows_shape(self, kind):
        return jax.ShapeDtypeStruct((self.units * self.tokens, self.local), kind)

    def chunks_shape(self):
        return jax.ShapeDtypeStruct((NARROW, self.units * self.tokens, self.local), BF16)

    def scratch(self):
        return pltpu.VMEM((self.group * self.tokens, self.local), F32)

    def load(self, step, a_ref, b_ref, scratch):
        @pl.when(step == 0)
        def _():
            scratch[...] = jnp.zeros_like(scratch)

        @pl.when(step < self.steps_a)
        def _():
            for u in range(self.group):
                base = u * self.tokens
                scratch[base : base + self.columns_a] = a_ref[u].astype(F32)

        @pl.when(step >= self.steps_a)
        def _():
            for u in range(self.group):
                base = u * self.tokens
                middle = base + self.columns_b
                scratch[base:middle] = b_ref[2 * u].astype(F32)
                scratch[middle : base + self.columns_a] = b_ref[2 * u + 1].astype(F32)

        return scratch[...]

    def parts(self, value):
        return [value[u * self.tokens : (u + 1) * self.tokens] for u in range(self.group)]

    def outs(self):
        last, first = self.steps_a - 1, self.steps_a
        return [
            pl.BlockSpec(
                (self.group, 1, self.columns_a, self.local),
                lambda i: (jnp.minimum(i, last), 0, 0, 0),
            ),
            pl.BlockSpec(
                (2 * self.group, 1, self.columns_b, self.local),
                lambda i: (jnp.maximum(i - first, 0), 0, 0, 0),
            ),
        ]

    def flat_outs(self):
        last, first = self.steps_a - 1, self.steps_a
        return [
            pl.BlockSpec(
                (self.group, self.columns_a, 1, self.local),
                lambda i: (jnp.minimum(i, last), 0, 0, 0),
            ),
            pl.BlockSpec(
                (2 * self.group, self.columns_b, 1, self.local),
                lambda i: (jnp.maximum(i - first, 0), 0, 0, 0),
            ),
        ]

    def store(self, step, value, a_ref, b_ref):
        units = self.parts(value)

        @pl.when(step < self.steps_a)
        def _():
            for u in range(self.group):
                a_ref[u, 0] = units[u][: self.columns_a].astype(a_ref.dtype)

        @pl.when(step >= self.steps_a)
        def _():
            for u in range(self.group):
                b_ref[2 * u, 0] = units[u][: self.columns_b].astype(b_ref.dtype)
                b_ref[2 * u + 1, 0] = units[u][self.columns_b : self.columns_a].astype(b_ref.dtype)

    def store_flat(self, step, value, a_ref, b_ref):
        units = self.parts(value)

        @pl.when(step < self.steps_a)
        def _():
            for u in range(self.group):
                a_ref[u, :, 0, :] = units[u][: self.columns_a]

        @pl.when(step >= self.steps_a)
        def _():
            for u in range(self.group):
                b_ref[2 * u, :, 0, :] = units[u][: self.columns_b]
                b_ref[2 * u + 1, :, 0, :] = units[u][self.columns_b : self.columns_a]

    def put_sends(self, product, unit, refs):
        size = self.local // len(refs)
        for index, ref in enumerate(refs):
            lanes = product[:, index * size : (index + 1) * size]
            ref[:, unit] = lanes.reshape(self.width, self.piece, size).astype(BF16)

    def from_sends(self, table, refs):
        depth = self.width * self.piece
        units = []
        for u in range(self.group):
            size = self.local // len(refs)
            parts = [ref[:, u].astype(F32).reshape(depth, size).astype(BF16) for ref in refs]
            units.append(jnp.concatenate([dot(table, part) for part in parts], axis=1))
        return jnp.concatenate(units, axis=0)

    def valid_rows(self, step, counts, shape):
        row = lax.broadcasted_iota(jnp.int32, shape, 0)
        inside = row >= 0
        used = row < 0
        for u in range(self.group):
            token = row - u * self.tokens
            here = (token >= 0) & (token < self.columns_a)
            in_a = (step < self.steps_a) & (step * self.group + u < counts[0])
            pair = 2 * ((step - self.steps_a) * self.group + u)
            in_b0 = (step >= self.steps_a) & (pair < counts[1])
            in_b1 = (step >= self.steps_a) & (pair + 1 < counts[1])
            first = (in_a | in_b0).astype(jnp.int32)
            second = (in_a | in_b1).astype(jnp.int32)
            flag = jnp.where(token < self.columns_b, first, second)
            used = used | (here & (flag > 0))
        return used


def first_kernel(plan, xa, xb, gain, bias, table, out0, out1, scratch):
    step = pl.program_id(0)
    standard, _ = layer_norm(plan.load(step, xa, xb, scratch))
    scale, shift = (ref[...].astype(F32).reshape(1, plan.local) for ref in (gain, bias))
    for u, part in enumerate(plan.parts(standard * scale + shift)):
        high, low = halves(part)
        spectrum = dot(table[0, 0], high) + (dot(table[0, 0], low) + dot(table[0, 1], high))
        plan.put_sends(spectrum, u, (out0, out1))


def cotangent_kernel(plan, counts, ca, cb, out, sums, scratch):
    step = pl.program_id(0)
    value = plan.load(step, ca, cb, scratch)
    value = jnp.where(plan.valid_rows(step, counts, value.shape), value, 0.0)
    out[...] = value.astype(BF16)

    @pl.when(step == 0)
    def _():
        sums[...] = jnp.zeros_like(sums)

    sums[...] += row_sums(value)


def gelu_both(value):
    bell = jnp.exp(-0.5 * value * value)
    cdf = 0.5 * (1.0 + lax.erf(value * ROOT_HALF))
    return value * cdf, cdf + value * bell * (1.0 / ROOT_TWO_PI)


def hidden_kernel(cot, w0, w1, w2, w3, out):
    for k, weight in enumerate((w0, w1, w2, w3)):
        out[k] = dot_t(cot[...], weight[...]).astype(BF16)


def middle_kernel(
    plan, xa, xb, got0, got1, gain, bias, gain2, bias2, inv, inv_t, w0, w1, w2, w3, shift, back,
    cot, mid, rows, hidden, grad_pre, dmid, out, sums, shift_sums, scratch,
):
    step = pl.program_id(0)

    @pl.when(step == 0)
    def _():
        sums[...] = jnp.zeros_like(sums)
        shift_sums[...] = jnp.zeros_like(shift_sums)

    value = plan.load(step, xa, xb, scratch)
    standard, _ = layer_norm(value)
    middle = value + standard * gain[...] + bias[...]
    middle += plan.from_sends(inv[0], (got0, got1))
    mid[...] = middle
    standard, scale = layer_norm(middle)
    flat = (standard * gain2[...] + bias2[...]).astype(BF16)
    rows[...] = flat
    weights = (w0, w1, w2, w3)
    grad = None
    for k, weight in enumerate(weights):
        for start in range(0, plan.local, CHUNK):
            lanes = slice(start, start + CHUNK)
            act, slope = gelu_both(dot(flat, weight[:, lanes]) + shift[k : k + 1, lanes])
            hidden[k, :, lanes] = act.astype(BF16)
            pre = back[k, :, lanes].astype(F32) * slope
            grad_pre[k, :, lanes] = pre.astype(BF16)
            shift_sums[k, :1, lanes] += jnp.sum(pre, axis=0, keepdims=True)
        part = dot_t(grad_pre[k], weight[...])
        grad = part if grad is None else grad + part
    sums[...] += row_sums(grad * standard, grad)
    result = cot[...].astype(F32) + layer_norm_back(grad, gain2[...], standard, scale)
    dmid[...] = result
    for u, part in enumerate(plan.parts(result)):
        plan.put_sends(dot(inv_t[0], part.astype(BF16)), u, (out,))


def mixed_kernel(
    plan, counts, hidden, w0, w1, w2, w3, bias, mid, dmid, xa, xb, outa, outb, sums, scratch
):
    step = pl.program_id(0)
    standard, _ = layer_norm(plan.load(step, xa, xb, scratch))
    grad = dmid[...]

    @pl.when(step == 0)
    def _():
        sums[...] = jnp.zeros_like(sums)

    sums[...] += row_sums(grad * standard, grad)
    value = mid[...] + bias[...]
    for k, weight in enumerate((w0, w1, w2, w3)):
        value += dot(hidden[k], weight[...])
    value = jnp.where(plan.valid_rows(step, counts, value.shape), value, 0.0)
    plan.store(step, value, outa, outb)


def products(plan, chunked, plain, first, chunk_left, got=None):
    count, local = plain.shape
    square = (1, local, local)
    chunk = pl.BlockSpec((1, count, local), lambda i: (2 * i + first, 0, 0))
    flat = pl.BlockSpec((count, local), lambda i: (0, 0))
    each = pl.BlockSpec(square, lambda i: (i, 0, 0))
    whole_out = pl.BlockSpec((local, local), lambda i: (0, 0))
    one = jax.ShapeDtypeStruct((local, local), BF16)

    def kernel(chunk_ref, plain_ref, *refs):
        pair = (chunk_ref[0], plain_ref[...])
        value = lax.dot_general(
            *(pair if chunk_left else pair[::-1]),
            (((0,), (0,)), ((), ())),
            preferred_element_type=F32,
        )
        if got is None:
            refs[0][0] = value.astype(BF16)
            return
        value += refs[0][0].astype(F32)
        for k in range(2):

            @pl.when(pl.program_id(0) == k)
            def _(k=k):
                refs[1 + k][...] = value.astype(BF16)

    if got is None:
        return call(
            kernel, (2,), [chunk, flat], each, jax.ShapeDtypeStruct((2, local, local), BF16)
        )(chunked, plain)
    return call(kernel, (2,), [chunk, flat, each], [whole_out] * 2, [one] * 2)(
        chunked, plain, got
    )


def last_kernel(plan, xa, xb, got, dmid, gain, table, outa, outb, scratch):
    step = pl.program_id(0)
    standard, scale = layer_norm(plan.load(step, xa, xb, scratch))
    passed = dmid[...]
    grad = plan.from_sends(table[0], (got,)) + passed
    total = passed + layer_norm_back(grad, gain[...], standard, scale)
    plan.store_flat(step, total, outa, outb)


def weights_kernel(plan, inner, outer, inner0, inner1, outer0, outer1):
    half = plan.half
    for weight, outs in ((inner, (inner0, inner1)), (outer, (outer0, outer1))):
        parts = [weight[k].astype(F32) for k in range(2)]
        for h, out in enumerate(outs):
            out[...] = jnp.zeros_like(out)
            for b in range(half // BS):
                lanes = slice(h * half + b * BS, h * half + (b + 1) * BS)
                near = slice(b * BS, (b + 1) * BS)
                late = slice(half + b * BS, half + (b + 1) * BS)
                real, imag = parts[0][:, lanes].astype(BF16), parts[1][:, lanes].astype(BF16)
                out[near, near] = real
                out[late, late] = real
                out[near, late] = imag
                out[late, near] = -imag


def nothing(*refs):
    return None


def hold(value, *before):
    anywhere = pl.BlockSpec(memory_space=pl.ANY)
    return pl.pallas_call(
        nothing,
        in_specs=[anywhere] * (1 + len(before)),
        out_specs=anywhere,
        out_shape=jax.ShapeDtypeStruct(value.shape, value.dtype),
        input_output_aliases={0: 0},
    )(value, *before)


def bit_of(place, link):
    return (place[link[0]] // link[1]) % 2


def fold_kernel(link, place, left, right, keep, send):
    total = left[...].astype(F32) + right[...].astype(F32)
    size = keep.shape[-2]
    near, far = total[..., :size, :], total[..., size:, :]
    bit = bit_of(place, link)

    @pl.when(bit == 0)
    def _():
        keep[...] = near.astype(keep.dtype)
        send[...] = far.astype(send.dtype)

    @pl.when(bit == 1)
    def _():
        keep[...] = far.astype(keep.dtype)
        send[...] = near.astype(send.dtype)


SMEM = pl.BlockSpec(memory_space=pltpu.SMEM)


def flat_call(kernel, place, operands, shapes, before=()):
    def spec(item):
        zeros = (0,) * len(item.shape)
        return pl.BlockSpec(item.shape, lambda: zeros)

    return call(
        kernel,
        (),
        [SMEM] + [spec(item) for item in operands],
        [spec(item) for item in shapes],
        list(shapes),
        after=len(before),
    )(place, *operands, *before)


def fold(place, link, left, right, *before):
    shape = left.shape[:-2] + (left.shape[-2] // 2, left.shape[-1])
    half = jax.ShapeDtypeStruct(shape, left.dtype)
    return flat_call(
        functools.partial(fold_kernel, link), place, (left, right), (half, half), before
    )


def both_fold(place, link, lefts, rights, *before):
    rows, local = lefts[0].shape
    half = jax.ShapeDtypeStruct((2, rows // 2, local), lefts[0].dtype)

    def kernel(place, left0, left1, right0, right1, keep, send):
        for k, (left, right) in enumerate(((left0, right0), (left1, right1))):
            fold_kernel(link, place, left, right, keep.at[k], send.at[k])

    return flat_call(kernel, place, (*lefts, *rights), (half, half), before)


def corners(place, links, pieces, *before):
    _, size, local = pieces[0].shape
    shape = jax.ShapeDtypeStruct((4 * size, local), F32)

    def kernel(place, *refs):
        outer, inner = (bit_of(place, link) for link in links)
        for k, piece in enumerate(refs[:4]):
            start = 2 * (outer ^ (k % 2)) + (inner ^ (k // 2))
            rows = pl.ds(pl.multiple_of(start * size, size), size)
            for j, out in enumerate(refs[4:]):
                out[rows, :] = piece[j].astype(F32)

    return flat_call(kernel, place, pieces, (shape, shape), before)


def total(place, parts, *before, kind=None):
    def kernel(_, *refs):
        values = [ref[...].astype(F32) for ref in refs[:-1]]
        while len(values) > 1:
            values = [a + b for a, b in zip(values[::2], values[1::2], strict=True)]
        refs[-1][...] = values[0].astype(refs[-1].dtype)

    return flat_call(
        kernel, place, parts, [jax.ShapeDtypeStruct(parts[0].shape, kind or parts[0].dtype)], before
    )[0]


def join(place, link, mine, other, *before, kind=None):
    size = mine.shape[-2]
    shape = mine.shape[:-2] + (2 * size, mine.shape[-1])

    def kernel(place, mine, other, out):
        bit = bit_of(place, link)

        def put(low, high):
            out[..., :size, :] = low[...].astype(out.dtype)
            out[..., size:, :] = high[...].astype(out.dtype)

        @pl.when(bit == 0)
        def _():
            put(mine, other)

        @pl.when(bit == 1)
        def _():
            put(other, mine)

    return flat_call(
        kernel, place, (mine, other), [jax.ShapeDtypeStruct(shape, kind or mine.dtype)], before
    )[0]


def last_join(place, link, mine, other, *before):
    size, local = mine.shape

    def kernel(place, mine, other, inner, outer, small, whole_pack):
        bit = bit_of(place, link)
        whole_pack[pl.ds(pl.multiple_of(bit * size, size), size), :] = mine[...].astype(F32)
        whole_pack[pl.ds(pl.multiple_of((1 - bit) * size, size), size), :] = other[...].astype(F32)
        for k in range(2):
            inner[k] = whole_pack[k * BS : (k + 1) * BS]
            outer[k] = whole_pack[(2 + k) * BS : (3 + k) * BS]
        small[...] = whole_pack[4 * BS : 4 * BS + small.shape[0]]

    def spec(item):
        zeros = (0,) * len(item.shape)
        return pl.BlockSpec(item.shape, lambda: zeros)

    matrix = jax.ShapeDtypeStruct((2, BS, local), F32)
    shapes = [matrix, matrix, jax.ShapeDtypeStruct((16, local), F32)]
    return call(
        kernel,
        (),
        [SMEM, spec(mine), spec(other)],
        [spec(item) for item in shapes],
        shapes,
        [pltpu.VMEM((2 * size, local), F32)],
        after=len(before),
    )(place, mine, other, *before)


def unpack(plan, got, part_a, part_b):
    rows_a = plan.rows_a * plan.piece
    rows_b = (plan.units - plan.rows_a) * plan.piece
    for j in range(plan.width):
        value = got[j].astype(F32)
        for part, rows, piece in (
            (part_a, rows_a, value[: plan.rows_a]),
            (part_b, rows_b, value[plan.rows_a :]),
        ):
            for g in range(plan.half // LANES):
                lanes = piece[:, :, g * LANES : (g + 1) * LANES]
                part[g, j * rows : (j + 1) * rows] = lanes.reshape(rows, LANES)


def repack(plan, part_a, part_b, out):
    rows_a = plan.rows_a * plan.piece
    rows_b = (plan.units - plan.rows_a) * plan.piece
    for j in range(plan.width):
        for part, rows, first, last in (
            (part_a, rows_a, 0, plan.rows_a),
            (part_b, rows_b, plan.rows_a, plan.units),
        ):
            for g in range(plan.half // LANES):
                out[j, first:last, :, g * LANES : (g + 1) * LANES] = (
                    part[g, j * rows : (j + 1) * rows]
                    .reshape(last - first, plan.piece, LANES)
                    .astype(BF16)
                )


def grids(plan):
    return (
        (plan.spread_a, plan.pad_a, plan.width * 2 * plan.rows_a, 0, 0),
        (plan.spread_b, plan.pad_b, plan.width * 2 * plan.rows_b, plan.points_a, 1),
    )


def to_points(plan, parts, tables, out, first=None):
    for spread, pad, depth, base, which in grids(plan):
        for f in range(spread):
            lanes = [
                parts[which][g, pl.ds(f, depth, stride=spread), :].astype(BF16)
                for g in range(plan.half // LANES)
            ]
            column = jnp.concatenate(lanes, axis=1)
            product = dot(tables[which][0], column)
            if first is not None:
                product += dot(tables[which][1], column)
                if f == 0:
                    first[which : which + 1] = product[:1]
            out[base + f * pad : base + (f + 1) * pad, :] = jnp.concatenate(
                [product[:pad], product[pad:]], axis=1
            ).astype(out.dtype)


def from_points(plan, points, tables, parts):
    for spread, pad, depth, base, which in grids(plan):
        for f in range(spread):
            value = points[base + f * pad : base + (f + 1) * pad, :]
            column = jnp.concatenate([value[:, : plan.half], value[:, plan.half :]], axis=0)
            product = dot(tables[which][...], column)
            for g in range(plan.half // LANES):
                parts[which][g, pl.ds(f, depth, stride=spread), :] = product[
                    :, g * LANES : (g + 1) * LANES
                ]


def spectral_kernel(
    plan, steps, got, ta, tb, tat, tbt, w1, b1, w2, b2, out, zed, act, slope1, slope2, dc, pa, pb, shrunk
):
    unpack(plan, got, pa, pb)
    dc[...] = jnp.zeros_like(dc)
    to_points(plan, (pa, pb), (ta, tb), zed, dc)
    size = plan.points // steps

    def body(index, carry):
        rows = slice(index * size, (index + 1) * size)
        pre_one = dot(zed[rows, :], w1[...]) + b1[...]
        cdf = 0.5 * (1.0 + lax.erf(pre_one * ROOT_HALF))
        hidden = (pre_one * cdf).astype(BF16)
        act[rows, :] = hidden
        slope1[rows, :] = (
            cdf + pre_one * jnp.exp(-0.5 * pre_one * pre_one) * (1.0 / ROOT_TWO_PI)
        ).astype(BF16)
        pre_two = dot(hidden, w2[...]) + b2[...]
        bent = jnp.tanh(pre_two * (1.0 / SHRINK))
        shrunk[rows, :] = (pre_two - SHRINK * bent).astype(BF16)
        slope2[rows, :] = (bent * bent).astype(BF16)
        return carry

    for index in range(steps):
        body(index, 0)
    from_points(plan, shrunk, (tat, tbt), (pa, pb))
    repack(plan, pa, pb, out)


def spectral_back_kernel(
    plan, steps, skip, got, ta, tb, tat, tbt, w1, w2, slope1, slope2, zed, *refs
):
    out, grad1, grad2, sums, pa, pb, work = refs[skip:]
    unpack(plan, got, pa, pb)
    to_points(plan, (pa, pb), (ta, tb), work)
    size = plan.points // steps
    sums[...] = jnp.zeros_like(sums)

    def body(index, carry):
        rows = slice(index * size, (index + 1) * size)
        two = (work[rows, :].astype(F32) * slope2[rows, :].astype(F32)).astype(BF16)
        grad2[rows, :] = two
        one = (dot_t(two, w2[...]) * slope1[rows, :].astype(F32)).astype(BF16)
        grad1[rows, :] = one
        grad = dot_t(one, w1[...])
        work[rows, :] = grad.astype(BF16)
        sums[...] += row_sums(one.astype(F32), two.astype(F32), grad * zed[rows, :].astype(F32))
        return carry

    for index in range(steps):
        body(index, 0)
    for which, start in enumerate((0, plan.points_a)):
        sums[3 + which : 4 + which] = work[start : start + 16, :].astype(F32)[:1]
        sums[5 + which : 6 + which] = zed[start : start + 16, :].astype(F32)[:1]
    from_points(plan, work, (tat, tbt), (pa, pb))
    repack(plan, pa, pb, out)


def pack_kernel(
    plan, place, products, backs, dcs, norm2, cot, norm1, shift, gain, bias, keep, send, out
):
    half, blocks = plan.half, plan.half // BS
    out[...] = jnp.zeros_like(out)
    for kind in range(2):
        for h in range(2):
            product = products[kind][h]
            for b in range(blocks):
                rows = slice(b * BS, (b + 1) * BS)
                late = slice(half + b * BS, half + (b + 1) * BS)
                real = product[rows, rows] + product[late, late]
                imag = product[rows, late] - product[late, rows]
                lanes = slice(h * half + b * BS, h * half + (b + 1) * BS)
                out[2 * kind * BS : (2 * kind + 1) * BS, lanes] = real
                out[(2 * kind + 1) * BS : (2 * kind + 2) * BS, lanes] = imag
    row = 4 * BS
    for kind in range(2):
        for part in range(2):
            for h in range(2):
                out[row : row + 1, h * half : (h + 1) * half] = backs[h][
                    kind : kind + 1, part * half : (part + 1) * half
                ]
            row += 1
    out[row : row + 2] = norm2[0:2]
    out[row + 2 : row + 3] = cot[0:1]
    row += 3
    first = jnp.where(place[0] == 0, 1.0, 0.0)
    roots = [math.sqrt(H_A * plan.columns_a), math.sqrt(H_B * plan.columns_b)]
    for h in range(2):
        lanes = slice(h * half, (h + 1) * half)
        total = backs[h][2:3, :half] + backs[h][2:3, half:]
        plain = norm1[1:2, lanes]
        for which in range(2):
            grad = backs[h][3 + which : 4 + which, :half] * first
            exact = dcs[h][which : which + 1] - bias[:, lanes] * roots[which]
            total += grad * (exact - backs[h][5 + which : 6 + which, :half])
            plain += grad * roots[which]
        out[row : row + 1, lanes] = norm1[0:1, lanes] + total / gain[:, lanes]
        out[row + 1 : row + 2, lanes] = plain
    row += 2
    for n in range(4):
        out[row + n : row + n + 1] = shift[n ^ place[1], :1]
    size = keep.shape[0]
    mine = pl.multiple_of((place[1] % 2) * size, size)
    keep[...] = out[pl.ds(mine, size), :]
    send[...] = out[pl.ds(size - mine, size), :]


def swap(value, axis, distance):
    size = lax.axis_size(axis)
    return lax.ppermute(value, axis, [(i, i ^ distance) for i in range(size)])


def fast_device(
    plan,
    field_a,
    field_b,
    cotangent_a,
    cotangent_b,
    offsets_a,
    offsets_b,
    first_gain,
    first_bias,
    inner_weight,
    inner_bias,
    outer_weight,
    outer_bias,
    second_gain,
    second_norm_bias,
    expand_weight,
    expand_bias,
    reduce_weight,
    reduce_bias,
):
    width, local, half = plan.width, plan.local, plan.half
    tokens, units = plan.tokens, plan.units
    myself = lax.axis_index("wide")
    xa = field_a.reshape(plan.rows_a, plan.columns_a, local)
    xb = field_b.reshape(plan.rows_b, plan.columns_b, local)
    ca = cotangent_a.reshape(plan.rows_a, plan.columns_a, local)
    cb = cotangent_b.reshape(plan.rows_b, plan.columns_b, local)
    gain1 = first_gain.astype(F32)[None]
    bias1 = first_bias.astype(F32)[None]
    gain2 = second_gain.astype(F32)[None]
    bias2 = second_norm_bias.astype(F32)[None]
    tables = [
        column_tables(plan.columns_a, plan.spread_a, width, 1, tokens),
        column_tables(plan.columns_b, plan.spread_b, width, 2, tokens),
    ]
    forward = np.stack([pair[0] for pair in tables])
    inverse = np.stack([pair[1] for pair in tables])
    depth = width * plan.piece
    fwd_w_t = jnp.asarray(forward.transpose(0, 2, 1).astype(jnp.bfloat16))
    inv_w_t = jnp.asarray(inverse.astype(jnp.bfloat16))
    inv_w = jnp.asarray(inverse.transpose(0, 2, 1).astype(jnp.bfloat16))
    fine = forward.astype(jnp.bfloat16)
    rest = (forward - fine.astype(np.float64)).astype(jnp.bfloat16)
    fwd_w = jnp.asarray(np.stack([fine, rest], axis=1))
    vector = pl.BlockSpec((1, local), lambda i: (0, 0))
    plain = pl.BlockSpec((local,), lambda i: (0,))
    sums_spec = pl.BlockSpec((PAD, local), lambda i: (0, 0))
    sums_shape = jax.ShapeDtypeStruct((PAD, local), F32)
    scratch = plan.scratch()
    counts = jnp.stack(
        [offsets_a[myself + 1] - offsets_a[myself], offsets_b[myself + 1] - offsets_b[myself]]
    )
    count_spec = pl.BlockSpec(memory_space=pltpu.SMEM)

    def exchange(parts):
        return [lax.all_to_all(part, "wide", 0, 0, tiled=True) for part in parts]

    sends = call(
        functools.partial(first_kernel, plan),
        (plan.steps,),
        [plan.spec_a(), plan.spec_b(), plain, plain, plan.table((2, depth, tokens))],
        [plan.sends(), plan.sends()],
        [plan.exchange_shape()] * 2,
        [scratch],
    )(xa, xb, first_gain, first_bias, fwd_w)

    own = (expand_weight, expand_bias, reduce_weight)
    far = tuple(swap(part, "narrow", 2) for part in own)
    near = tuple(swap(part, "narrow", 1) for part in own)
    cross = tuple(swap(part, "narrow", 1) for part in far)
    chunks = (own, near, far, cross)
    expand = [chunk[0] for chunk in chunks]
    expand_b = jnp.stack([chunk[1] for chunk in chunks]).astype(F32)
    reduce = [chunk[2] for chunk in chunks]
    square = pl.BlockSpec(own[0].shape, lambda i: (0, 0), pipeline_mode=pl.Buffered(1))

    cot, cot_sums = call(
        functools.partial(cotangent_kernel, plan),
        (plan.steps,),
        [count_spec, plan.spec_a(), plan.spec_b()],
        [plan.rows(), sums_spec],
        [plan.rows_shape(BF16), sums_shape],
        [scratch],
    )(counts, ca, cb)
    block_shape = jax.ShapeDtypeStruct((2 * half, 2 * half), BF16)
    block_spec = pl.BlockSpec((2 * half, 2 * half), lambda: (0, 0))
    *ones, two0, two1 = call(
        functools.partial(weights_kernel, plan),
        (),
        [whole(inner_weight), whole(outer_weight)],
        [block_spec] * 4,
        [block_shape] * 4,
    )(inner_weight, outer_weight)
    twos = (two0, two1)

    table = []
    for offsets, height, rows, padded in (
        (offsets_a, H_A, plan.rows_a, plan.pad_a),
        (offsets_b, H_B, plan.rows_b, plan.pad_b),
    ):
        line, valid = row_slots(offsets, rows, width)
        table.append(jnp.stack(halves(row_table(height, line, valid, padded))))
    row_tables = (table[0], table[1], table[0][0].T, table[1][0].T)
    arrived = exchange([sends[0], hold(sends[1], *ones, cot, *row_tables, far[0], far[2])])
    shift1 = inner_bias.astype(F32).reshape(2, 2, half)
    shift2 = outer_bias.astype(F32).reshape(2, 2, half)
    points_shape = jax.ShapeDtypeStruct((plan.points, 2 * half), BF16)
    points_spec = pl.BlockSpec((plan.points, 2 * half), lambda: (0, 0))
    exchange_spec = pl.BlockSpec((width, units, plan.piece, half), lambda: (0, 0, 0, 0))
    parts_scratch = [
        pltpu.VMEM((half // LANES, width * plan.rows_a * plan.piece, LANES), F32),
        pltpu.VMEM((half // LANES, width * (units - plan.rows_a) * plan.piece, LANES), F32),
        pltpu.VMEM((plan.points, 2 * half), BF16),
    ]
    steps = 5 if plan.points % 80 == 0 else 1
    kept, outgoing = [], []
    ready = ((), (near[0], near[2], cross[0], cross[2], expand_b))
    for h in range(2):
        operands = (
            arrived[h],
            *row_tables,
            ones[h],
            shift1[:, h].reshape(1, 2 * half),
            twos[h],
            shift2[:, h].reshape(1, 2 * half),
        )
        got = call(
            functools.partial(spectral_kernel, plan, steps),
            (),
            [whole(item) for item in operands],
            [exchange_spec] + [points_spec] * 4 + [pl.BlockSpec((PAD, half), lambda: (0, 0))],
            [plan.exchange_shape()] + [points_shape] * 4 + [jax.ShapeDtypeStruct((PAD, half), F32)],
            parts_scratch,
            after=len(ready[h]),
        )(*operands, *ready[h])
        outgoing.append(got[0])
        kept.append(got[1:])
    returned = exchange(outgoing)
    grad_hidden = call(
        hidden_kernel,
        (plan.steps,),
        [plan.rows()] + [square] * 4,
        plan.chunks(),
        plan.chunks_shape(),
        after=1,
    )(cot, *reduce, returned[0])

    (
        middle, rows, hidden, grad_pre, dmid, send, norm2_sums, shift_sums
    ) = call(
        functools.partial(middle_kernel, plan),
        (plan.steps,),
        [plan.spec_a(), plan.spec_b(), plan.sends(), plan.sends()]
        + [vector] * 4
        + [plan.table((tokens, depth)), plan.table((depth, tokens))]
        + [square] * 4
        + [
            pl.BlockSpec(expand_b.shape, lambda i: (0, 0)),
            plan.chunks(),
            plan.rows(),
        ],
        [
            plan.rows(),
            plan.rows(),
            plan.chunks(),
            plan.chunks(),
            plan.rows(),
            plan.full_sends(),
            sums_spec,
            pl.BlockSpec((NARROW, PAD, local), lambda i: (0, 0, 0)),
        ],
        [
            plan.rows_shape(F32),
            plan.rows_shape(BF16),
            plan.chunks_shape(),
            plan.chunks_shape(),
            plan.rows_shape(F32),
            plan.full_shape(),
            sums_shape,
            jax.ShapeDtypeStruct((NARROW, PAD, local), F32),
        ],
        [scratch],
        limit=60,
    )(
        xa, xb, *returned, gain1, bias1, gain2, bias2, inv_w, inv_w_t, *expand, expand_b,
        grad_hidden, cot,
    )
    place = jnp.stack([myself, lax.axis_index("narrow")])
    row_link, low_link, high_link = ("wide", 1), ("wide", 2), ("wide", 4)
    axes = ("wide", "narrow")

    def over(value, link):
        return swap(value, *link)

    def at(link):
        return axes.index(link[0]), link[1]

    core_link, column_link = ("narrow", 1), ("narrow", 2)
    reduce_got = over(products(plan, hidden, cot, 1, True), core_link)
    expand_got = over(products(plan, grad_pre, rows, 1, False), core_link)
    reduce_keep, reduce_send = products(plan, hidden, cot, 0, True, reduce_got)
    expand_keep, expand_send = products(plan, grad_pre, rows, 0, False, expand_got)
    reduce_got = over(reduce_send, column_link)
    expand_got = over(expand_send, column_link)
    (arrived,) = exchange([send])

    mixed_a, mixed_b, norm1_sums = call(
        functools.partial(mixed_kernel, plan),
        (plan.steps,),
        [count_spec, plan.chunks()]
        + [square] * 4
        + [vector, plan.rows(), plan.rows(), plan.spec_a(), plan.spec_b()],
        [*plan.outs(), sums_spec],
        [
            jax.ShapeDtypeStruct(field_a.shape, BF16),
            jax.ShapeDtypeStruct(field_b.shape, BF16),
            sums_shape,
        ],
        [scratch],
        after=1,
    )(
        counts, hidden, *reduce, reduce_bias.astype(F32)[None], middle, dmid, xa, xb,
        reduce_send,
    )
    keep, send = both_fold(
        place,
        at(row_link),
        (reduce_keep, expand_keep),
        (reduce_got, expand_got),
        mixed_a,
    )
    row_got = over(send, row_link)

    backs = []
    back_shape = jax.ShapeDtypeStruct((PAD, 2 * half), F32)
    weight_sums, pairs = ([], []), []
    over_points = (((0,), (0,)), ((), ()))
    for h in range(2):
        zed, act, slope1, slope2, _ = kept[h]
        operands = (*row_tables, ones[h], twos[h], slope1, slope2, zed)
        block = pl.BlockSpec((width, units, plan.piece, half), lambda i, h=h: (0, 0, 0, h))
        earlier = [keep] if h == 0 else [outgoing]
        outgoing, grad1, grad2, sums = pl.pallas_call(
            functools.partial(spectral_back_kernel, plan, steps, len(earlier)),
            grid=(1,),
            in_specs=[block]
            + [whole(item) for item in operands]
            + [pl.BlockSpec(memory_space=pl.ANY)] * len(earlier),
            out_specs=[block] + [whole(points_shape)] * 2 + [whole(back_shape)],
            out_shape=[plan.full_shape(), points_shape, points_shape, back_shape],
            input_output_aliases={1 + len(operands): 0} if h else {},
            scratch_shapes=parts_scratch,
            compiler_params=pltpu.CompilerParams(vmem_limit_bytes=60 * MIB),
        )(arrived, *operands, *earlier)
        backs.append(sums)
        pairs.append(((zed, grad1), (act, grad2)))
    for h in range(2):
        for index, (left, right) in enumerate(pairs[h]):
            if h == 0:
                right = hold(right, sums)
            weight_sums[index].append(
                lax.dot_general(left, right, over_points, preferred_element_type=F32)
            )
    keep, send = fold(place, at(low_link), keep, row_got, sums)
    outgoing = hold(outgoing, send)
    flat = (
        *weight_sums[0],
        *weight_sums[1],
        *backs,
        kept[0][4],
        kept[1][4],
        norm2_sums,
        cot_sums,
        norm1_sums,
        shift_sums,
        gain1,
        bias1,
    )

    def pack_body(place, *refs):
        pack_kernel(
            plan, place, (refs[0:2], refs[2:4]), refs[4:6], refs[6:8], *refs[8:]
        )

    pack_links = (core_link, column_link, row_link)
    pack_rows = round_up(4 * BS + 13, 8 << (len(pack_links) + 1)) // 2
    pack_half = jax.ShapeDtypeStruct((pack_rows, local), F32)
    pack_keep, pack_send = call(
        pack_body,
        (),
        [count_spec] + [whole(item) for item in flat],
        [pl.BlockSpec((pack_rows, local), lambda: (0, 0))] * 2,
        [pack_half] * 2,
        [pltpu.VMEM((2 * pack_rows, local), F32)],
    )(place, *flat)
    pack_keep, pack_send = fold(place, at(column_link), pack_keep, over(pack_send, core_link))
    pack_keep, pack_send = fold(place, at(row_link), pack_keep, over(pack_send, column_link))
    keep, send = fold(place, at(high_link), keep, over(send, low_link), pack_send)
    shared = total(place, (keep, over(send, high_link)))
    high_got = over(shared, high_link)

    pack = total(place, (pack_keep, over(pack_send, pack_links[-1])))
    (returned,) = exchange([outgoing])
    layers = [over(pack, ("wide", 2 * k)) for k in range(1, width // 2)]

    grad_a, grad_b = call(
        functools.partial(last_kernel, plan),
        (plan.steps,),
        [plan.spec_a(), plan.spec_b(), plan.full_sends(), plan.rows(), vector]
        + [plan.table((tokens, depth))],
        plan.flat_outs(),
        [
            jax.ShapeDtypeStruct((plan.rows_a, plan.columns_a, 1, local), F32),
            jax.ShapeDtypeStruct((plan.rows_b, plan.columns_b, 1, local), F32),
        ],
        [scratch],
        after=2,
    )(xa, xb, returned, dmid, gain1, fwd_w_t, pack, shared)

    pack = total(place, [pack] + layers, grad_a, kind=BF16)
    shared = join(place, at(high_link), shared, high_got, pack)
    low_got = over(shared, low_link)
    row_got = over(shared, row_link)
    reduce_sum, expand_sum = corners(
        place,
        (at(row_link), at(low_link)),
        (shared, row_got, low_got, over(low_got, row_link)),
    )
    pack = join(place, at(row_link), pack, over(pack, row_link), row_got)
    pack = join(place, at(column_link), pack, over(pack, column_link), low_got)
    inner_grad, outer_grad, small = last_join(
        place, at(core_link), pack, over(pack, core_link), reduce_sum
    )
    own_row = lax.dynamic_slice_in_dim(small, 9 + place[1], 1)[0]
    return (
        mixed_a,
        mixed_b,
        grad_a.transpose(0, 2, 1, 3),
        grad_b.transpose(0, 2, 1, 3),
        small[7],
        small[8],
        inner_grad,
        small[0:2],
        outer_grad,
        small[2:4],
        small[4],
        small[5],
        expand_sum,
        own_row,
        reduce_sum,
        small[6],
    )


def choose(field_a, field_b, *rest):
    plan = Plan(
        lax.axis_size("wide"),
        field_a.shape[0],
        field_a.shape[2],
        field_b.shape[0],
        field_b.shape[2],
        field_a.shape[3],
    )
    alone = field_a.shape[1] == 1 and field_b.shape[1] == 1
    if plan.fits() and alone and lax.axis_size("narrow") == 4:
        return fast_device(plan, field_a, field_b, *rest)
    return general_device(field_a, field_b, *rest)


def solution(mesh):
    placed = (
        P("wide", "narrow", None, None),
        P("wide", "narrow", None, None),
        P("wide", "narrow", None, None),
        P("wide", "narrow", None, None),
        P(),
        P(),
        P(),
        P(),
        P(),
        P(),
        P(),
        P(),
        P(),
        P(),
        P(None, "narrow"),
        P("narrow"),
        P("narrow", None),
        P(),
    )
    return jax.shard_map(
        choose,
        mesh=mesh,
        in_specs=placed,
        out_specs=(
            P("wide", "narrow", None, None),
            P("wide", "narrow", None, None),
            P("wide", "narrow", None, None),
            P("wide", "narrow", None, None),
            P(),
            P(),
            P(),
            P(),
            P(),
            P(),
            P(),
            P(),
            P(None, "narrow"),
            P("narrow"),
            P("narrow", None),
            P(),
        ),
        check_vma=False,
    )
```
